32 devices in a mesh: expert: 4 (over x, core), context: 4 (over z), dp: 2 (over y).
Axes of the slice: x: 2, y: 2, z: 4, core: 2. Of those that a mesh axis runs over, the one named last changes fastest.
Arguments:
- tokens: bfloat16 [4, 2048, 768], P('dp', ('expert', 'context'))
- cotangent: bfloat16 [4, 2048, 768], P('dp', ('expert', 'context')), may hold values from -6 to 6
- query_key_value_weight: bfloat16 [768, 2304], replicated, may hold values from -0.21875 to 0.21875
- output_weight: bfloat16 [768, 768], replicated, may hold values from -1.25 to 1.25
- gain_one: float32 [768], replicated, may hold values from 0.25 to 1.75
- gain_two: float32 [768], replicated, may hold values from 0.25 to 1.75
- router_weight: float32 [768, 4], replicated, may hold values from -0.15625 to 0.15625
- w_in: bfloat16 [4, 768, 3072], P('expert', None, 'context'), may hold values from -0.21875 to 0.21875
- w_down: bfloat16 [4, 768, 3072], P('expert', None, 'context'), may hold values from -0.4375 to 0.4375
- position_bias: float32 [32, 12], replicated, may hold values from -4 to 4
- bucket: int32 [4095], replicated, may hold values from 0 to 31
- route: int32 [4, 2048], P('dp', ('expert', 'context')), may hold values from 0 to 3, as said below
- slot: int32 [4, 2048], P('dp', ('expert', 'context')), may hold values from 0 to 79, as said below
- dropped: int32 [4, 2048], P('dp', ('expert', 'context')), may hold values from 0 to 1, as said below
Outputs:
- output: bfloat16 [4, 2048, 768], P('dp', ('expert', 'context'))
- d_tokens: bfloat16 [4, 2048, 768], P('dp', ('expert', 'context'))
- grad_w_qkv: float32 [768, 2304], P(('expert', 'context', 'dp'))
- grad_w_out: float32 [768, 768], P(('expert', 'context', 'dp'))
- grad_gain_one: float32 [768], P(('expert', 'context', 'dp'))
- grad_gain_two: float32 [768], P(('expert', 'context', 'dp'))
- grad_w_router: float32 [768, 4], P(('expert', 'context', 'dp'))
- grad_w_in: float32 [4, 768, 3072], P('expert', None, ('context', 'dp'))
- grad_w_down: float32 [4, 768, 3072], P('expert', None, ('context', 'dp'))
- grad_position_bias: float32 [32, 12], replicated
The draws below stay inside these ranges and needn't reach their ends.
Inputs may be any that keep to these rules, and one draw needn't show every extreme that they name: `route`: in the 256 tokens of one device's block some expert is named by more than 80 tokens; the blocks of devices that differ only in their index of expert share that expert. Among the kept tokens of one block that name the same expert the slots are distinct; slot is 0 where dropped is 1. In each block an expert keeps at most 80 tokens, a token is dropped only where its expert keeps 80, and some expert keeps exactly 80 in every block.
All inputs are finite; a program needn't handle non-finite values.
Results may differ from the reference program's by a relative error of at most 0.02.
Values may be sent and summed in bfloat16 or wider, within the bound.
No kernel may reach another device: no remote copies, remote signals or barrier semaphores. Data moves between devices by JAX's collectives and lax.ppermute only.
A program may use at most 256 MiB of HBM per device.

```python
import math
from functools import partial
import jax
import jax.numpy as jnp
from jax import lax

D = 768
HEADS = 12
HEAD_DIM = 64
FF = 3072
BUCKETS = 32
SEQ_LEN = 2048
SEQ_DEV = 2
EXPERTS = 4
CAP = 80
SEQS = 4
N_EXPERT = 4
N_CONTEXT = 4
N_DP = 2


def arrange_rows(values, tok_count):
    shaped = values.reshape(N_DP, N_EXPERT * N_CONTEXT, SEQ_DEV, tok_count)
    return jnp.transpose(shaped, (0, 2, 1, 3)).reshape(SEQS, SEQ_LEN).astype(jnp.int32)


def draw_common(key):
    blocks_seq = N_EXPERT * N_CONTEXT
    tok_count = SEQ_LEN // blocks_seq
    rows_block = SEQ_DEV * tok_count
    forced = CAP + rows_block // 8
    key_hot, key_pick, key_free, key_order = jax.random.split(key, 4)
    hot_base = jax.random.randint(key_hot, (N_DP, 1, N_CONTEXT), 0, EXPERTS)
    hot_expert = jnp.broadcast_to(hot_base, (N_DP, N_EXPERT, N_CONTEXT)).reshape(N_DP, blocks_seq)
    block_shape = (N_DP, blocks_seq, rows_block)
    positions = jnp.arange(rows_block, dtype=jnp.int32)
    priority = jax.random.randint(key_pick, block_shape, 0, 1 << 16) * rows_block + positions
    ranking = jnp.argsort(jnp.argsort(priority, axis=-1), axis=-1)
    free_route = jax.random.randint(key_free, block_shape, 0, EXPERTS)
    routes = jnp.where(ranking < forced, hot_expert[..., None], free_route).astype(jnp.int32)
    precedence = jax.random.randint(key_order, block_shape, 0, 1 << 16) * rows_block + positions
    same_route = routes[..., :, None] == routes[..., None, :]
    before = precedence[..., None, :] < precedence[..., :, None]
    counted = jnp.sum(same_route & before, axis=-1).astype(jnp.int32)
    dropped_now = (counted >= CAP).astype(jnp.int32)
    slot_ids = jnp.where(dropped_now == 1, 0, counted).astype(jnp.int32)
    return (arrange_rows(routes, tok_count), arrange_rows(slot_ids, tok_count), arrange_rows(dropped_now, tok_count))


def draw_route(key, part):
    return draw_common(key)[0]


def draw_slot(key, part):
    return draw_common(key)[1]


def draw_dropped(key, part):
    return draw_common(key)[2]


def draw_tokens(key, part):
    key = jax.random.fold_in(key, 11)
    key_scale, key_body = jax.random.split(key, 2)
    scales = jnp.exp(jax.random.uniform(key_scale, (SEQS, SEQ_LEN, 1), minval=math.log(0.5), maxval=math.log(5.0)))
    values_drawn = jax.random.normal(key_body, (SEQS, SEQ_LEN, D))
    return (values_drawn * scales).astype(jnp.bfloat16)


def place_ends(values, stream_key, low, top_value):
    spot = [jax.random.randint(jax.random.fold_in(stream_key, axis), (), 0, length) for axis, length in enumerate(values.shape)]
    longest = values.shape.index(max(values.shape))
    next_to = spot[:longest] + [(spot[longest] + 1) % values.shape[longest]] + spot[longest + 1:]
    return values.at[tuple(spot)].set(low).at[tuple(next_to)].set(top_value)


def block_levels(own_key, shape, pieces, smallest, high):
    factor_of, own = 1.0, jax.random.fold_in(own_key, 6)
    for dim, parts in pieces:
        steps = jnp.exp(jax.random.uniform(jax.random.fold_in(own, dim), (parts,), jnp.float32, smallest / len(pieces), high / len(pieces)))
        factor_of = factor_of * jnp.repeat(steps, shape[dim] // parts).reshape([-1 if axis == dim else 1 for axis in range(len(shape))])
    return factor_of


def scatter_about(stream_key, shape, scale, reach, pieces=(), kind=jnp.bfloat16):
    factor_of = block_levels(stream_key, shape, pieces, -0.22, 0.18) if pieces else 1.0
    values = jax.random.normal(stream_key, shape, jnp.float32) * scale * factor_of
    return jnp.minimum(jnp.maximum(values, -reach), reach).astype(kind)


def setup_inputs(seed: int = 0) -> dict:
    keys = jax.random.split(jax.random.key(seed), 15)
    return {
        "tokens": draw_tokens(jax.random.fold_in(keys[14], 71), 0),
        "cotangent": scatter_about(keys[1], (SEQS, SEQ_LEN, D), 1.0, 6.0, ((0, 2), (1, 16))),
        "query_key_value_weight": scatter_about(keys[2], (D, 3 * D), D ** -0.5, 0.21875),
        "output_weight": scatter_about(keys[3], (D, D), (D // 32) ** -0.5, 1.25),
        "gain_one": jnp.clip(1.0 + 0.15 * jax.random.normal(keys[4], (D,), jnp.float32), 0.25, 1.75),
        "gain_two": jnp.clip(1.0 + 0.15 * jax.random.normal(keys[5], (D,), jnp.float32), 0.25, 1.75),
        "router_weight": scatter_about(keys[6], (D, EXPERTS), (2 * D) ** -0.5, 0.15625, (), jnp.float32),
        "w_in": scatter_about(keys[7], (EXPERTS, D, FF), D ** -0.5, 0.21875, ((0, 4), (2, 4))),
        "w_down": scatter_about(keys[8], (EXPERTS, D, FF), (FF // 16) ** -0.5, 0.4375, ((0, 4), (2, 4))),
        "position_bias": scatter_about(keys[9], (BUCKETS, HEADS), 1.0, 4.0, (), jnp.float32),
        "bucket": place_ends(jax.random.randint(keys[10], (2 * SEQ_LEN - 1,), 0, BUCKETS), jax.random.fold_in(keys[10], 1), 0, BUCKETS - 1).astype(jnp.int32),
        "route": draw_route(jax.random.fold_in(keys[14], 71), 0),
        "slot": draw_slot(jax.random.fold_in(keys[14], 71), 0),
        "dropped": draw_dropped(jax.random.fold_in(keys[14], 71), 0),
    }


norm_epsilon = 1e-06
score_scale = 0.125
precise_mode = lax.Precision.HIGHEST

@jax.custom_vjp
def reduced_precision(v):
    return lax.optimization_barrier(v.astype(jnp.bfloat16)).astype(jnp.float32)

@jax.custom_vjp
def reduced_backward(v):
    return v

def low_keep(v):
    return (reduced_precision(v), None)

def low_pass(kept, grad):
    return (grad,)

def back_keep(v):
    return (v, None)

def back_low(kept, grad):
    return (reduced_precision(grad),)
reduced_precision.defvjp(low_keep, low_pass)
reduced_backward.defvjp(back_keep, back_low)

def gelu_act(values):
    return jax.nn.gelu(values, approximate=True)

def rms_norm(values, gain):
    factor = lax.rsqrt(lax.optimization_barrier(jnp.mean(values * values, axis=-1, keepdims=True)) + norm_epsilon)
    return values * factor * gain

def attend_one(packed, bias_all):
    query_rows, key_rows, value_rows = packed
    scores = jnp.einsum('qhd,khd->hqk', query_rows, key_rows, precision=precise_mode) * score_scale + bias_all
    scores = reduced_backward(scores)
    weights = reduced_precision(jax.nn.softmax(scores, axis=-1))
    blended = jnp.einsum('hqk,khd->qhd', weights, value_rows, precision=precise_mode)
    return blended.reshape(blended.shape[0], -1)

def expert_one(packed):
    rows_in, weight_in, weight_down = packed
    pre_act = reduced_backward(jnp.dot(rows_in, weight_in, precision=precise_mode))
    hidden = reduced_precision(gelu_act(pre_act))
    return reduced_precision(jnp.dot(hidden, weight_down.T, precision=precise_mode))

def layer(tokens, query_key_value_weight, output_weight, gain_one, gain_two, router_weight, w_in, w_down, position_bias, bucket, route, slot, dropped):
    seq_count, seq_len, width_all = tokens.shape
    normalized_input = reduced_precision(rms_norm(tokens, gain_one))
    attention_projected = reduced_backward(reduced_precision(jnp.einsum('ocp,py->ocy', normalized_input, query_key_value_weight, precision=precise_mode)))
    query_rows = attention_projected[..., :width_all].reshape(seq_count, seq_len, HEADS, HEAD_DIM)
    key_rows = attention_projected[..., width_all:2 * width_all].reshape(seq_count, seq_len, HEADS, HEAD_DIM)
    value_rows = attention_projected[..., 2 * width_all:].reshape(seq_count, seq_len, HEADS, HEAD_DIM)
    offsets = jnp.arange(seq_len, dtype=jnp.int32)[None, :] - jnp.arange(seq_len, dtype=jnp.int32)[:, None] + seq_len - 1
    bias_all = jnp.transpose(position_bias[bucket][offsets], (2, 0, 1))
    attention_result = lax.map(jax.checkpoint(partial(attend_one, bias_all=bias_all)), (query_rows, key_rows, value_rows))
    attention_result = reduced_backward(reduced_precision(attention_result))
    residual_branch = reduced_backward(jnp.einsum('ocp,py->ocy', attention_result, output_weight, precision=precise_mode))
    middle = tokens + residual_branch
    normalized_second = rms_norm(middle, gain_two)
    router_logits = jnp.einsum('ocp,py->ocy', normalized_second, router_weight, precision=precise_mode)
    router = jax.nn.softmax(router_logits, axis=-1)
    expert_count = w_in.shape[0]
    chosen = (route[..., None] == jnp.arange(expert_count, dtype=jnp.int32)).astype(jnp.float32)
    gate = lax.optimization_barrier(jnp.sum(router * chosen, axis=-1, keepdims=True))
    sent = reduced_backward(reduced_precision(normalized_second))
    blocks_seq = N_EXPERT * N_CONTEXT
    tok_count = seq_len // blocks_seq
    block_count = seq_count // SEQ_DEV * blocks_seq
    rows_all = expert_count * block_count * CAP
    block_ids = (jnp.arange(seq_count, dtype=jnp.int32) // SEQ_DEV)[:, None] * blocks_seq + jnp.arange(seq_len, dtype=jnp.int32)[None, :] // tok_count
    target = jnp.where(dropped == 1, rows_all, route * (block_count * CAP) + block_ids * CAP + slot).astype(jnp.int32)
    flat_target = target.reshape(-1)
    buffer = jnp.zeros((rows_all + 1, width_all), jnp.float32).at[flat_target].add(sent.reshape(-1, width_all))
    expert_rows = buffer[:rows_all].reshape(expert_count, block_count * CAP, width_all)
    results = lax.map(jax.checkpoint(expert_one), (expert_rows, w_in, w_down))
    results = jnp.concatenate([results.reshape(rows_all, width_all), jnp.zeros((1, width_all), jnp.float32)], axis=0)
    returned = reduced_backward(results[flat_target].reshape(seq_count, seq_len, width_all))
    return middle + gate * returned

def reference(tokens, cotangent, query_key_value_weight, output_weight, gain_one, gain_two, router_weight, w_in, w_down, position_bias, bucket, route, slot, dropped):
    floats = tuple((value.astype(jnp.float32) for value in (tokens, query_key_value_weight, output_weight, gain_one, gain_two, router_weight, w_in, w_down, position_bias)))

    def whole(*operands):
        return layer(*operands, bucket, route, slot, dropped)
    output, pull_back = jax.vjp(whole, *floats)
    grads = pull_back(cotangent.astype(jnp.float32))
    return (output.astype(jnp.bfloat16), grads[0].astype(jnp.bfloat16), grads[1], grads[2], grads[3], grads[4], grads[5], grads[6], grads[7], grads[8])
```

```python
import functools

import jax
import jax.numpy as jnp
from jax import lax
from jax.experimental import pallas as pl
from jax.experimental.pallas import tpu as pltpu
from jax.sharding import Mesh, PartitionSpec as P

D = 768
HEADS = 12
HEAD_DIM = 64
GROUP_HEADS = 3
HEAD_GROUPS = HEADS // GROUP_HEADS
SEQ_DEV = 2
GROUPS = SEQ_DEV * HEAD_GROUPS
WIDTH = 256
SKEW = 128

norm_epsilon = 1e-06
score_scale = 0.125
precise_mode = lax.Precision.HIGHEST
vmem_bytes = 50 * 1024 * 1024
f32 = jnp.float32
bf16 = jnp.bfloat16


def matmul(left, right):
    return jnp.dot(left, right, preferred_element_type=f32)


def contract_rows(left, right):
    return lax.dot_general(left, right, (((0,), (0,)), ((), ())), preferred_element_type=f32)


def contract_cols(left, right):
    return lax.dot_general(left, right, (((1,), (1,)), ((), ())), preferred_element_type=f32)


def skewed_table(table_row):
    wide = jnp.broadcast_to(table_row, (SKEW, table_row.shape[1]))
    return pltpu.roll(wide, 1, 1, stride=1, stride_axis=0)


def forward_kernel(
    chunk, qs_ref, ks_ref, table_ref, q_ref, kv_ref, out_ref, lse_ref, skew, score, weight, rows
):
    half = table_ref.shape[2] // 2
    key_count = kv_ref.shape[2]
    skew[...] = skewed_table(table_ref[0])
    rows[...] = kv_ref[0].T
    per_chunk = chunk // WIDTH

    def one_tile(tile, carry):
        lanes = pl.ds(pl.multiple_of(tile * WIDTH, WIDTH), WIDTH)
        query = q_ref[0, :, lanes] * jnp.asarray(score_scale, bf16)
        query = jnp.concatenate([query, jnp.zeros_like(query)], axis=0)
        start = qs_ref[tile // per_chunk] + (tile % per_chunk) * WIDTH
        top = jnp.full((8, WIDTH), -jnp.inf, f32)
        for block in range(key_count // SKEW):
            offset = block * SKEW
            behind = start - ks_ref[offset // chunk] - (offset % chunk)
            bias = skew[:, pl.ds(pl.multiple_of(half + behind, SKEW), WIDTH)]
            part = matmul(rows[offset : offset + SKEW, :], query) + bias
            score[offset : offset + SKEW, :] = part
            top = jnp.maximum(top, jnp.max(part.reshape(SKEW // 8, 8, WIDTH), axis=0))
        top = jnp.max(top, axis=0, keepdims=True)
        total = jnp.zeros((8, WIDTH), f32)
        for block in range(key_count // SKEW):
            offset = block * SKEW
            part = jnp.exp(score[offset : offset + SKEW, :] - top)
            total = total + jnp.sum(part.reshape(SKEW // 8, 8, WIDTH), axis=0)
            weight[offset : offset + SKEW, :] = part.astype(bf16)
        total = jnp.sum(total, axis=0, keepdims=True)
        blended = matmul(kv_ref[0, HEAD_DIM:, :], weight[...])
        out_ref[0, :, lanes] = blended / total
        lse_ref[0, :, lanes] = top + jnp.log(total)
        return carry

    lax.fori_loop(0, q_ref.shape[2] // WIDTH, one_tile, 0)


def backward_kernel(
    chunk,
    qs_ref,
    ks_ref,
    table_ref,
    q_ref,
    kv_ref,
    out_ref,
    lse_ref,
    grad_ref,
    dq_ref,
    dkv_ref,
    dtable_ref,
    skew,
    dskew,
    rows,
    dkv,
):
    span = table_ref.shape[2]
    half = span // 2
    key_count = kv_ref.shape[2]
    skew[...] = skewed_table(table_ref[0])
    rows[...] = kv_ref[0].T
    dskew[...] = jnp.zeros_like(dskew)
    dkv[...] = jnp.zeros_like(dkv)
    per_chunk = chunk // WIDTH

    def one_tile(tile, carry):
        lanes = pl.ds(pl.multiple_of(tile * WIDTH, WIDTH), WIDTH)
        query = q_ref[0, :, lanes] * jnp.asarray(score_scale, bf16)
        grad = grad_ref[0, :, lanes]
        lse = lse_ref[0, :, lanes]
        delta = jnp.sum(grad.astype(f32) * out_ref[0, :, lanes], axis=0, keepdims=True)
        query = jnp.concatenate([query, jnp.zeros_like(query)], axis=0)
        grad = jnp.concatenate([jnp.zeros_like(grad), grad], axis=0)
        query_rows = query.T
        grad_rows = grad.T
        start = qs_ref[tile // per_chunk] + (tile % per_chunk) * WIDTH
        dq = jnp.zeros((HEAD_DIM, WIDTH), f32)
        step = 2 * SKEW
        for block in range(key_count // step):
            offset = block * step
            keys = rows[offset : offset + step, :]
            raw = matmul(keys, query)
            dprob = matmul(keys, grad)
            probs = []
            dscores = []
            for part in range(2):
                inner = offset + part * SKEW
                behind = start - ks_ref[inner // chunk] - (inner % chunk)
                here = pl.ds(pl.multiple_of(half + behind, SKEW), WIDTH)
                own = slice(part * SKEW, (part + 1) * SKEW)
                prob = jnp.exp(raw[own] + skew[:, here] - lse)
                dscore = prob * (dprob[own] - delta)
                dskew[:, here] += dscore
                probs.append(prob.astype(bf16))
                dscores.append(dscore.astype(bf16))
            prob = jnp.concatenate(probs, axis=0)
            dscore = jnp.concatenate(dscores, axis=0)
            dkv[offset : offset + step, :] += matmul(dscore, query_rows) + matmul(prob, grad_rows)
            dq = dq + matmul(kv_ref[0, :HEAD_DIM, offset : offset + step], dscore)
        dq_ref[0, :, lanes] = (dq * score_scale).astype(bf16)
        return carry

    lax.fori_loop(0, q_ref.shape[2] // WIDTH, one_tile, 0)
    dkv_ref[0] = dkv[...].T.astype(bf16)
    folded = dskew[...]
    count = SKEW
    while count > 8:
        count //= 2
        folded = folded[:count] + pltpu.roll(folded[count:], span - count, 1)
    dtable_ref[0] = folded


def head_spec(*shape):
    return pl.BlockSpec((1,) + shape, lambda head: (head, 0, 0))


def attention_forward(chunk, qs, ks, table, query, key_value):
    count, keys, span = query.shape[2], key_value.shape[2], table.shape[2]
    scalars = pl.BlockSpec(memory_space=pltpu.SMEM)
    return pl.pallas_call(
        functools.partial(forward_kernel, chunk),
        grid=(GROUP_HEADS,),
        in_specs=[
            scalars,
            scalars,
            head_spec(1, span),
            head_spec(HEAD_DIM, count),
            head_spec(2 * HEAD_DIM, keys),
        ],
        out_specs=[head_spec(HEAD_DIM, count), head_spec(1, count)],
        out_shape=[
            jax.ShapeDtypeStruct((GROUP_HEADS, HEAD_DIM, count), f32),
            jax.ShapeDtypeStruct((GROUP_HEADS, 1, count), f32),
        ],
        scratch_shapes=[
            pltpu.VMEM((SKEW, span), f32),
            pltpu.VMEM((keys, WIDTH), f32),
            pltpu.VMEM((keys, WIDTH), bf16),
            pltpu.VMEM((keys, 2 * HEAD_DIM), bf16),
        ],
        compiler_params=pltpu.CompilerParams(vmem_limit_bytes=vmem_bytes),
        cost_estimate=pl.CostEstimate(
            flops=4 * GROUP_HEADS * HEAD_DIM * count * keys * 4,
            bytes_accessed=4 * GROUP_HEADS * HEAD_DIM * (count + keys) * 2,
            transcendentals=GROUP_HEADS * count * keys,
        ),
        name="attention_forward",
    )(qs, ks, table, query, key_value)


def attention_backward(chunk, qs, ks, table, query, key_value, out, lse, grad):
    count, keys, span = query.shape[2], key_value.shape[2], table.shape[2]
    scalars = pl.BlockSpec(memory_space=pltpu.SMEM)
    return pl.pallas_call(
        functools.partial(backward_kernel, chunk),
        grid=(GROUP_HEADS,),
        in_specs=[
            scalars,
            scalars,
            head_spec(1, span),
            head_spec(HEAD_DIM, count),
            head_spec(2 * HEAD_DIM, keys),
            head_spec(HEAD_DIM, count),
            head_spec(1, count),
            head_spec(HEAD_DIM, count),
        ],
        out_specs=[
            head_spec(HEAD_DIM, count),
            head_spec(2 * HEAD_DIM, keys),
            head_spec(8, span),
        ],
        out_shape=[
            jax.ShapeDtypeStruct((GROUP_HEADS, HEAD_DIM, count), bf16),
            jax.ShapeDtypeStruct((GROUP_HEADS, 2 * HEAD_DIM, keys), bf16),
            jax.ShapeDtypeStruct((GROUP_HEADS, 8, span), f32),
        ],
        scratch_shapes=[
            pltpu.VMEM((SKEW, span), f32),
            pltpu.VMEM((SKEW, span), f32),
            pltpu.VMEM((keys, 2 * HEAD_DIM), bf16),
            pltpu.VMEM((keys, 2 * HEAD_DIM), f32),
        ],
        compiler_params=pltpu.CompilerParams(vmem_limit_bytes=vmem_bytes),
        cost_estimate=pl.CostEstimate(
            flops=10 * GROUP_HEADS * HEAD_DIM * count * keys * 4,
            bytes_accessed=4 * GROUP_HEADS * HEAD_DIM * (count + keys) * 4,
            transcendentals=GROUP_HEADS * count * keys,
        ),
        name="attention_backward",
    )(qs, ks, table, query, key_value, out, lse, grad)


def shift(value, axis, step):
    size = lax.axis_size(axis)
    return lax.ppermute(value, axis, [(i, (i + step) % size) for i in range(size)])


def pick(value, index, dim=0):
    return lax.dynamic_index_in_dim(value, index, dim, keepdims=False)


def spread(parts, axis):
    return [parts[0]] + [shift(parts[k], axis, k) for k in range(1, len(parts))]


def give_back(parts, axis):
    return [parts[0]] + [shift(parts[k], axis, -k) for k in range(1, len(parts))]


def scatter_sum(value, axis, dim, wire=bf16):
    size = lax.axis_size(axis)
    index = lax.axis_index(axis)
    total = pick(value, index, dim)
    for k in range(1, size):
        part = pick(value, lax.rem(index + k, size), dim).astype(wire)
        total = total + shift(part, axis, k).astype(f32)
    return total


def sum_everywhere(value, axes):
    for axis in axes:
        size = lax.axis_size(axis)
        step = 1
        while step < size:
            value = value + lax.ppermute(value, axis, [(i, i ^ step) for i in range(size)])
            step *= 2
    return value


def scatter_rows(value, wire=bf16):
    ga, gb, ctx, dp = (lax.axis_size(a) for a in ("ga", "gb", "context", "dp"))
    rows, cols = value.shape
    own = rows // (ga * gb * ctx * dp)
    value = value.reshape(ga, gb, ctx * dp * own, cols)
    value = scatter_sum(value, "gb", 1, wire)
    value = scatter_sum(value, "ga", 0, wire)
    value = value.reshape(ctx, dp, own, cols)
    value = scatter_sum(value, "dp", 1, wire)
    return scatter_sum(value, "context", 0, wire)


def split_halves(value):
    high = value.astype(bf16)
    return high, (value - high.astype(f32)).astype(bf16)


def gelu_parts(values):
    c = 0.7978845608028654
    square = values * values
    bent = jnp.tanh(c * values * (1.0 + 0.044715 * square))
    act = 0.5 * values * (1.0 + bent)
    slope = 0.5 * (1.0 + bent) + 0.5 * values * (1.0 - bent * bent) * c * (
        1.0 + 3 * 0.044715 * square
    )
    return act, slope


def local(
    tokens,
    cotangent,
    query_key_value_weight,
    output_weight,
    gain_one,
    gain_two,
    router_weight,
    w_in,
    w_down,
    position_bias,
    bucket,
    route,
    slot,
    dropped,
):
    seq_count, tok_count = tokens.shape[:2]
    row_count = seq_count * tok_count
    ga, gb, ctx = (lax.axis_size(a) for a in ("ga", "gb", "context"))
    experts = ga * gb
    seq_len = tok_count * experts * ctx
    chunk = ctx * tok_count
    capacity = (5 * row_count + 4 * experts - 1) // (4 * experts)
    expert_axis = ("ga", "gb")
    group_axis = ("ga", "context")
    ga_index, gb_index = lax.axis_index("ga"), lax.axis_index("gb")
    expert_index = lax.axis_index(expert_axis)
    head_group = lax.rem(lax.axis_index(group_axis), HEAD_GROUPS)

    inputs = tokens.reshape(row_count, D).astype(f32)
    scale_one = lax.rsqrt(jnp.mean(inputs * inputs, axis=-1, keepdims=True) + norm_epsilon)
    normed_low = (inputs * scale_one * gain_one).astype(bf16)
    projected = lax.dot_general(
        query_key_value_weight,
        normed_low,
        (((0,), (1,)), ((), ())),
        preferred_element_type=f32,
    ).astype(bf16)
    projected = projected.reshape(3, HEAD_GROUPS, GROUP_HEADS, HEAD_DIM, seq_count, tok_count)
    projected = jnp.transpose(projected, (4, 1, 2, 0, 3, 5)).reshape(
        GROUPS, GROUP_HEADS * 3 * HEAD_DIM, tok_count
    )
    gathered = lax.all_to_all(projected, group_axis, 0, 0, tiled=True)
    gathered = jnp.transpose(
        gathered.reshape(GROUPS, GROUP_HEADS, 3 * HEAD_DIM, tok_count), (1, 2, 0, 3)
    ).reshape(GROUP_HEADS, 3 * HEAD_DIM, GROUPS * tok_count)
    query = gathered[:, :HEAD_DIM]
    own_keys = gathered[:, HEAD_DIM:]
    key_value = jnp.concatenate(
        [own_keys] + [shift(own_keys, "gb", k) for k in range(1, gb)], axis=2
    )
    in_chunk = jnp.arange(ga, dtype=jnp.int32)[None, :] * gb
    peers = lax.rem(gb_index - jnp.arange(gb, dtype=jnp.int32) + gb, gb)[:, None]
    key_starts = ((in_chunk + peers) * chunk).reshape(-1).astype(jnp.int32)
    query_starts = key_starts[:ga]

    onehot = (
        jnp.arange(position_bias.shape[0], dtype=jnp.int32)[:, None]
        == jnp.pad(bucket[::-1], (0, 1), constant_values=-1)[None, :]
    ).astype(f32)
    bias_heads = lax.dynamic_slice_in_dim(position_bias.T, head_group * GROUP_HEADS, GROUP_HEADS, 0)
    table = jnp.dot(bias_heads, onehot, precision=precise_mode, preferred_element_type=f32)
    table = table[:, None, :]

    route_flat = route.reshape(-1)
    relative = lax.rem(route_flat - expert_index + experts, experts)
    position = relative * capacity + slot.reshape(-1)
    assign = (
        (jnp.arange(experts * capacity, dtype=jnp.int32)[:, None] == position[None, :])
        & (dropped.reshape(-1) == 0)[None, :]
    ).astype(bf16)
    grad_low = cotangent.reshape(row_count, D)
    grad_low, key_value = lax.optimization_barrier((grad_low, key_value))
    grad_buffer = matmul(assign, grad_low).astype(bf16).reshape(experts, capacity, D)
    grad_rows = jnp.concatenate(
        spread([grad_buffer[k] for k in range(experts)], expert_axis), axis=0
    )
    grad_blocks = spread([grad_rows] * ctx, "context")

    attended, lse = attention_forward(chunk, query_starts, key_starts, table, query, key_value)
    attended_parts = jnp.transpose(
        attended.astype(bf16).reshape(GROUP_HEADS * HEAD_DIM, GROUPS, tok_count), (1, 0, 2)
    )
    attended_parts = lax.all_to_all(attended_parts, group_axis, 0, 0, tiled=True)
    attended_low = jnp.transpose(
        attended_parts.reshape(seq_count, D, tok_count), (1, 0, 2)
    ).reshape(D, row_count)
    middle = inputs + contract_rows(attended_low, output_weight)
    scale_two = lax.rsqrt(jnp.mean(middle * middle, axis=-1, keepdims=True) + norm_epsilon)
    normalized_second = middle * scale_two * gain_two
    router_logits = jnp.dot(
        normalized_second, router_weight, precision=precise_mode, preferred_element_type=f32
    )
    router = jax.nn.softmax(router_logits, axis=-1)
    chosen = (route_flat[:, None] == jnp.arange(experts, dtype=jnp.int32)[None, :]).astype(f32)
    gate = jnp.sum(router * chosen, axis=-1, keepdims=True)

    gate_high, gate_low = split_halves(gate)
    payload = jnp.concatenate(
        [
            normalized_second.astype(bf16),
            gate_high,
            gate_low,
            jnp.zeros((row_count, 126), bf16),
        ],
        axis=1,
    )
    buffer = matmul(assign, payload).astype(bf16).reshape(experts, capacity, D + 128)
    received = jnp.concatenate(
        spread([buffer[k] for k in range(experts)], expert_axis), axis=0
    )
    row_blocks = spread([received[:, :D]] * ctx, "context")
    gate_blocks = spread([received[:, D:]] * ctx, "context")

    local_in = w_in[0]
    local_down = w_down[0]
    ones = jnp.ones((8, local_in.shape[1]), bf16)
    hidden_blocks, slope_blocks, back_parts, out_parts, gate_parts = [], [], [], [], []
    for k in range(ctx):
        act, slope = gelu_parts(matmul(row_blocks[k], local_in))
        hidden = act.astype(bf16)
        grad_hidden = matmul(grad_blocks[k], local_down)
        grad_pre = grad_hidden * slope
        hidden_blocks.append(hidden)
        slope_blocks.append(grad_pre)
        back_parts.append(contract_cols(grad_pre.astype(bf16), local_in).astype(bf16))
        gate_parts.append(contract_cols(ones, (grad_hidden * hidden.astype(f32)).astype(bf16)))
        out_parts.append(contract_cols(hidden, local_down).astype(bf16))

    def add_up(parts):
        total = parts[0].astype(f32)
        for part in parts[1:]:
            total = total + part.astype(f32)
        return total

    back_sum = add_up(give_back(back_parts, "context")).astype(bf16)
    gate_sum = add_up(give_back(gate_parts, "context"))
    back_rows = jnp.concatenate(
        give_back(
            [back_sum[k * capacity : (k + 1) * capacity] for k in range(experts)], expert_axis
        ),
        axis=0,
    )
    gate_row = jnp.concatenate(
        give_back(
            [gate_sum[:, k * capacity : (k + 1) * capacity] for k in range(experts)], expert_axis
        ),
        axis=1,
    )
    grad_sent = contract_rows(assign, back_rows) * gate
    grad_gate = lax.dot_general(
        assign.astype(f32),
        gate_row,
        (((0,), (1,)), ((), ())),
        precision=precise_mode,
        preferred_element_type=f32,
    )[:, :1]

    grad_out = cotangent.reshape(row_count, D).astype(f32)
    grad_logits = grad_gate * gate * (chosen - router)
    grad_normed_two = grad_sent + lax.dot_general(
        grad_logits,
        router_weight,
        (((1,), (1,)), ((), ())),
        precision=precise_mode,
        preferred_element_type=f32,
    )
    scaled_two = gain_two * grad_normed_two
    cube_two = scale_two * scale_two * scale_two
    grad_middle = (
        grad_out
        + scale_two * scaled_two
        - middle * cube_two * jnp.mean(scaled_two * middle, axis=-1, keepdims=True)
    )
    grad_branch = grad_middle.astype(bf16)

    grad_heads = contract_cols(output_weight, grad_branch).astype(bf16)
    grad_heads = jnp.transpose(
        grad_heads.reshape(HEAD_GROUPS, GROUP_HEADS * HEAD_DIM, seq_count, tok_count), (2, 0, 1, 3)
    ).reshape(GROUPS, GROUP_HEADS * HEAD_DIM, tok_count)
    grad_heads = lax.all_to_all(grad_heads, group_axis, 0, 0, tiled=True)
    grad_heads = jnp.transpose(
        grad_heads.reshape(GROUPS, GROUP_HEADS, HEAD_DIM, tok_count), (1, 2, 0, 3)
    ).reshape(GROUP_HEADS, HEAD_DIM, GROUPS * tok_count)
    grad_query, grad_kv, grad_table = attention_backward(
        chunk, query_starts, key_starts, table, query, key_value, attended, lse, grad_heads
    )
    grad_kv = grad_kv.reshape(GROUP_HEADS, 2 * HEAD_DIM, gb, GROUPS * tok_count)
    grad_kv = add_up(give_back([grad_kv[:, :, k] for k in range(gb)], "gb")).astype(bf16)
    grad_projected = jnp.concatenate([grad_query, grad_kv], axis=1)
    grad_projected = jnp.transpose(
        grad_projected.reshape(GROUP_HEADS * 3 * HEAD_DIM, GROUPS, tok_count), (1, 0, 2)
    )
    grad_projected = lax.all_to_all(grad_projected, group_axis, 0, 0, tiled=True)
    grad_projected = jnp.transpose(
        grad_projected.reshape(
            seq_count, HEAD_GROUPS, GROUP_HEADS, 3, HEAD_DIM, tok_count
        ),
        (3, 1, 2, 4, 0, 5),
    ).reshape(3 * D, row_count)
    qkv_grad = lax.dot_general(
        normed_low, grad_projected, (((0,), (1,)), ((), ())), preferred_element_type=f32
    )
    grad_normed = lax.dot_general(
        grad_projected,
        query_key_value_weight,
        (((0,), (1,)), ((), ())),
        preferred_element_type=f32,
    )
    scaled_one = gain_one * grad_normed
    cube_one = scale_one * scale_one * scale_one
    grad_inputs = (
        grad_middle
        + scale_one * scaled_one
        - inputs * cube_one * jnp.mean(scaled_one * inputs, axis=-1, keepdims=True)
    )
    gain_one_grad = jnp.sum(grad_normed * inputs * scale_one, axis=0)

    result = add_up(give_back(out_parts, "context")).astype(bf16)
    returned_rows = jnp.concatenate(
        give_back(
            [result[k * capacity : (k + 1) * capacity] for k in range(experts)], expert_axis
        ),
        axis=0,
    )
    returned = contract_rows(assign, returned_rows)
    output = (middle + gate * returned).astype(bf16)

    all_rows = jnp.concatenate(row_blocks, axis=0)
    all_grads = jnp.concatenate(grad_blocks, axis=0)
    all_gates = jnp.concatenate(gate_blocks, axis=0)[:, :2].astype(f32)
    all_gates = all_gates[:, :1] + all_gates[:, 1:2]
    all_hidden = jnp.concatenate(hidden_blocks, axis=0)
    all_pre = (jnp.concatenate(slope_blocks, axis=0) * all_gates).astype(bf16)
    all_returned = (all_gates * all_grads.astype(f32)).astype(bf16)
    down_part = contract_rows(all_returned, all_hidden)
    in_part = contract_rows(all_rows, all_pre)
    dp_size = lax.axis_size("dp")
    in_grad = scatter_sum(in_part.reshape(D, dp_size, -1), "dp", 1)
    down_grad = scatter_sum(down_part.reshape(D, dp_size, -1), "dp", 1)

    out_grad = scatter_rows(matmul(attended_low, grad_branch))
    router_grad = lax.dot_general(
        normalized_second,
        grad_logits,
        (((0,), (0,)), ((), ())),
        precision=precise_mode,
        preferred_element_type=f32,
    )
    gain_two_grad = jnp.sum(grad_normed_two * middle * scale_two, axis=0)
    small = scatter_rows(
        jnp.concatenate([router_grad, gain_two_grad[:, None]], axis=1), f32
    )
    qkv_total = scatter_rows(qkv_grad)
    gain_one_total = scatter_rows(gain_one_grad[:, None], f32)
    span = bucket.shape[0]
    grad_table = jnp.pad(grad_table, ((0, 0), (0, 0), (0, 8)))
    by_offset = grad_table[:, 0, 1 : 1 + span]
    for r in range(1, 8):
        by_offset = by_offset + grad_table[:, r, r + 1 : r + 1 + span]
    bias_part = lax.dot_general(
        by_offset,
        onehot[:, :span],
        (((1,), (1,)), ((), ())),
        precision=precise_mode,
        preferred_element_type=f32,
    )
    bias_grad = lax.dynamic_update_slice_in_dim(
        jnp.zeros((HEADS, bias_part.shape[1]), f32), bias_part, head_group * GROUP_HEADS, 0
    )
    bias_grad = sum_everywhere(bias_grad, ("gb", "ga", "dp", "context")).T
    return (
        output.reshape(seq_count, tok_count, D),
        grad_inputs.astype(bf16).reshape(seq_count, tok_count, D),
        qkv_total,
        out_grad,
        gain_one_total[:, 0],
        small[:, -1],
        small[:, :-1],
        in_grad[None],
        down_grad[None],
        bias_grad,
    )


def solution(mesh):
    ctx = mesh.shape["context"]
    ga = max(GROUPS // ctx, 1)
    gb = mesh.shape["expert"] // ga
    fine = Mesh(
        mesh.devices.reshape(ga, gb, ctx, mesh.shape["dp"]), ("ga", "gb", "context", "dp")
    )
    expert = ("ga", "gb")
    blocks = ("ga", "gb", "context")
    everywhere = ("ga", "gb", "context", "dp")
    return jax.shard_map(
        local,
        mesh=fine,
        in_specs=(
            P("dp", blocks, None),
            P("dp", blocks, None),
            P(),
            P(),
            P(),
            P(),
            P(),
            P(expert, None, "context"),
            P(expert, None, "context"),
            P(),
            P(),
            P("dp", blocks),
            P("dp", blocks),
            P("dp", blocks),
        ),
        out_specs=(
            P("dp", blocks, None),
            P("dp", blocks, None),
            P(everywhere, None),
            P(everywhere, None),
            P(everywhere),
            P(everywhere),
            P(everywhere, None),
            P(expert, None, ("context", "dp")),
            P(expert, None, ("context", "dp")),
            P(),
        ),
        check_vma=False,
    )
```

```python
import functools

import jax
import jax.numpy as jnp
from jax import lax
from jax.experimental import pallas as pl
from jax.experimental.pallas import tpu as pltpu
from jax.sharding import Mesh, PartitionSpec as P

D = 768
HEADS = 12
HEAD_DIM = 64
GROUP_HEADS = 3
HEAD_GROUPS = HEADS // GROUP_HEADS
SEQ_DEV = 2
GROUPS = SEQ_DEV * HEAD_GROUPS
WIDTH = 256
BLOCK = 128

norm_epsilon = 1e-06
score_scale = 0.125
precise_mode = lax.Precision.HIGHEST
vmem_bytes = 50 * 1024 * 1024
f32 = jnp.float32
bf16 = jnp.bfloat16


def matmul(left, right):
    return jnp.dot(left, right, preferred_element_type=f32)


def contract_rows(left, right):
    return lax.dot_general(left, right, (((0,), (0,)), ((), ())), preferred_element_type=f32)


def contract_cols(left, right):
    return lax.dot_general(left, right, (((1,), (1,)), ((), ())), preferred_element_type=f32)


def skewed_table(table_row):
    wide = jnp.broadcast_to(table_row, (BLOCK, table_row.shape[1]))
    return pltpu.roll(wide, 1, 1, stride=1, stride_axis=0)


def key_rows(kv_refs, rows):
    for part, kv_ref in enumerate(kv_refs):
        count = kv_ref.shape[1]
        rows[part * count : (part + 1) * count, :] = kv_ref[...].T


def forward_kernel(parts, qs_ref, ks_ref, place_ref, table_ref, q_ref, *refs):
    kv_refs = refs[:parts]
    out_ref, full_ref, lse_ref, skew, score, weight, rows = refs[parts:]
    half = table_ref.shape[2] // 2
    own_count = kv_refs[0].shape[1]
    key_count = parts * own_count
    skew[...] = skewed_table(table_ref[0])
    key_rows(kv_refs, rows)
    blocks = WIDTH // BLOCK

    def one_tile(tile, carry):
        lanes = pl.ds(pl.multiple_of(tile * WIDTH, WIDTH), WIDTH)
        query = q_ref[:, lanes] * jnp.asarray(score_scale, bf16)
        query = jnp.concatenate([query, jnp.zeros_like(query)], axis=0)
        starts = [half + qs_ref[tile * blocks + i] for i in range(blocks)]
        top = jnp.full((8, WIDTH), -jnp.inf, f32)
        for block in range(key_count // BLOCK):
            offset = block * BLOCK
            bias = jnp.concatenate(
                [
                    skew[:, pl.ds(pl.multiple_of(start - ks_ref[block], BLOCK), BLOCK)]
                    for start in starts
                ],
                axis=1,
            )
            part = matmul(rows[offset : offset + BLOCK, :], query) + bias
            score[offset : offset + BLOCK, :] = part
            top = jnp.maximum(top, jnp.max(part.reshape(BLOCK // 8, 8, WIDTH), axis=0))
        top = jnp.max(top, axis=0, keepdims=True)
        total = jnp.zeros((8, WIDTH), f32)
        for block in range(key_count // BLOCK):
            offset = block * BLOCK
            part = jnp.exp(score[offset : offset + BLOCK, :] - top)
            total = total + jnp.sum(part.reshape(BLOCK // 8, 8, WIDTH), axis=0)
            weight[offset : offset + BLOCK, :] = part.astype(bf16)
        total = jnp.sum(total, axis=0, keepdims=True)
        blended = jnp.zeros((HEAD_DIM, WIDTH), f32)
        for part, kv_ref in enumerate(kv_refs):
            own = weight[part * own_count : (part + 1) * own_count, :]
            blended = blended + matmul(kv_ref[HEAD_DIM:, :], own)
        blended = blended / total
        full_ref[:, lanes] = blended
        for i in range(blocks):
            piece = blended[:, i * BLOCK : (i + 1) * BLOCK]
            out_ref[place_ref[tile * blocks + i]] = piece.astype(bf16)
        lse_ref[0, :, lanes] = top + jnp.log(total)
        return carry

    lax.fori_loop(0, q_ref.shape[1] // WIDTH, one_tile, 0)


def backward_kernel(
    parts, qs_ref, ks_ref, place_ref, table_ref, q_ref, full_ref, lse_ref, grad_ref, *refs
):
    kv_refs = refs[:parts]
    dq_ref = refs[parts]
    dkv_refs = refs[parts + 1 : 2 * parts + 1]
    dtable_ref, skew, dskew, rows, dkv = refs[2 * parts + 1 :]
    span = table_ref.shape[2]
    half = span // 2
    own_count = kv_refs[0].shape[1]
    key_count = parts * own_count
    skew[...] = skewed_table(table_ref[0])
    key_rows(kv_refs, rows)
    dskew[...] = jnp.zeros_like(dskew)
    dkv[...] = jnp.zeros_like(dkv)
    blocks = WIDTH // BLOCK
    step = 2 * BLOCK

    def one_tile(tile, carry):
        lanes = pl.ds(pl.multiple_of(tile * WIDTH, WIDTH), WIDTH)
        query = q_ref[:, lanes] * jnp.asarray(score_scale, bf16)
        grad = jnp.concatenate(
            [grad_ref[place_ref[tile * blocks + i]] for i in range(blocks)], axis=1
        )
        lse = lse_ref[0, :, lanes]
        delta = jnp.sum(grad.astype(f32) * full_ref[:, lanes], axis=0, keepdims=True)
        query = jnp.concatenate([query, jnp.zeros_like(query)], axis=0)
        grad = jnp.concatenate([jnp.zeros_like(grad), grad], axis=0)
        query_rows = query.T
        grad_rows = grad.T
        starts = [half + qs_ref[tile * blocks + i] for i in range(blocks)]
        dq = jnp.zeros((HEAD_DIM, WIDTH), f32)
        for offset in range(0, key_count, step):
            keys = rows[offset : offset + step, :]
            raw = matmul(keys, query)
            dprob = matmul(keys, grad)
            probs = []
            dscores = []
            for inner in range(0, step, BLOCK):
                key_start = ks_ref[(offset + inner) // BLOCK]
                own = slice(inner, inner + BLOCK)
                prob_row = []
                dscore_row = []
                for i, start in enumerate(starts):
                    here = pl.ds(pl.multiple_of(start - key_start, BLOCK), BLOCK)
                    cols = slice(i * BLOCK, (i + 1) * BLOCK)
                    prob = jnp.exp(raw[own, cols] + skew[:, here] - lse[:, cols])
                    dscore = prob * (dprob[own, cols] - delta[:, cols])
                    dskew[:, here] += dscore
                    prob_row.append(prob.astype(bf16))
                    dscore_row.append(dscore.astype(bf16))
                probs.append(jnp.concatenate(prob_row, axis=1))
                dscores.append(jnp.concatenate(dscore_row, axis=1))
            prob = jnp.concatenate(probs, axis=0)
            dscore = jnp.concatenate(dscores, axis=0)
            dkv[offset : offset + step, :] += matmul(dscore, query_rows) + matmul(prob, grad_rows)
            part, inside = divmod(offset, own_count)
            dq = dq + matmul(kv_refs[part][:HEAD_DIM, inside : inside + step], dscore)
        dq_ref[:, lanes] = (dq * score_scale).astype(bf16)
        return carry

    lax.fori_loop(0, q_ref.shape[1] // WIDTH, one_tile, 0)
    for part, dkv_ref in enumerate(dkv_refs):
        dkv_ref[...] = dkv[part * own_count : (part + 1) * own_count, :].T.astype(bf16)
    folded = dskew[...]
    count = BLOCK
    while count > 8:
        count //= 2
        folded = folded[:count] + pltpu.roll(folded[count:], span - count, 1)
    dtable_ref[0] = folded


def stack_spec(*shape):
    return pl.BlockSpec((1,) + shape, lambda head: (head, 0, 0))


def rows_spec(*shape):
    return pl.BlockSpec(shape, lambda head: (head, 0))


def place_spec(blocks):
    return pl.BlockSpec((blocks, HEAD_DIM, BLOCK), lambda head: (0, head, 0))


def attention_forward(qs, ks, place, table, query, kvs):
    count, span, parts = query.shape[1], table.shape[2], len(kvs)
    keys = parts * count
    scalars = pl.BlockSpec(memory_space=pltpu.SMEM)
    return pl.pallas_call(
        functools.partial(forward_kernel, parts),
        grid=(GROUP_HEADS,),
        in_specs=[scalars, scalars, scalars, stack_spec(1, span), rows_spec(HEAD_DIM, count)]
        + [rows_spec(2 * HEAD_DIM, count)] * parts,
        out_specs=[
            place_spec(count // BLOCK),
            rows_spec(HEAD_DIM, count),
            stack_spec(1, count),
        ],
        out_shape=[
            jax.ShapeDtypeStruct((count // BLOCK, GROUP_HEADS * HEAD_DIM, BLOCK), bf16),
            jax.ShapeDtypeStruct((GROUP_HEADS * HEAD_DIM, count), f32),
            jax.ShapeDtypeStruct((GROUP_HEADS, 1, count), f32),
        ],
        scratch_shapes=[
            pltpu.VMEM((BLOCK, span), f32),
            pltpu.VMEM((keys, WIDTH), f32),
            pltpu.VMEM((keys, WIDTH), bf16),
            pltpu.VMEM((keys, 2 * HEAD_DIM), bf16),
        ],
        compiler_params=pltpu.CompilerParams(vmem_limit_bytes=vmem_bytes),
        cost_estimate=pl.CostEstimate(
            flops=4 * GROUP_HEADS * HEAD_DIM * count * keys * 4,
            bytes_accessed=4 * GROUP_HEADS * HEAD_DIM * (count + keys) * 2,
            transcendentals=GROUP_HEADS * count * keys,
        ),
        name="attention_forward",
    )(qs, ks, place, table, query, *kvs)


def attention_backward(qs, ks, place, table, query, full, lse, grad, kvs):
    count, span, parts = query.shape[1], table.shape[2], len(kvs)
    keys = parts * count
    scalars = pl.BlockSpec(memory_space=pltpu.SMEM)
    return pl.pallas_call(
        functools.partial(backward_kernel, parts),
        grid=(GROUP_HEADS,),
        in_specs=[
            scalars,
            scalars,
            scalars,
            stack_spec(1, span),
            rows_spec(HEAD_DIM, count),
            rows_spec(HEAD_DIM, count),
            stack_spec(1, count),
            place_spec(count // BLOCK),
        ]
        + [rows_spec(2 * HEAD_DIM, count)] * parts,
        out_specs=[rows_spec(HEAD_DIM, count)]
        + [rows_spec(2 * HEAD_DIM, count)] * parts
        + [stack_spec(8, span)],
        out_shape=[jax.ShapeDtypeStruct((GROUP_HEADS * HEAD_DIM, count), bf16)]
        + [jax.ShapeDtypeStruct((GROUP_HEADS * 2 * HEAD_DIM, count), bf16)] * parts
        + [jax.ShapeDtypeStruct((GROUP_HEADS, 8, span), f32)],
        scratch_shapes=[
            pltpu.VMEM((BLOCK, span), f32),
            pltpu.VMEM((BLOCK, span), f32),
            pltpu.VMEM((keys, 2 * HEAD_DIM), bf16),
            pltpu.VMEM((keys, 2 * HEAD_DIM), f32),
        ],
        compiler_params=pltpu.CompilerParams(vmem_limit_bytes=vmem_bytes),
        cost_estimate=pl.CostEstimate(
            flops=10 * GROUP_HEADS * HEAD_DIM * count * keys * 4,
            bytes_accessed=4 * GROUP_HEADS * HEAD_DIM * (count + keys) * 4,
            transcendentals=GROUP_HEADS * count * keys,
        ),
        name="attention_backward",
    )(qs, ks, place, table, query, full, lse, grad, *kvs)


def shift(value, axis, step):
    size = lax.axis_size(axis)
    return lax.ppermute(value, axis, [(i, (i + step) % size) for i in range(size)])


def pick(value, index, dim=0):
    return lax.dynamic_index_in_dim(value, index, dim, keepdims=False)


def spread(parts, axis):
    return [parts[0]] + [shift(parts[k], axis, k) for k in range(1, len(parts))]


def give_back(parts, axis):
    return [parts[0]] + [shift(parts[k], axis, -k) for k in range(1, len(parts))]


def scatter_sum(value, axis, dim, wire=bf16):
    size = lax.axis_size(axis)
    index = lax.axis_index(axis)
    total = pick(value, index, dim)
    for k in range(1, size):
        part = pick(value, lax.rem(index + k, size), dim).astype(wire)
        total = total + shift(part, axis, k).astype(f32)
    return total


def sum_everywhere(value, axes):
    for axis in axes:
        size = lax.axis_size(axis)
        step = 1
        while step < size:
            value = value + lax.ppermute(value, axis, [(i, i ^ step) for i in range(size)])
            step *= 2
    return value


def scatter_rows(value, wire=bf16):
    ga, gb, ctx, dp = (lax.axis_size(a) for a in ("ga", "gb", "context", "dp"))
    rows, cols = value.shape
    own = rows // (ga * gb * ctx * dp)
    value = value.reshape(ga, gb, ctx * dp * own, cols)
    value = scatter_sum(value, "gb", 1, wire)
    value = scatter_sum(value, "ga", 0, wire)
    value = value.reshape(ctx, dp, own, cols)
    return scatter_sum(value, "dp", 1, wire)


def split_halves(value):
    high = value.astype(bf16)
    return high, (value - high.astype(f32)).astype(bf16)


def gelu_parts(values):
    c = 0.7978845608028654
    square = values * values
    bent = jnp.tanh(c * values * (1.0 + 0.044715 * square))
    act = 0.5 * values * (1.0 + bent)
    slope = 0.5 * (1.0 + bent) + 0.5 * values * (1.0 - bent * bent) * c * (
        1.0 + 3 * 0.044715 * square
    )
    return act, slope


def after(value, *others):
    return lax.optimization_barrier((value,) + others)[0]


def add_up(parts):
    total = parts[0].astype(f32)
    for part in parts[1:]:
        total = total + part.astype(f32)
    return total


def exchange(value, axis):
    return lax.all_to_all(value, axis, 0, 0, tiled=True)


def local(
    tokens,
    cotangent,
    query_key_value_weight,
    output_weight,
    gain_one,
    gain_two,
    router_weight,
    w_in,
    w_down,
    position_bias,
    bucket,
    route,
    slot,
    dropped,
):
    seq_count, tok_count = tokens.shape[:2]
    row_count = seq_count * tok_count
    ga, gb, ctx, dp = (lax.axis_size(a) for a in ("ga", "gb", "context", "dp"))
    experts = ga * gb
    capacity = (5 * row_count + 4 * experts - 1) // (4 * experts)
    group_rows = GROUPS * tok_count
    expert_axis = ("ga", "gb")
    group_axis = ("ga", "context")
    ga_index, gb_index = lax.axis_index("ga"), lax.axis_index("gb")
    ctx_index, dp_index = lax.axis_index("context"), lax.axis_index("dp")
    group_index = lax.axis_index(group_axis)
    head_group = lax.rem(group_index, HEAD_GROUPS)
    in_order = tok_count % BLOCK != 0

    picked = {}

    def group_perm(dga, dz):
        flat = []
        for a in range(ga):
            for z in range(ctx):
                flat.append((a * ctx + z, (a + dga) % ga * ctx + (z + dz) % ctx))
        return flat

    steps = [(dga, dz) for dga in range(ga) for dz in range(ctx)]

    def sequence_at(dga, dz):
        key = dga if ctx == HEAD_GROUPS else (dga, dz)
        if key not in picked:
            to_ga = lax.rem(ga_index + dga, ga)
            to_ctx = 0 if ctx == HEAD_GROUPS else lax.rem(ctx_index + dz, ctx)
            picked[key] = pick(tokens, (to_ga * ctx + to_ctx) // HEAD_GROUPS)
        return picked[key]

    token_blocks = [
        sequence_at(*step)
        if step == (0, 0)
        else lax.ppermute(sequence_at(*step), group_axis, group_perm(*step))
        for step in steps
    ]
    source_ga = [lax.rem(ga_index - dga + ga, ga) for dga, dz in steps]
    source_ctx = [lax.rem(ctx_index - dz + ctx, ctx) for dga, dz in steps]
    source = jnp.stack([a * ctx + z for a, z in zip(source_ga, source_ctx)]).astype(jnp.int32)
    if in_order:
        group_tokens = jnp.concatenate(token_blocks, axis=0).reshape(GROUPS, tok_count, D)
        group_tokens = group_tokens[jnp.argsort(source)].reshape(group_rows, D)
        place = jnp.arange(group_rows // BLOCK, dtype=jnp.int32)
    else:
        group_tokens = jnp.concatenate(token_blocks, axis=0)
        place = jnp.repeat(source, tok_count // BLOCK) * (tok_count // BLOCK) + jnp.tile(
            jnp.arange(tok_count // BLOCK, dtype=jnp.int32), GROUPS
        )
    per_span = ctx * tok_count // BLOCK

    def begins(core):
        return ((place // per_span * gb + core) * per_span + place % per_span) * BLOCK

    query_starts = begins(gb_index)
    key_starts = jnp.concatenate(
        [begins(lax.rem(gb_index - k + gb, gb)) for k in range(gb)]
    ).astype(jnp.int32)

    weight_group = query_key_value_weight.T.reshape(3, HEAD_GROUPS, GROUP_HEADS, HEAD_DIM, D)
    weight_group = pick(weight_group, head_group, 1)
    weight_query = weight_group[0].reshape(GROUP_HEADS * HEAD_DIM, D)
    weight_kv = jnp.transpose(weight_group[1:], (1, 0, 2, 3)).reshape(-1, D)

    route_flat = route.reshape(-1)
    position = route_flat * capacity + slot.reshape(-1)
    assign = (
        (jnp.arange(experts * capacity, dtype=jnp.int32)[:, None] == position[None, :])
        & (dropped.reshape(-1) == 0)[None, :]
    ).astype(bf16)
    grad_low = cotangent.reshape(row_count, D)
    grad_buffer = matmul(assign, grad_low).astype(bf16).reshape(experts, capacity, D)
    grad_rows = exchange(grad_buffer, expert_axis).reshape(-1, D)

    onehot = (
        jnp.arange(position_bias.shape[0], dtype=jnp.int32)[:, None]
        == jnp.pad(bucket[::-1], (0, 1), constant_values=-1)[None, :]
    ).astype(f32)
    bias_heads = lax.dynamic_slice_in_dim(position_bias.T, head_group * GROUP_HEADS, GROUP_HEADS, 0)
    table = jnp.dot(bias_heads, onehot, precision=precise_mode, preferred_element_type=f32)
    table = table[:, None, :]

    def normalised(values):
        scale = lax.rsqrt(jnp.mean(values * values, axis=-1, keepdims=True) + norm_epsilon)
        return scale, values * scale

    group_normed = (normalised(group_tokens.astype(f32))[1] * gain_one).astype(bf16)
    own_kv = contract_cols(weight_kv, group_normed).astype(bf16)
    kvs = [own_kv] + [shift(own_kv, "gb", k) for k in range(1, gb)]
    query = contract_cols(weight_query, group_normed).astype(bf16)

    early = [k for k in range(1, ctx) if k == ctx // 2]
    late = [k for k in range(1, ctx) if k != ctx // 2]
    grad_blocks = {0: grad_rows}
    first_rows = after(grad_rows, group_tokens)
    for k in early:
        grad_blocks[k] = shift(first_rows, "context", k)

    attended_parts, attended, lse = attention_forward(
        query_starts, key_starts, place, table, query, kvs
    )

    def to_sources(parts):
        parts = parts.reshape(group_rows // BLOCK, -1, BLOCK)
        if in_order:
            parts = jnp.transpose(
                parts.reshape(group_rows // BLOCK, parts.shape[1], BLOCK // tok_count, tok_count),
                (0, 2, 1, 3),
            ).reshape(GROUPS, parts.shape[1], tok_count)
        return parts

    def from_sources(parts):
        if in_order:
            merged = BLOCK // tok_count
            parts = jnp.transpose(
                parts.reshape(GROUPS // merged, merged, parts.shape[1], tok_count), (0, 2, 1, 3)
            ).reshape(GROUPS // merged, parts.shape[1], BLOCK)
        return parts

    attended_low = exchange(to_sources(attended_parts), group_axis)
    attended_low = attended_low.reshape(seq_count, D, tok_count)
    second_rows = after(grad_rows, attended_low)
    for k in late:
        grad_blocks[k] = shift(second_rows, "context", k)

    inputs = tokens.reshape(row_count, D).astype(f32)
    branch = jnp.concatenate(
        [contract_rows(attended_low[i], output_weight) for i in range(seq_count)], axis=0
    )
    middle = inputs + branch
    scale_two, unit_two = normalised(middle)
    normalized_second = unit_two * gain_two
    router_logits = jnp.dot(
        normalized_second, router_weight, precision=precise_mode, preferred_element_type=f32
    )
    router = jax.nn.softmax(router_logits, axis=-1)
    chosen = (route_flat[:, None] == jnp.arange(experts, dtype=jnp.int32)[None, :]).astype(f32)
    gate = jnp.sum(router * chosen, axis=-1, keepdims=True)

    gate_high, gate_low = split_halves(gate)
    payload = jnp.concatenate(
        [
            normalized_second.astype(bf16),
            gate_high,
            gate_low,
            jnp.zeros((row_count, 126), bf16),
        ],
        axis=1,
    )
    buffer = matmul(assign, payload).astype(bf16).reshape(experts, capacity, D + 128)
    received = exchange(buffer, expert_axis).reshape(-1, D + 128)
    row_blocks = spread([received[:, :D]] * ctx, "context")

    local_in = w_in[0]
    local_down = w_down[0]
    ones = jnp.ones((8, local_in.shape[1]), bf16)
    hidden_blocks, pre_blocks, back_parts, gate_parts = [], [], [], []
    for k in range(ctx):
        grad_hidden = matmul(after(grad_blocks[k], received), local_down)
        act, slope = gelu_parts(matmul(row_blocks[k], local_in))
        hidden = act.astype(bf16)
        grad_pre = grad_hidden * slope
        hidden_blocks.append(hidden)
        pre_blocks.append(grad_pre.astype(bf16))
        back_parts.append(contract_cols(pre_blocks[k], local_in).astype(bf16))
        gate_parts.append(contract_cols(ones, (grad_hidden * hidden.astype(f32)).astype(bf16)))

    back_sum = add_up(give_back(back_parts, "context")).astype(bf16)
    gate_sum = add_up(give_back(gate_parts, "context"))
    gate_halves = split_halves(gate_sum[:1])
    gate_column = contract_rows(
        jnp.concatenate(gate_halves + (jnp.zeros((6, gate_sum.shape[1]), bf16),), axis=0),
        jnp.eye(8, 128, dtype=bf16),
    ).astype(bf16)
    back_rows = jnp.concatenate([back_sum, gate_column], axis=1)
    back_rows = exchange(back_rows.reshape(experts, capacity, D + 128), expert_axis)
    back_rows = contract_rows(assign, back_rows.reshape(-1, D + 128))
    grad_sent = back_rows[:, :D] * gate
    grad_gate = back_rows[:, D : D + 1] + back_rows[:, D + 1 : D + 2]

    grad_out = grad_low.astype(f32)
    grad_logits = grad_gate * gate * (chosen - router)
    grad_normed_two = grad_sent + lax.dot_general(
        grad_logits,
        router_weight,
        (((1,), (1,)), ((), ())),
        precision=precise_mode,
        preferred_element_type=f32,
    )
    scaled_two = gain_two * grad_normed_two
    cube_two = scale_two * scale_two * scale_two
    grad_middle = (
        grad_out
        + scale_two * scaled_two
        - middle * cube_two * jnp.mean(scaled_two * middle, axis=-1, keepdims=True)
    )
    grad_branch = grad_middle.astype(bf16)

    grad_heads = jnp.concatenate(
        [
            contract_cols(output_weight, grad_branch[i * tok_count : (i + 1) * tok_count])
            for i in range(seq_count)
        ],
        axis=0,
    ).astype(bf16)
    grad_heads = exchange(
        grad_heads.reshape(GROUPS, GROUP_HEADS * HEAD_DIM, tok_count), group_axis
    )

    def out_part(k, *others):
        return contract_cols(after(hidden_blocks[k], *others), local_down).astype(bf16)

    result_parts = {0: out_part(0, back_sum)}
    for k in early:
        result_parts[k] = shift(out_part(k, back_sum), "context", -k)
    for k in late:
        result_parts[k] = shift(after(out_part(k, back_sum), grad_heads), "context", -k)
    gate_rows = after(received[:, D:], back_sum)
    gate_blocks = spread([gate_rows] * ctx, "context")

    outs = attention_backward(
        query_starts,
        key_starts,
        place,
        table,
        query,
        attended,
        lse,
        from_sources(grad_heads),
        kvs,
    )
    grad_query, grad_kvs, grad_table = outs[0], outs[1:-1], outs[-1]
    grad_kv = add_up(give_back(grad_kvs, "gb")).astype(bf16)
    grad_projected = jnp.concatenate([grad_query, grad_kv], axis=0)
    weight_all = jnp.concatenate([weight_query, weight_kv], axis=0)
    part_normed = contract_rows(grad_projected, weight_all).astype(bf16)
    part_normed = part_normed.reshape(GROUPS, tok_count, D)
    if in_order:
        part_normed = part_normed[source]
    returned_normed = [
        part_normed[0]
        if step == (0, 0)
        else lax.ppermute(
            part_normed[i], group_axis, [(b, a) for a, b in group_perm(*step)]
        )
        for i, step in enumerate(steps)
    ]
    sums = [0.0] * seq_count
    for (dga, dz), part in zip(steps, returned_normed):
        from_ga = lax.rem(ga_index + dga, ga)
        from_ctx = lax.rem(ctx_index + dz, ctx)
        of_sequence = (from_ga * ctx + from_ctx) // HEAD_GROUPS
        for i in range(seq_count):
            sums[i] = sums[i] + jnp.where(of_sequence == i, part.astype(f32), 0.0)
    grad_normed = jnp.concatenate(sums, axis=0)
    scale_one = normalised(inputs)[0]
    scaled_one = gain_one * grad_normed
    cube_one = scale_one * scale_one * scale_one
    grad_inputs = (
        grad_middle
        + scale_one * scaled_one
        - inputs * cube_one * jnp.mean(scaled_one * inputs, axis=-1, keepdims=True)
    )

    qkv_part = lax.dot_general(
        group_normed, grad_projected, (((0,), (1,)), ((), ())), preferred_element_type=f32
    )
    own_rows = D // (ga * gb * ctx * dp)
    qkv_part = scatter_rows(qkv_part)
    by_group = [0.0] * HEAD_GROUPS
    for k in range(ctx):
        part = pick(qkv_part, lax.rem(ctx_index + k, ctx))
        if k:
            part = shift(part.astype(bf16), "context", k)
        by_group[k % HEAD_GROUPS] = by_group[k % HEAD_GROUPS] + part.astype(f32)
    by_group = jnp.stack(by_group)
    order = lax.rem(
        ctx_index - jnp.arange(HEAD_GROUPS, dtype=jnp.int32) + 2 * HEAD_GROUPS, HEAD_GROUPS
    )
    by_group = jnp.stack([pick(by_group, order[i]) for i in range(HEAD_GROUPS)], axis=1)
    width = GROUP_HEADS * HEAD_DIM
    query_cols = by_group[:, :, :width].reshape(own_rows, 1, D)
    kv_cols = by_group[:, :, width:].reshape(own_rows, HEADS, 2, HEAD_DIM)
    kv_cols = jnp.transpose(kv_cols, (0, 2, 1, 3)).reshape(own_rows, 2, D)
    qkv_total = jnp.concatenate([query_cols, kv_cols], axis=1).reshape(own_rows, 3 * D)
    first_row = (lax.axis_index(("ga", "gb", "context", "dp"))) * own_rows
    weight_rows = lax.dynamic_slice_in_dim(query_key_value_weight, first_row, own_rows, 0)
    gain_rows = lax.dynamic_slice_in_dim(gain_one, first_row, own_rows, 0)
    gain_one_total = jnp.sum(qkv_total * weight_rows.astype(f32), axis=1) / gain_rows

    result = add_up([result_parts[k] for k in range(ctx)]).astype(bf16)
    returned_rows = exchange(result.reshape(experts, capacity, D), expert_axis).reshape(-1, D)
    returned = contract_rows(assign, returned_rows)
    output = (middle + gate * returned).astype(bf16)

    all_rows = jnp.concatenate(row_blocks, axis=0)
    all_grads = jnp.concatenate([grad_blocks[k] for k in range(ctx)], axis=0)
    all_gates = jnp.concatenate(gate_blocks, axis=0)[:, :2].astype(f32)
    all_gates = all_gates[:, :1] + all_gates[:, 1:2]
    all_gates = after(all_gates, grad_query)
    all_hidden = jnp.concatenate(hidden_blocks, axis=0)
    all_pre = (jnp.concatenate(pre_blocks, axis=0).astype(f32) * all_gates).astype(bf16)
    all_returned = (all_gates * all_grads.astype(f32)).astype(bf16)
    down_part = contract_rows(all_returned, all_hidden)
    in_part = contract_rows(all_rows, all_pre)
    in_grad = scatter_sum(in_part.reshape(D, dp, -1), "dp", 1)
    down_grad = scatter_sum(down_part.reshape(D, dp, -1), "dp", 1)

    late_branch = after(grad_branch, grad_heads)
    out_part_grad = add_up(
        [
            matmul(attended_low[i], late_branch[i * tok_count : (i + 1) * tok_count])
            for i in range(seq_count)
        ]
    )
    router_grad = lax.dot_general(
        normalized_second,
        grad_logits,
        (((0,), (0,)), ((), ())),
        precision=precise_mode,
        preferred_element_type=f32,
    )
    gain_two_grad = jnp.sum(grad_normed_two * unit_two, axis=0)
    dense = jnp.concatenate(
        [out_part_grad, router_grad, gain_two_grad[:, None], jnp.zeros((D, 123), f32)], axis=1
    )
    dense = scatter_sum(scatter_rows(dense), "context", 0)
    span = bucket.shape[0]
    grad_table = jnp.pad(grad_table, ((0, 0), (0, 0), (0, 8)))
    by_offset = grad_table[:, 0, 1 : 1 + span]
    for r in range(1, 8):
        by_offset = by_offset + grad_table[:, r, r + 1 : r + 1 + span]
    bias_part = lax.dot_general(
        by_offset,
        onehot[:, :span],
        (((1,), (1,)), ((), ())),
        precision=precise_mode,
        preferred_element_type=f32,
    )
    bias_grad = lax.dynamic_update_slice_in_dim(
        jnp.zeros((HEADS, bias_part.shape[1]), f32), bias_part, head_group * GROUP_HEADS, 0
    )
    bias_grad = sum_everywhere(bias_grad, ("gb", "ga", "dp", "context")).T
    return (
        output.reshape(seq_count, tok_count, D),
        grad_inputs.astype(bf16).reshape(seq_count, tok_count, D),
        qkv_total,
        dense[:, :D],
        gain_one_total,
        dense[:, D + 4],
        dense[:, D : D + 4],
        in_grad[None],
        down_grad[None],
        bias_grad,
    )


def solution(mesh):
    ctx = mesh.shape["context"]
    ga = max(GROUPS // ctx, 1)
    gb = mesh.shape["expert"] // ga
    fine = Mesh(
        mesh.devices.reshape(ga, gb, ctx, mesh.shape["dp"]), ("ga", "gb", "context", "dp")
    )
    expert = ("ga", "gb")
    blocks = ("ga", "gb", "context")
    everywhere = ("ga", "gb", "context", "dp")
    return jax.shard_map(
        local,
        mesh=fine,
        in_specs=(
            P("dp", blocks, None),
            P("dp", blocks, None),
            P(),
            P(),
            P(),
            P(),
            P(),
            P(expert, None, "context"),
            P(expert, None, "context"),
            P(),
            P(),
            P("dp", blocks),
            P("dp", blocks),
            P("dp", blocks),
        ),
        out_specs=(
            P("dp", blocks, None),
            P("dp", blocks, None),
            P(everywhere, None),
            P(everywhere, None),
            P(everywhere),
            P(everywhere),
            P(everywhere, None),
            P(expert, None, ("context", "dp")),
            P(expert, None, ("context", "dp")),
            P(),
        ),
        check_vma=False,
    )
```

```python
import functools

import jax
import jax.numpy as jnp
from jax import lax
from jax.experimental import pallas as pl
from jax.experimental.pallas import tpu as pltpu
from jax.sharding import Mesh, PartitionSpec as P

D = 768
HEADS = 12
HEAD_DIM = 64
GROUP_HEADS = 3
HEAD_GROUPS = HEADS // GROUP_HEADS
SEQ_DEV = 2
GROUPS = SEQ_DEV * HEAD_GROUPS
WIDTH = 256
BLOCK = 128

norm_epsilon = 1e-06
score_scale = 0.125
precise_mode = lax.Precision.HIGHEST
vmem_bytes = 50 * 1024 * 1024
f32 = jnp.float32
bf16 = jnp.bfloat16


def matmul(left, right):
    return jnp.dot(left, right, preferred_element_type=f32)


def contract_rows(left, right):
    return lax.dot_general(left, right, (((0,), (0,)), ((), ())), preferred_element_type=f32)


def contract_cols(left, right):
    return lax.dot_general(left, right, (((1,), (1,)), ((), ())), preferred_element_type=f32)


def skewed_table(table_row):
    wide = jnp.broadcast_to(table_row, (BLOCK, table_row.shape[1]))
    return pltpu.roll(wide, 1, 1, stride=1, stride_axis=0)


def key_rows(kv_refs, rows):
    for part, kv_ref in enumerate(kv_refs):
        count = kv_ref.shape[1]
        rows[part * count : (part + 1) * count, :] = kv_ref[...].T


def begins(block, core, cores, span_blocks):
    return ((block // span_blocks * cores + core) * span_blocks + block % span_blocks) * BLOCK


def key_begins(offset, core, parts, own_count, span_blocks):
    part, inside = divmod(offset, own_count)
    owner = lax.rem(core - part + parts, parts)
    return begins(inside // BLOCK, owner, parts, span_blocks)


def forward_kernel(parts, span_blocks, core_ref, table_ref, q_ref, *refs):
    kv_refs = refs[:parts]
    out_ref, full_ref, lse_ref, skew, score, weight, rows = refs[parts:]
    half = table_ref.shape[2] // 2
    own_count = kv_refs[0].shape[1]
    key_count = parts * own_count
    skew[...] = skewed_table(table_ref[0])
    key_rows(kv_refs, rows)
    blocks = WIDTH // BLOCK
    core = core_ref[0]

    def one_tile(tile, carry):
        lanes = pl.ds(pl.multiple_of(tile * WIDTH, WIDTH), WIDTH)
        query = q_ref[:, lanes] * jnp.asarray(score_scale, bf16)
        query = jnp.concatenate([query, jnp.zeros_like(query)], axis=0)
        start = half + begins(tile * blocks, core, parts, span_blocks)
        top = jnp.full((8, WIDTH), -jnp.inf, f32)
        for block in range(key_count // BLOCK):
            offset = block * BLOCK
            behind = start - key_begins(offset, core, parts, own_count, span_blocks)
            bias = skew[:, pl.ds(pl.multiple_of(behind, BLOCK), WIDTH)]
            part = matmul(rows[offset : offset + BLOCK, :], query) + bias
            score[offset : offset + BLOCK, :] = part
            top = jnp.maximum(top, jnp.max(part.reshape(BLOCK // 8, 8, WIDTH), axis=0))
        top = jnp.max(top, axis=0, keepdims=True)
        total = jnp.zeros((8, WIDTH), f32)
        for block in range(key_count // BLOCK):
            offset = block * BLOCK
            part = jnp.exp(score[offset : offset + BLOCK, :] - top)
            total = total + jnp.sum(part.reshape(BLOCK // 8, 8, WIDTH), axis=0)
            weight[offset : offset + BLOCK, :] = part.astype(bf16)
        total = jnp.sum(total, axis=0, keepdims=True)
        blended = jnp.zeros((HEAD_DIM, WIDTH), f32)
        for part, kv_ref in enumerate(kv_refs):
            own = weight[part * own_count : (part + 1) * own_count, :]
            blended = blended + matmul(kv_ref[HEAD_DIM:, :], own)
        blended = blended / total
        full_ref[:, lanes] = blended
        for i in range(blocks):
            piece = blended[:, i * BLOCK : (i + 1) * BLOCK]
            out_ref[tile * blocks + i] = piece.astype(bf16)
        lse_ref[0, :, lanes] = top + jnp.log(total)
        return carry

    lax.fori_loop(0, q_ref.shape[1] // WIDTH, one_tile, 0)


def backward_kernel(
    parts, span_blocks, core_ref, table_ref, q_ref, full_ref, lse_ref, grad_ref, *refs
):
    kv_refs = refs[:parts]
    dq_ref = refs[parts]
    dkv_refs = refs[parts + 1 : 2 * parts + 1]
    dtable_ref, skew, dskew, rows, dkv = refs[2 * parts + 1 :]
    span = table_ref.shape[2]
    half = span // 2
    own_count = kv_refs[0].shape[1]
    key_count = parts * own_count
    skew[...] = skewed_table(table_ref[0])
    key_rows(kv_refs, rows)
    dskew[...] = jnp.zeros_like(dskew)
    dkv[...] = jnp.zeros_like(dkv)
    blocks = WIDTH // BLOCK
    step = 2 * BLOCK
    core = core_ref[0]

    def one_tile(tile, carry):
        lanes = pl.ds(pl.multiple_of(tile * WIDTH, WIDTH), WIDTH)
        query = q_ref[:, lanes] * jnp.asarray(score_scale, bf16)
        grad = jnp.concatenate(
            [grad_ref[tile * blocks + i] for i in range(blocks)], axis=1
        )
        lse = lse_ref[0, :, lanes]
        delta = jnp.sum(grad.astype(f32) * full_ref[:, lanes], axis=0, keepdims=True)
        query = jnp.concatenate([query, jnp.zeros_like(query)], axis=0)
        grad = jnp.concatenate([jnp.zeros_like(grad), grad], axis=0)
        query_rows = query.T
        grad_rows = grad.T
        start = half + begins(tile * blocks, core, parts, span_blocks)
        dq = jnp.zeros((HEAD_DIM, WIDTH), f32)
        for offset in range(0, key_count, step):
            keys = rows[offset : offset + step, :]
            raw = matmul(keys, query)
            dprob = matmul(keys, grad)
            probs = []
            dscores = []
            for inner in range(0, step, BLOCK):
                behind = start - key_begins(offset + inner, core, parts, own_count, span_blocks)
                here = pl.ds(pl.multiple_of(behind, BLOCK), WIDTH)
                own = slice(inner, inner + BLOCK)
                prob = jnp.exp(raw[own] + skew[:, here] - lse)
                dscore = prob * (dprob[own] - delta)
                dskew[:, here] += dscore
                probs.append(prob.astype(bf16))
                dscores.append(dscore.astype(bf16))
            prob = jnp.concatenate(probs, axis=0)
            dscore = jnp.concatenate(dscores, axis=0)
            dkv[offset : offset + step, :] += matmul(dscore, query_rows) + matmul(prob, grad_rows)
            part, inside = divmod(offset, own_count)
            dq = dq + matmul(kv_refs[part][:HEAD_DIM, inside : inside + step], dscore)
        dq_ref[:, lanes] = (dq * score_scale).astype(bf16)
        return carry

    lax.fori_loop(0, q_ref.shape[1] // WIDTH, one_tile, 0)
    for part, dkv_ref in enumerate(dkv_refs):
        dkv_ref[...] = dkv[part * own_count : (part + 1) * own_count, :].T.astype(bf16)
    folded = dskew[...]
    count = BLOCK
    while count > 1:
        count //= 2
        folded = folded[:count] + pltpu.roll(folded[count:], span - count, 1)
    dtable_ref[0] = pltpu.roll(folded, span - 1, 1)


def stack_spec(*shape):
    return pl.BlockSpec((1,) + shape, lambda head: (head, 0, 0))


def rows_spec(*shape):
    return pl.BlockSpec(shape, lambda head: (head, 0))


def place_spec(blocks):
    return pl.BlockSpec((blocks, HEAD_DIM, BLOCK), lambda head: (0, head, 0))


def attention_forward(span_blocks, core, table, query, kvs):
    count, span, parts = query.shape[1], table.shape[2], len(kvs)
    keys = parts * count
    scalars = pl.BlockSpec(memory_space=pltpu.SMEM)
    return pl.pallas_call(
        functools.partial(forward_kernel, parts, span_blocks),
        grid=(GROUP_HEADS,),
        in_specs=[scalars, stack_spec(1, span), rows_spec(HEAD_DIM, count)]
        + [rows_spec(2 * HEAD_DIM, count)] * parts,
        out_specs=[
            place_spec(count // BLOCK),
            rows_spec(HEAD_DIM, count),
            stack_spec(1, count),
        ],
        out_shape=[
            jax.ShapeDtypeStruct((count // BLOCK, GROUP_HEADS * HEAD_DIM, BLOCK), bf16),
            jax.ShapeDtypeStruct((GROUP_HEADS * HEAD_DIM, count), f32),
            jax.ShapeDtypeStruct((GROUP_HEADS, 1, count), f32),
        ],
        scratch_shapes=[
            pltpu.VMEM((BLOCK, span), f32),
            pltpu.VMEM((keys, WIDTH), f32),
            pltpu.VMEM((keys, WIDTH), bf16),
            pltpu.VMEM((keys, 2 * HEAD_DIM), bf16),
        ],
        compiler_params=pltpu.CompilerParams(vmem_limit_bytes=vmem_bytes),
        cost_estimate=pl.CostEstimate(
            flops=4 * GROUP_HEADS * HEAD_DIM * count * keys * 4,
            bytes_accessed=4 * GROUP_HEADS * HEAD_DIM * (count + keys) * 2,
            transcendentals=GROUP_HEADS * count * keys,
        ),
        name="attention_forward",
    )(core, table, query, *kvs)


def attention_backward(span_blocks, core, table, query, full, lse, grad, kvs):
    count, span, parts = query.shape[1], table.shape[2], len(kvs)
    keys = parts * count
    scalars = pl.BlockSpec(memory_space=pltpu.SMEM)
    return pl.pallas_call(
        functools.partial(backward_kernel, parts, span_blocks),
        grid=(GROUP_HEADS,),
        in_specs=[
            scalars,
            stack_spec(1, span),
            rows_spec(HEAD_DIM, count),
            rows_spec(HEAD_DIM, count),
            stack_spec(1, count),
            place_spec(count // BLOCK),
        ]
        + [rows_spec(2 * HEAD_DIM, count)] * parts,
        out_specs=[rows_spec(HEAD_DIM, count)]
        + [rows_spec(2 * HEAD_DIM, count)] * parts
        + [stack_spec(1, span)],
        out_shape=[jax.ShapeDtypeStruct((GROUP_HEADS * HEAD_DIM, count), bf16)]
        + [jax.ShapeDtypeStruct((GROUP_HEADS * 2 * HEAD_DIM, count), bf16)] * parts
        + [jax.ShapeDtypeStruct((GROUP_HEADS, 1, span), f32)],
        scratch_shapes=[
            pltpu.VMEM((BLOCK, span), f32),
            pltpu.VMEM((BLOCK, span), f32),
            pltpu.VMEM((keys, 2 * HEAD_DIM), bf16),
            pltpu.VMEM((keys, 2 * HEAD_DIM), f32),
        ],
        compiler_params=pltpu.CompilerParams(vmem_limit_bytes=vmem_bytes),
        cost_estimate=pl.CostEstimate(
            flops=10 * GROUP_HEADS * HEAD_DIM * count * keys * 4,
            bytes_accessed=4 * GROUP_HEADS * HEAD_DIM * (count + keys) * 4,
            transcendentals=GROUP_HEADS * count * keys,
        ),
        name="attention_backward",
    )(core, table, query, full, lse, grad, *kvs)


def shift(value, axis, step):
    size = lax.axis_size(axis)
    return lax.ppermute(value, axis, [(i, (i + step) % size) for i in range(size)])


def pick(value, index, dim=0):
    return lax.dynamic_index_in_dim(value, index, dim, keepdims=False)


def spread(parts, axis):
    return [parts[0]] + [shift(parts[k], axis, k) for k in range(1, len(parts))]


def give_back(parts, axis):
    return [parts[0]] + [shift(parts[k], axis, -k) for k in range(1, len(parts))]


def scatter_sum(value, axis, dim, wire=bf16):
    size = lax.axis_size(axis)
    index = lax.axis_index(axis)
    if size == 2:
        low = lax.index_in_dim(value, 0, dim, keepdims=False)
        high = lax.index_in_dim(value, 1, dim, keepdims=False)
        first = index == 0
        got = shift(jnp.where(first, high, low).astype(wire), axis, 1)
        return jnp.where(first, low, high).astype(f32) + got.astype(f32)
    total = pick(value, index, dim).astype(f32)
    for k in range(1, size):
        part = pick(value, lax.rem(index + k, size), dim).astype(wire)
        total = total + shift(part, axis, k).astype(f32)
    return total


def sum_everywhere(value, axes):
    for axis in axes:
        size = lax.axis_size(axis)
        step = 1
        while step < size:
            value = value + lax.ppermute(value, axis, [(i, i ^ step) for i in range(size)])
            step *= 2
    return value


def scatter_rows(value, *others):
    ga, gb, ctx, dp = (lax.axis_size(a) for a in ("ga", "gb", "context", "dp"))
    rows, cols = value.shape
    own = rows // (ga * gb * ctx * dp)
    value = value.reshape(ga, gb, ctx * dp * own, cols)
    value = after(scatter_sum(value, "gb", 1), *others)
    value = scatter_sum(value, "ga", 0)
    value = value.reshape(ctx, dp, own, cols)
    return scatter_sum(value, "dp", 1)


def split_halves(value):
    high = value.astype(bf16)
    return high, (value - high.astype(f32)).astype(bf16)


def gelu_parts(values):
    c = 0.7978845608028654
    square = values * values
    bent = jnp.tanh(c * values * (1.0 + 0.044715 * square))
    act = 0.5 * values * (1.0 + bent)
    slope = 0.5 * (1.0 + bent) + 0.5 * values * (1.0 - bent * bent) * c * (
        1.0 + 3 * 0.044715 * square
    )
    return act, slope


def after(value, *others):
    width = value.shape[-1]
    for other in others:
        first = other.reshape(-1, other.shape[-1])[:1]
        if first.shape[1] < width:
            first = jnp.concatenate([first] * -(-width // first.shape[1]), axis=1)
        first = first[:, :width]
        value = jnp.where(first == first, value, jnp.zeros_like(value))
    return value


def add_up(parts):
    total = parts[0].astype(f32)
    for part in parts[1:]:
        total = total + part.astype(f32)
    return total


def exchange(value, axis):
    return lax.all_to_all(value, axis, 0, 0, tiled=True)


def local(
    tokens,
    cotangent,
    query_key_value_weight,
    output_weight,
    gain_one,
    gain_two,
    router_weight,
    w_in,
    w_down,
    position_bias,
    bucket,
    route,
    slot,
    dropped,
):
    seq_count, tok_count = tokens.shape[:2]
    row_count = seq_count * tok_count
    ga, gb, ctx, dp = (lax.axis_size(a) for a in ("ga", "gb", "context", "dp"))
    experts = ga * gb
    capacity = (5 * row_count + 4 * experts - 1) // (4 * experts)
    group_rows = GROUPS * tok_count
    expert_axis = ("ga", "gb")
    group_axis = ("ga", "context")
    ga_index, gb_index, ctx_index = (lax.axis_index(a) for a in ("ga", "gb", "context"))
    group_index = lax.axis_index(group_axis)
    head_group = lax.rem(group_index, HEAD_GROUPS)
    in_order = tok_count % BLOCK != 0

    outgoing = jnp.broadcast_to(tokens[:, None], (SEQ_DEV, HEAD_GROUPS, tok_count, D))
    group_tokens = exchange(outgoing.reshape(GROUPS, tok_count, D), group_axis)
    group_tokens = group_tokens.reshape(group_rows, D)
    span_blocks = ctx * tok_count // BLOCK
    core = gb_index.astype(jnp.int32)[None]

    weight_group = query_key_value_weight.T.reshape(3, HEAD_GROUPS, GROUP_HEADS, HEAD_DIM, D)
    weight_group = pick(weight_group, head_group, 1)
    weight_query = weight_group[0].reshape(GROUP_HEADS * HEAD_DIM, D)
    weight_kv = jnp.transpose(weight_group[1:], (1, 0, 2, 3)).reshape(-1, D)

    def pair(value):
        return lax.ppermute(value, "context", [(i, i ^ 1) for i in range(ctx)])

    def every_other(value):
        return [value] + [shift(value, "context", 2 * k) for k in range(1, ctx // 2)]

    def every_other_back(parts):
        return [parts[0]] + [shift(parts[k], "context", -2 * k) for k in range(1, len(parts))]


    dp_index = lax.axis_index("dp")

    def by_owner(weight):
        cut = weight.shape[1] // dp
        if dp == 2:
            low, high = weight[:, :cut], weight[:, cut:]
            first = dp_index == 0
            parts = [jnp.where(first, low, high), jnp.where(first, high, low)]
            return jnp.concatenate(parts, axis=1)
        return jnp.roll(weight.reshape(D, dp, cut), -dp_index, axis=1).reshape(D, -1)

    own_in, own_down = by_owner(w_in[0]), by_owner(w_down[0])

    route_flat = route.reshape(-1)
    position = route_flat * capacity + slot.reshape(-1)
    assign = (
        (jnp.arange(experts * capacity, dtype=jnp.int32)[:, None] == position[None, :])
        & (dropped.reshape(-1) == 0)[None, :]
    ).astype(bf16)
    grad_low = cotangent.reshape(row_count, D)
    grad_buffer = matmul(assign, grad_low).astype(bf16).reshape(experts, capacity, D)
    expert_index = lax.axis_index(expert_axis)
    grad_rows = jnp.zeros((experts, capacity, D), bf16)
    for k in range(experts):
        part = pick(grad_buffer, lax.rem(expert_index + k, experts))
        part = shift(part, expert_axis, k) if k else part
        came_from = lax.rem(expert_index - k + experts, experts)
        grad_rows = lax.dynamic_update_index_in_dim(grad_rows, part, came_from, 0)
    grad_rows = grad_rows.reshape(-1, D)

    onehot = (
        jnp.arange(position_bias.shape[0], dtype=jnp.int32)[:, None]
        == jnp.pad(bucket[::-1], (0, 1), constant_values=-1)[None, :]
    ).astype(f32)
    bias_heads = lax.dynamic_slice_in_dim(position_bias.T, head_group * GROUP_HEADS, GROUP_HEADS, 0)
    table = jnp.dot(bias_heads, onehot, precision=precise_mode, preferred_element_type=f32)
    table = table[:, None, :]

    def normalised(values):
        scale = lax.rsqrt(jnp.mean(values * values, axis=-1, keepdims=True) + norm_epsilon)
        return scale, values * scale

    group_normed = (normalised(group_tokens.astype(f32))[1] * gain_one).astype(bf16)
    own_kv = contract_cols(weight_kv, group_normed).astype(bf16)
    kvs = [own_kv] + [shift(own_kv, "gb", k) for k in range(1, gb)]
    query = contract_cols(weight_query, group_normed).astype(bf16)
    query = after(query, grad_rows)

    grad_blocks = every_other(after(grad_rows, group_normed))
    both_in = [own_in, pair(after(own_in, group_normed))]

    attended_parts, attended, lse = attention_forward(
        span_blocks, core, table, query, kvs
    )

    def to_sources(parts):
        parts = parts.reshape(group_rows // BLOCK, -1, BLOCK)
        if in_order:
            parts = jnp.transpose(
                parts.reshape(group_rows // BLOCK, parts.shape[1], BLOCK // tok_count, tok_count),
                (0, 2, 1, 3),
            ).reshape(GROUPS, parts.shape[1], tok_count)
        return parts

    def from_sources(parts):
        if in_order:
            merged = BLOCK // tok_count
            parts = jnp.transpose(
                parts.reshape(GROUPS // merged, merged, parts.shape[1], tok_count), (0, 2, 1, 3)
            ).reshape(GROUPS // merged, parts.shape[1], BLOCK)
        return parts

    attended_low = exchange(to_sources(attended_parts), group_axis)
    attended_low = attended_low.reshape(seq_count, D, tok_count)
    both_down = [own_down, pair(after(own_down, attended_low))]

    inputs = tokens.reshape(row_count, D).astype(f32)
    branch = jnp.concatenate(
        [contract_rows(attended_low[i], output_weight) for i in range(seq_count)], axis=0
    )
    middle = inputs + branch
    scale_two, unit_two = normalised(middle)
    normalized_second = unit_two * gain_two
    router_logits = jnp.dot(
        normalized_second, router_weight, precision=precise_mode, preferred_element_type=f32
    )
    router = jax.nn.softmax(router_logits, axis=-1)
    chosen = (route_flat[:, None] == jnp.arange(experts, dtype=jnp.int32)[None, :]).astype(f32)
    gate = jnp.sum(router * chosen, axis=-1, keepdims=True)

    gate_high, gate_low = split_halves(gate)
    payload = jnp.concatenate(
        [
            after(
                normalized_second.astype(bf16), *grad_blocks[1:], both_in[1]
            ),
            gate_high,
            gate_low,
            jnp.zeros((row_count, 126), bf16),
        ],
        axis=1,
    )
    buffer = matmul(assign, payload).astype(bf16).reshape(experts, capacity, D + 128)
    received = exchange(buffer, expert_axis).reshape(-1, D + 128)
    row_total = received.shape[0]
    gate_rows = contract_cols(jnp.eye(16, 128, dtype=bf16), received[:, D:]).astype(bf16)
    gate_rows = jnp.pad(gate_rows, ((0, 0), (0, -row_total % D)))[:, :D]
    sent_blocks = every_other(jnp.concatenate([received[:, :D], gate_rows], axis=0))
    row_blocks = [block[:row_total] for block in sent_blocks]
    gate_blocks = [block[row_total:, :row_total] for block in sent_blocks]
    gate_width = jnp.where(jnp.arange(16)[:, None] < 2, 1.0, 0.0) * jnp.ones((1, D), f32)
    gate_width = gate_width.astype(bf16)

    ones = jnp.ones((8, own_in.shape[1]), bf16)
    hidden_blocks, pre_blocks, back_parts = [], [], []
    for rows_now, grads_now in zip(row_blocks, grad_blocks):
        hidden_blocks.append([])
        pre_blocks.append([])
        back = gate_part = 0.0
        for weight_in, weight_down in zip(both_in, both_down):
            grad_hidden = matmul(after(grads_now, sent_blocks[0]), weight_down)
            act, slope = gelu_parts(matmul(rows_now, weight_in))
            hidden = act.astype(bf16)
            grad_pre = (grad_hidden * slope).astype(bf16)
            hidden_blocks[-1].append(hidden)
            pre_blocks[-1].append(grad_pre)
            back = back + contract_cols(grad_pre, weight_in)
            product = (grad_hidden * hidden.astype(f32)).astype(bf16)
            gate_part = gate_part + contract_cols(ones, product)[:1]
        gate_part = jnp.concatenate(
            split_halves(gate_part) + (jnp.zeros((14, row_total), bf16),), axis=0
        )
        gate_part = jnp.pad(gate_part, ((0, 0), (0, -row_total % D)))[:, :D]
        back = jnp.concatenate([back.astype(bf16), gate_part], axis=0)
        back_parts.append(after(back, *sent_blocks[1:]))

    back_total = add_up(every_other_back(back_parts))
    back_sum = back_total[:row_total].astype(bf16)
    gate_sum = back_total[row_total : row_total + 2, :row_total]
    gate_sum = gate_sum[:1] + gate_sum[1:]
    gate_halves = split_halves(gate_sum[:1])
    gate_column = contract_rows(
        jnp.concatenate(gate_halves + (jnp.zeros((6, gate_sum.shape[1]), bf16),), axis=0),
        jnp.eye(8, 128, dtype=bf16),
    ).astype(bf16)
    back_rows = jnp.concatenate([back_sum, gate_column], axis=1)
    back_rows = exchange(back_rows.reshape(experts, capacity, D + 128), expert_axis)
    back_rows = contract_rows(assign, back_rows.reshape(-1, D + 128))
    grad_sent = back_rows[:, :D] * gate
    grad_gate = back_rows[:, D : D + 1] + back_rows[:, D + 1 : D + 2]

    grad_out = grad_low.astype(f32)
    grad_logits = grad_gate * gate * (chosen - router)
    grad_normed_two = grad_sent + lax.dot_general(
        grad_logits,
        router_weight,
        (((1,), (1,)), ((), ())),
        precision=precise_mode,
        preferred_element_type=f32,
    )
    scaled_two = gain_two * grad_normed_two
    cube_two = scale_two * scale_two * scale_two
    grad_middle = (
        grad_out
        + scale_two * scaled_two
        - middle * cube_two * jnp.mean(scaled_two * middle, axis=-1, keepdims=True)
    )
    grad_branch = grad_middle.astype(bf16)

    grad_heads = jnp.concatenate(
        [
            contract_cols(output_weight, grad_branch[i * tok_count : (i + 1) * tok_count])
            for i in range(seq_count)
        ],
        axis=0,
    ).astype(bf16)
    grad_heads = exchange(
        grad_heads.reshape(GROUPS, GROUP_HEADS * HEAD_DIM, tok_count), group_axis
    )

    out_parts = [
        add_up([contract_cols(h, w) for h, w in zip(hidden, both_down)]).astype(bf16)
        for hidden in hidden_blocks
    ]
    result_parts = every_other_back(
        out_parts[:1] + [after(part, grad_heads) for part in out_parts[1:]]
    )

    all_rows = jnp.concatenate(row_blocks, axis=0)
    all_grads = jnp.concatenate(grad_blocks, axis=0)
    all_gates = contract_rows(jnp.concatenate(gate_blocks, axis=1), gate_width)
    all_returned = (all_gates * all_grads.astype(f32)).astype(bf16)
    all_hidden = [jnp.concatenate(blocks, axis=0) for blocks in zip(*hidden_blocks)]
    all_pre = [
        (jnp.concatenate(blocks, axis=0).astype(f32) * all_gates[:, :1]).astype(bf16)
        for blocks in zip(*pre_blocks)
    ]
    cut = own_in.shape[1] // dp

    def reduced(left, rights):
        def columns(k):
            piece = [right[:, k * cut : (k + 1) * cut] for right in rights]
            return contract_rows(left, jnp.concatenate(piece, axis=1)).astype(bf16)

        came = [shift(columns(k), "dp", k) for k in range(1, dp)]
        mine = columns(0)
        own = add_up([mine[:, :cut]] + [part[:, :cut] for part in came])
        partner = add_up([mine[:, cut:]] + [part[:, cut:] for part in came]).astype(bf16)
        return own, partner

    in_grad, in_partner = reduced(all_rows, all_pre)
    down_grad, down_partner = reduced(all_returned, all_hidden)
    in_came = pair(after(in_partner, back_sum))
    down_came = pair(after(down_partner, grad_heads))
    grad_heads = after(grad_heads, in_came)

    outs = attention_backward(
        span_blocks,
        core,
        table,
        query,
        attended,
        lse,
        from_sources(grad_heads),
        kvs,
    )
    grad_query, grad_kvs, grad_table = outs[0], outs[1:-1], outs[-1]
    grad_kv = add_up(give_back(grad_kvs, "gb")).astype(bf16)
    grad_projected = jnp.concatenate([grad_query, grad_kv], axis=0)
    weight_all = jnp.concatenate([weight_query, weight_kv], axis=0)
    part_normed = contract_rows(grad_projected, weight_all).astype(bf16)
    part_normed = part_normed.reshape(ga, ctx, tok_count, D)

    def over_context(parts):
        sums = {}
        for k in range(ctx):
            part = pick(parts, lax.rem(ctx_index - k + ctx, ctx))
            part = shift(part, "context", -k) if k else part
            from_ctx = lax.rem(ctx_index + k, ctx)
            for i in range(1 if ctx == HEAD_GROUPS else seq_count):
                kept = part.astype(f32)
                if ctx != HEAD_GROUPS:
                    kept = jnp.where(from_ctx // HEAD_GROUPS == i, kept, 0.0)
                sums[i] = sums[i] + kept if i in sums else kept
        return list(sums.values())

    if ga == 1:
        grad_normed = over_context(part_normed[0])
        first_sum = part_normed
    else:
        on_low = ga_index == 0
        total = over_context(jnp.transpose(part_normed, (1, 0, 2, 3)))[0]
        first_sum = jnp.where(on_low, total[1], total[0]).astype(bf16)
        came = shift(first_sum, "ga", 1).astype(f32)
        own_sum = jnp.where(on_low, total[0], total[1])
        grad_normed = [jnp.where(on_low, own_sum, came), jnp.where(on_low, came, own_sum)]

    result = after(add_up(result_parts).astype(bf16), part_normed)
    returned_rows = exchange(result.reshape(experts, capacity, D), expert_axis).reshape(-1, D)
    padding = jnp.zeros((-grad_projected.shape[0] % BLOCK, grad_projected.shape[1]), bf16)
    qkv_part = lax.dot_general(
        after(group_normed, part_normed),
        jnp.concatenate([grad_projected, padding], axis=0),
        (((0,), (1,)), ((), ())),
        preferred_element_type=f32,
    ).astype(bf16)
    out_part_grad = add_up(
        [
            matmul(attended_low[i], grad_branch[i * tok_count : (i + 1) * tok_count])
            for i in range(seq_count)
        ]
    )
    router_grad = lax.dot_general(
        normalized_second,
        grad_logits,
        (((0,), (0,)), ((), ())),
        precision=precise_mode,
        preferred_element_type=f32,
    )
    gain_two_grad = jnp.sum(grad_normed_two * unit_two, axis=0)
    dense = jnp.concatenate(
        [out_part_grad, router_grad, gain_two_grad[:, None], jnp.zeros((D, 123), f32)], axis=1
    ).astype(bf16)
    bias_part = lax.dot_general(
        after(grad_table, part_normed)[:, 0],
        onehot,
        (((1,), (1,)), ((), ())),
        precision=precise_mode,
        preferred_element_type=f32,
    )
    width_qkv = qkv_part.shape[1]
    bias_grad = lax.dynamic_update_slice_in_dim(
        jnp.zeros((HEADS, bias_part.shape[1]), f32), bias_part, head_group * GROUP_HEADS, 0
    )

    own_rows = D // (ga * gb * ctx * dp)
    bias_rows = jnp.pad(bias_grad, ((0, 16 - HEADS), (0, width_qkv - bias_grad.shape[1])))

    def first_exchange(value, *riders):
        value = value.astype(bf16).reshape(experts, -1, value.shape[1])
        for rider in riders:
            rider = jnp.broadcast_to(rider.astype(bf16), (experts,) + rider.shape)
            value = jnp.concatenate([value, rider], axis=1)
        return add_up(list(exchange(value, expert_axis)))

    def second_exchange(value, *riders):
        value = value.astype(bf16).reshape(ctx * dp, own_rows, value.shape[1])
        for rider in riders:
            rider = jnp.broadcast_to(rider.astype(bf16), (ctx * dp,) + rider.shape)
            value = jnp.concatenate([value, rider], axis=1)
        return exchange(value, ("context", "dp"))

    dense = first_exchange(dense)
    summed = first_exchange(after(qkv_part, dense, returned_rows), bias_rows)
    bias_rows = jnp.pad(summed[-16:], ((0, 0), (0, dense.shape[1])))
    summed = after(
        jnp.concatenate([summed[:-16], dense], axis=1), first_sum, down_came
    )
    summed = second_exchange(summed, bias_rows).astype(f32)
    bias_grad = add_up(list(summed[:, own_rows:]))[:HEADS, : bias_grad.shape[1]].T
    dense = add_up(list(summed[:, :own_rows, width_qkv:]))
    summed = summed[:, :own_rows, :width_qkv].reshape(ctx, dp, own_rows, width_qkv)
    by_group = []
    for group in range(HEAD_GROUPS):
        by_group.append(add_up([summed[z, d] for z in range(group, ctx, HEAD_GROUPS) for d in range(dp)]))
    by_group = jnp.stack(by_group, axis=1)
    width = GROUP_HEADS * HEAD_DIM
    query_cols = by_group[:, :, :width].reshape(own_rows, 1, D)
    kv_cols = by_group[:, :, width : 3 * width].reshape(own_rows, HEADS, 2, HEAD_DIM)
    kv_cols = jnp.transpose(kv_cols, (0, 2, 1, 3)).reshape(own_rows, 2, D)
    qkv_total = jnp.concatenate([query_cols, kv_cols], axis=1).reshape(own_rows, 3 * D)
    first_row = (lax.axis_index(("ga", "gb", "context", "dp"))) * own_rows
    weight_rows = lax.dynamic_slice_in_dim(query_key_value_weight, first_row, own_rows, 0)
    gain_rows = lax.dynamic_slice_in_dim(gain_one, first_row, own_rows, 0)
    gain_one_total = jnp.sum(qkv_total * weight_rows.astype(f32), axis=1) / gain_rows

    returned = contract_rows(assign, returned_rows)
    output = (middle + gate * returned).astype(bf16)

    grad_normed = after(jnp.concatenate(grad_normed, axis=0), qkv_total, dense, bias_grad)
    scale_one = normalised(inputs)[0]
    scaled_one = gain_one * grad_normed
    cube_one = scale_one * scale_one * scale_one
    grad_inputs = (
        grad_middle
        + scale_one * scaled_one
        - inputs * cube_one * jnp.mean(scaled_one * inputs, axis=-1, keepdims=True)
    )

    return (
        output.reshape(seq_count, tok_count, D),
        grad_inputs.astype(bf16).reshape(seq_count, tok_count, D),
        qkv_total,
        dense[:, :D],
        gain_one_total,
        dense[:, D + 4],
        dense[:, D : D + 4],
        (in_grad + in_came.astype(f32))[None],
        (down_grad + down_came.astype(f32))[None],
        bias_grad,
    )


def solution(mesh):
    ctx = mesh.shape["context"]
    ga = max(GROUPS // ctx, 1)
    gb = mesh.shape["expert"] // ga
    fine = Mesh(
        mesh.devices.reshape(ga, gb, ctx, mesh.shape["dp"]), ("ga", "gb", "context", "dp")
    )
    expert = ("ga", "gb")
    blocks = ("ga", "gb", "context")
    everywhere = ("ga", "gb", "context", "dp")
    return jax.shard_map(
        local,
        mesh=fine,
        in_specs=(
            P("dp", blocks, None),
            P("dp", blocks, None),
            P(),
            P(),
            P(),
            P(),
            P(),
            P(expert, None, "context"),
            P(expert, None, "context"),
            P(),
            P(),
            P("dp", blocks),
            P("dp", blocks),
            P("dp", blocks),
        ),
        out_specs=(
            P("dp", blocks, None),
            P("dp", blocks, None),
            P(everywhere, None),
            P(everywhere, None),
            P(everywhere),
            P(everywhere),
            P(everywhere, None),
            P(expert, None, ("context", "dp")),
            P(expert, None, ("context", "dp")),
            P(),
        ),
        check_vma=False,
    )
```

```python
import functools

import jax
import jax.numpy as jnp
from jax import lax
from jax.experimental import pallas as pl
from jax.experimental.pallas import tpu as pltpu
from jax.sharding import Mesh, PartitionSpec as P

D = 768
HEADS = 12
HEAD_DIM = 64
GROUP_HEADS = 3
HEAD_GROUPS = HEADS // GROUP_HEADS
SEQ_DEV = 2
GROUPS = SEQ_DEV * HEAD_GROUPS
WIDTH = 256
BLOCK = 128

norm_epsilon = 1e-06
score_scale = 0.125
precise_mode = lax.Precision.HIGHEST
vmem_bytes = 50 * 1024 * 1024
f32 = jnp.float32
bf16 = jnp.bfloat16


def matmul(left, right):
    return jnp.dot(left, right, preferred_element_type=f32)


def contract_rows(left, right):
    return lax.dot_general(left, right, (((0,), (0,)), ((), ())), preferred_element_type=f32)


def contract_cols(left, right):
    return lax.dot_general(left, right, (((1,), (1,)), ((), ())), preferred_element_type=f32)


def skewed_table(table_row):
    wide = jnp.broadcast_to(table_row, (BLOCK, table_row.shape[1]))
    return pltpu.roll(wide, 1, 1, stride=1, stride_axis=0)


def key_rows(kv_refs, rows):
    for part, kv_ref in enumerate(kv_refs):
        count = kv_ref.shape[1]
        rows[part * count : (part + 1) * count, :] = kv_ref[...].T


def begins(block, core, cores, span_blocks):
    return ((block // span_blocks * cores + core) * span_blocks + block % span_blocks) * BLOCK


def key_begins(offset, core, parts, own_count, span_blocks):
    part, inside = divmod(offset, own_count)
    owner = lax.rem(core - part + parts, parts)
    return begins(inside // BLOCK, owner, parts, span_blocks)


def forward_kernel(parts, span_blocks, core_ref, table_ref, q_ref, *refs):
    kv_refs = refs[:parts]
    out_ref, full_ref, lse_ref, skew, score, weight, rows = refs[parts:]
    half = table_ref.shape[2] // 2
    own_count = kv_refs[0].shape[1]
    key_count = parts * own_count
    skew[...] = skewed_table(table_ref[0])
    key_rows(kv_refs, rows)
    blocks = WIDTH // BLOCK
    core = core_ref[0]

    def one_tile(tile, carry):
        lanes = pl.ds(pl.multiple_of(tile * WIDTH, WIDTH), WIDTH)
        query = q_ref[:, lanes] * jnp.asarray(score_scale, bf16)
        query = jnp.concatenate([query, jnp.zeros_like(query)], axis=0)
        start = half + begins(tile * blocks, core, parts, span_blocks)
        top = jnp.full((8, WIDTH), -jnp.inf, f32)
        for block in range(key_count // BLOCK):
            offset = block * BLOCK
            behind = start - key_begins(offset, core, parts, own_count, span_blocks)
            bias = skew[:, pl.ds(pl.multiple_of(behind, BLOCK), WIDTH)]
            part = matmul(rows[offset : offset + BLOCK, :], query) + bias
            score[offset : offset + BLOCK, :] = part
            top = jnp.maximum(top, jnp.max(part.reshape(BLOCK // 8, 8, WIDTH), axis=0))
        top = jnp.max(top, axis=0, keepdims=True)
        total = jnp.zeros((8, WIDTH), f32)
        for block in range(key_count // BLOCK):
            offset = block * BLOCK
            part = jnp.exp(score[offset : offset + BLOCK, :] - top)
            total = total + jnp.sum(part.reshape(BLOCK // 8, 8, WIDTH), axis=0)
            weight[offset : offset + BLOCK, :] = part.astype(bf16)
        total = jnp.sum(total, axis=0, keepdims=True)
        blended = jnp.zeros((HEAD_DIM, WIDTH), f32)
        for part, kv_ref in enumerate(kv_refs):
            own = weight[part * own_count : (part + 1) * own_count, :]
            blended = blended + matmul(kv_ref[HEAD_DIM:, :], own)
        blended = blended / total
        full_ref[:, lanes] = blended
        for i in range(blocks):
            piece = blended[:, i * BLOCK : (i + 1) * BLOCK]
            out_ref[tile * blocks + i] = piece.astype(bf16)
        lse_ref[0, :, lanes] = top + jnp.log(total)
        return carry

    lax.fori_loop(0, q_ref.shape[1] // WIDTH, one_tile, 0)


def backward_kernel(
    parts, span_blocks, core_ref, table_ref, q_ref, full_ref, lse_ref, grad_ref, *refs
):
    kv_refs = refs[:parts]
    dq_ref = refs[parts]
    dkv_refs = refs[parts + 1 : 2 * parts + 1]
    dtable_ref, skew, dskew, rows, dkv = refs[2 * parts + 1 :]
    span = table_ref.shape[2]
    half = span // 2
    own_count = kv_refs[0].shape[1]
    key_count = parts * own_count
    skew[...] = skewed_table(table_ref[0])
    key_rows(kv_refs, rows)
    dskew[...] = jnp.zeros_like(dskew)
    dkv[...] = jnp.zeros_like(dkv)
    blocks = WIDTH // BLOCK
    step = 2 * BLOCK
    core = core_ref[0]

    def one_tile(tile, carry):
        lanes = pl.ds(pl.multiple_of(tile * WIDTH, WIDTH), WIDTH)
        query = q_ref[:, lanes] * jnp.asarray(score_scale, bf16)
        grad = jnp.concatenate(
            [grad_ref[tile * blocks + i] for i in range(blocks)], axis=1
        )
        lse = lse_ref[0, :, lanes]
        delta = jnp.sum(grad.astype(f32) * full_ref[:, lanes], axis=0, keepdims=True)
        query = jnp.concatenate([query, jnp.zeros_like(query)], axis=0)
        grad = jnp.concatenate([jnp.zeros_like(grad), grad], axis=0)
        query_rows = query.T
        grad_rows = grad.T
        start = half + begins(tile * blocks, core, parts, span_blocks)
        dq = jnp.zeros((HEAD_DIM, WIDTH), f32)
        for offset in range(0, key_count, step):
            keys = rows[offset : offset + step, :]
            raw = matmul(keys, query)
            dprob = matmul(keys, grad)
            probs = []
            dscores = []
            for inner in range(0, step, BLOCK):
                behind = start - key_begins(offset + inner, core, parts, own_count, span_blocks)
                here = pl.ds(pl.multiple_of(behind, BLOCK), WIDTH)
                own = slice(inner, inner + BLOCK)
                prob = jnp.exp(raw[own] + skew[:, here] - lse)
                dscore = prob * (dprob[own] - delta)
                dskew[:, here] += dscore
                probs.append(prob.astype(bf16))
                dscores.append(dscore.astype(bf16))
            prob = jnp.concatenate(probs, axis=0)
            dscore = jnp.concatenate(dscores, axis=0)
            dkv[offset : offset + step, :] += matmul(dscore, query_rows) + matmul(prob, grad_rows)
            part, inside = divmod(offset, own_count)
            dq = dq + matmul(kv_refs[part][:HEAD_DIM, inside : inside + step], dscore)
        dq_ref[:, lanes] = (dq * score_scale).astype(bf16)
        return carry

    lax.fori_loop(0, q_ref.shape[1] // WIDTH, one_tile, 0)
    for part, dkv_ref in enumerate(dkv_refs):
        dkv_ref[...] = dkv[part * own_count : (part + 1) * own_count, :].T.astype(bf16)
    folded = dskew[...]
    count = BLOCK
    while count > 1:
        count //= 2
        folded = folded[:count] + pltpu.roll(folded[count:], span - count, 1)
    dtable_ref[0] = pltpu.roll(folded, span - 1, 1)


def stack_spec(*shape):
    return pl.BlockSpec((1,) + shape, lambda head: (head, 0, 0))


def rows_spec(*shape):
    return pl.BlockSpec(shape, lambda head: (head, 0))


def place_spec(blocks):
    return pl.BlockSpec((blocks, HEAD_DIM, BLOCK), lambda head: (0, head, 0))


def attention_forward(span_blocks, core, table, query, kvs):
    count, span, parts = query.shape[1], table.shape[2], len(kvs)
    keys = parts * count
    scalars = pl.BlockSpec(memory_space=pltpu.SMEM)
    return pl.pallas_call(
        functools.partial(forward_kernel, parts, span_blocks),
        grid=(GROUP_HEADS,),
        in_specs=[scalars, stack_spec(1, span), rows_spec(HEAD_DIM, count)]
        + [rows_spec(2 * HEAD_DIM, count)] * parts,
        out_specs=[
            place_spec(count // BLOCK),
            rows_spec(HEAD_DIM, count),
            stack_spec(1, count),
        ],
        out_shape=[
            jax.ShapeDtypeStruct((count // BLOCK, GROUP_HEADS * HEAD_DIM, BLOCK), bf16),
            jax.ShapeDtypeStruct((GROUP_HEADS * HEAD_DIM, count), f32),
            jax.ShapeDtypeStruct((GROUP_HEADS, 1, count), f32),
        ],
        scratch_shapes=[
            pltpu.VMEM((BLOCK, span), f32),
            pltpu.VMEM((keys, WIDTH), f32),
            pltpu.VMEM((keys, WIDTH), bf16),
            pltpu.VMEM((keys, 2 * HEAD_DIM), bf16),
        ],
        compiler_params=pltpu.CompilerParams(vmem_limit_bytes=vmem_bytes),
        cost_estimate=pl.CostEstimate(
            flops=4 * GROUP_HEADS * HEAD_DIM * count * keys * 4,
            bytes_accessed=4 * GROUP_HEADS * HEAD_DIM * (count + keys) * 2,
            transcendentals=GROUP_HEADS * count * keys,
        ),
        name="attention_forward",
    )(core, table, query, *kvs)


def attention_backward(span_blocks, core, table, query, full, lse, grad, kvs):
    count, span, parts = query.shape[1], table.shape[2], len(kvs)
    keys = parts * count
    scalars = pl.BlockSpec(memory_space=pltpu.SMEM)
    return pl.pallas_call(
        functools.partial(backward_kernel, parts, span_blocks),
        grid=(GROUP_HEADS,),
        in_specs=[
            scalars,
            stack_spec(1, span),
            rows_spec(HEAD_DIM, count),
            rows_spec(HEAD_DIM, count),
            stack_spec(1, count),
            place_spec(count // BLOCK),
        ]
        + [rows_spec(2 * HEAD_DIM, count)] * parts,
        out_specs=[rows_spec(HEAD_DIM, count)]
        + [rows_spec(2 * HEAD_DIM, count)] * parts
        + [stack_spec(1, span)],
        out_shape=[jax.ShapeDtypeStruct((GROUP_HEADS * HEAD_DIM, count), bf16)]
        + [jax.ShapeDtypeStruct((GROUP_HEADS * 2 * HEAD_DIM, count), bf16)] * parts
        + [jax.ShapeDtypeStruct((GROUP_HEADS, 1, span), f32)],
        scratch_shapes=[
            pltpu.VMEM((BLOCK, span), f32),
            pltpu.VMEM((BLOCK, span), f32),
            pltpu.VMEM((keys, 2 * HEAD_DIM), bf16),
            pltpu.VMEM((keys, 2 * HEAD_DIM), f32),
        ],
        compiler_params=pltpu.CompilerParams(vmem_limit_bytes=vmem_bytes),
        cost_estimate=pl.CostEstimate(
            flops=10 * GROUP_HEADS * HEAD_DIM * count * keys * 4,
            bytes_accessed=4 * GROUP_HEADS * HEAD_DIM * (count + keys) * 4,
            transcendentals=GROUP_HEADS * count * keys,
        ),
        name="attention_backward",
    )(core, table, query, full, lse, grad, *kvs)


def shift(value, axis, step):
    size = lax.axis_size(axis)
    return lax.ppermute(value, axis, [(i, (i + step) % size) for i in range(size)])


def pick(value, index, dim=0):
    return lax.dynamic_index_in_dim(value, index, dim, keepdims=False)


def spread(parts, axis):
    return [parts[0]] + [shift(parts[k], axis, k) for k in range(1, len(parts))]


def give_back(parts, axis):
    return [parts[0]] + [shift(parts[k], axis, -k) for k in range(1, len(parts))]


def scatter_sum(value, axis, dim, wire=bf16):
    size = lax.axis_size(axis)
    index = lax.axis_index(axis)
    if size == 2:
        low = lax.index_in_dim(value, 0, dim, keepdims=False)
        high = lax.index_in_dim(value, 1, dim, keepdims=False)
        first = index == 0
        got = shift(jnp.where(first, high, low).astype(wire), axis, 1)
        return jnp.where(first, low, high).astype(f32) + got.astype(f32)
    total = pick(value, index, dim).astype(f32)
    for k in range(1, size):
        part = pick(value, lax.rem(index + k, size), dim).astype(wire)
        total = total + shift(part, axis, k).astype(f32)
    return total


def sum_everywhere(value, axes):
    for axis in axes:
        size = lax.axis_size(axis)
        step = 1
        while step < size:
            value = value + lax.ppermute(value, axis, [(i, i ^ step) for i in range(size)])
            step *= 2
    return value


def scatter_rows(value, *others):
    ga, gb, ctx, dp = (lax.axis_size(a) for a in ("ga", "gb", "context", "dp"))
    rows, cols = value.shape
    own = rows // (ga * gb * ctx * dp)
    value = value.reshape(ga, gb, ctx * dp * own, cols)
    value = after(scatter_sum(value, "gb", 1), *others)
    value = scatter_sum(value, "ga", 0)
    value = value.reshape(ctx, dp, own, cols)
    return scatter_sum(value, "dp", 1)


def split_halves(value):
    high = value.astype(bf16)
    return high, (value - high.astype(f32)).astype(bf16)


def gelu_parts(values):
    c = 0.7978845608028654
    square = values * values
    bent = jnp.tanh(c * values * (1.0 + 0.044715 * square))
    act = 0.5 * values * (1.0 + bent)
    slope = 0.5 * (1.0 + bent) + 0.5 * values * (1.0 - bent * bent) * c * (
        1.0 + 3 * 0.044715 * square
    )
    return act, slope


def after(value, *others):
    width = value.shape[-1]
    for other in others:
        first = other.reshape(-1, other.shape[-1])[:1]
        if first.shape[1] < width:
            first = jnp.concatenate([first] * -(-width // first.shape[1]), axis=1)
        first = first[:, :width]
        value = jnp.where(first == first, value, jnp.zeros_like(value))
    return value


def add_up(parts):
    total = parts[0].astype(f32)
    for part in parts[1:]:
        total = total + part.astype(f32)
    return total


def exchange(value, axis):
    return lax.all_to_all(value, axis, 0, 0, tiled=True)


def local(
    tokens,
    cotangent,
    query_key_value_weight,
    output_weight,
    gain_one,
    gain_two,
    router_weight,
    w_in,
    w_down,
    position_bias,
    bucket,
    route,
    slot,
    dropped,
):
    seq_count, tok_count = tokens.shape[:2]
    row_count = seq_count * tok_count
    ga, gb, ctx, dp = (lax.axis_size(a) for a in ("ga", "gb", "context", "dp"))
    experts = ga * gb
    capacity = (5 * row_count + 4 * experts - 1) // (4 * experts)
    group_rows = GROUPS * tok_count
    expert_axis = ("ga", "gb")
    group_axis = ("ga", "context")
    ga_index, gb_index, ctx_index = (lax.axis_index(a) for a in ("ga", "gb", "context"))
    group_index = lax.axis_index(group_axis)
    head_group = lax.rem(group_index, HEAD_GROUPS)
    in_order = tok_count % BLOCK != 0

    outgoing = jnp.broadcast_to(tokens[:, None], (SEQ_DEV, HEAD_GROUPS, tok_count, D))
    group_tokens = exchange(outgoing.reshape(GROUPS, tok_count, D), group_axis)
    group_tokens = group_tokens.reshape(group_rows, D)
    span_blocks = ctx * tok_count // BLOCK
    core = gb_index.astype(jnp.int32)[None]

    weight_group = query_key_value_weight.T.reshape(3, HEAD_GROUPS, GROUP_HEADS, HEAD_DIM, D)
    weight_group = pick(weight_group, head_group, 1)
    weight_query = weight_group[0].reshape(GROUP_HEADS * HEAD_DIM, D)
    weight_kv = jnp.transpose(weight_group[1:], (1, 0, 2, 3)).reshape(-1, D)

    def pair(value):
        return lax.ppermute(value, "context", [(i, i ^ 1) for i in range(ctx)])

    def every_other(value):
        return [value] + [shift(value, "context", 2 * k) for k in range(1, ctx // 2)]

    def every_other_back(parts):
        return [parts[0]] + [shift(parts[k], "context", -2 * k) for k in range(1, len(parts))]


    dp_index = lax.axis_index("dp")

    def by_owner(weight):
        cut = weight.shape[1] // dp
        if dp == 2:
            low, high = weight[:, :cut], weight[:, cut:]
            first = dp_index == 0
            parts = [jnp.where(first, low, high), jnp.where(first, high, low)]
            return jnp.concatenate(parts, axis=1)
        return jnp.roll(weight.reshape(D, dp, cut), -dp_index, axis=1).reshape(D, -1)

    own_in, own_down = by_owner(w_in[0]), by_owner(w_down[0])

    route_flat = route.reshape(-1)
    position = route_flat * capacity + slot.reshape(-1)
    assign = (
        (jnp.arange(experts * capacity, dtype=jnp.int32)[:, None] == position[None, :])
        & (dropped.reshape(-1) == 0)[None, :]
    ).astype(bf16)
    grad_low = cotangent.reshape(row_count, D)
    grad_buffer = matmul(assign, grad_low).astype(bf16).reshape(experts, capacity, D)
    expert_index = lax.axis_index(expert_axis)
    grad_rows = jnp.zeros((experts, capacity, D), bf16)
    for k in range(experts):
        part = pick(grad_buffer, lax.rem(expert_index + k, experts))
        part = shift(part, expert_axis, k) if k else part
        came_from = lax.rem(expert_index - k + experts, experts)
        grad_rows = lax.dynamic_update_index_in_dim(grad_rows, part, came_from, 0)
    grad_rows = grad_rows.reshape(-1, D)

    onehot = (
        jnp.arange(position_bias.shape[0], dtype=jnp.int32)[:, None]
        == jnp.pad(bucket[::-1], (0, 1), constant_values=-1)[None, :]
    ).astype(f32)
    bias_heads = lax.dynamic_slice_in_dim(position_bias.T, head_group * GROUP_HEADS, GROUP_HEADS, 0)
    table = jnp.dot(bias_heads, onehot, precision=precise_mode, preferred_element_type=f32)
    table = table[:, None, :]

    def normalised(values):
        scale = lax.rsqrt(jnp.mean(values * values, axis=-1, keepdims=True) + norm_epsilon)
        return scale, values * scale

    group_normed = (normalised(group_tokens.astype(f32))[1] * gain_one).astype(bf16)
    own_kv = contract_cols(weight_kv, group_normed).astype(bf16)
    kvs = [own_kv] + [shift(own_kv, "gb", k) for k in range(1, gb)]
    query = contract_cols(weight_query, group_normed).astype(bf16)
    query = after(query, grad_rows)

    grad_blocks = every_other(after(grad_rows, group_normed))
    both_in = [own_in, pair(after(own_in, group_normed))]

    attended_parts, attended, lse = attention_forward(
        span_blocks, core, table, query, kvs
    )

    def to_sources(parts):
        parts = parts.reshape(group_rows // BLOCK, -1, BLOCK)
        if in_order:
            parts = jnp.transpose(
                parts.reshape(group_rows // BLOCK, parts.shape[1], BLOCK // tok_count, tok_count),
                (0, 2, 1, 3),
            ).reshape(GROUPS, parts.shape[1], tok_count)
        return parts

    def from_sources(parts):
        if in_order:
            merged = BLOCK // tok_count
            parts = jnp.transpose(
                parts.reshape(GROUPS // merged, merged, parts.shape[1], tok_count), (0, 2, 1, 3)
            ).reshape(GROUPS // merged, parts.shape[1], BLOCK)
        return parts

    attended_low = exchange(to_sources(attended_parts), group_axis)
    attended_low = attended_low.reshape(seq_count, D, tok_count)
    both_down = [own_down, pair(after(own_down, attended_low))]

    inputs = tokens.reshape(row_count, D).astype(f32)
    branch = jnp.concatenate(
        [contract_rows(attended_low[i], output_weight) for i in range(seq_count)], axis=0
    )
    middle = inputs + branch
    scale_two, unit_two = normalised(middle)
    normalized_second = unit_two * gain_two
    router_logits = jnp.dot(
        normalized_second, router_weight, precision=precise_mode, preferred_element_type=f32
    )
    router = jax.nn.softmax(router_logits, axis=-1)
    chosen = (route_flat[:, None] == jnp.arange(experts, dtype=jnp.int32)[None, :]).astype(f32)
    gate = jnp.sum(router * chosen, axis=-1, keepdims=True)

    gate_high, gate_low = split_halves(gate)
    payload = jnp.concatenate(
        [
            after(
                normalized_second.astype(bf16), *grad_blocks[1:], both_in[1]
            ),
            gate_high,
            gate_low,
            jnp.zeros((row_count, 126), bf16),
        ],
        axis=1,
    )
    buffer = matmul(assign, payload).astype(bf16).reshape(experts, capacity, D + 128)
    received = exchange(buffer, expert_axis).reshape(-1, D + 128)
    row_total = received.shape[0]
    gate_rows = contract_cols(jnp.eye(16, 128, dtype=bf16), received[:, D:]).astype(bf16)
    gate_rows = jnp.pad(gate_rows, ((0, 0), (0, -row_total % D)))[:, :D]
    sent_blocks = every_other(jnp.concatenate([received[:, :D], gate_rows], axis=0))
    row_blocks = [block[:row_total] for block in sent_blocks]
    gate_blocks = [block[row_total:, :row_total] for block in sent_blocks]
    gate_width = jnp.where(jnp.arange(16)[:, None] < 2, 1.0, 0.0) * jnp.ones((1, D), f32)
    gate_width = gate_width.astype(bf16)

    ones = jnp.ones((8, own_in.shape[1]), bf16)
    hidden_blocks, pre_blocks, back_parts = [], [], []
    for rows_now, grads_now in zip(row_blocks, grad_blocks):
        hidden_blocks.append([])
        pre_blocks.append([])
        back = gate_part = 0.0
        for weight_in, weight_down in zip(both_in, both_down):
            grad_hidden = matmul(after(grads_now, sent_blocks[0]), weight_down)
            act, slope = gelu_parts(matmul(rows_now, weight_in))
            hidden = act.astype(bf16)
            grad_pre = (grad_hidden * slope).astype(bf16)
            hidden_blocks[-1].append(hidden)
            pre_blocks[-1].append(grad_pre)
            back = back + contract_cols(grad_pre, weight_in)
            product = (grad_hidden * hidden.astype(f32)).astype(bf16)
            gate_part = gate_part + contract_cols(ones, product)[:1]
        gate_part = jnp.concatenate(
            split_halves(gate_part) + (jnp.zeros((14, row_total), bf16),), axis=0
        )
        gate_part = jnp.pad(gate_part, ((0, 0), (0, -row_total % D)))[:, :D]
        back = jnp.concatenate([back.astype(bf16), gate_part], axis=0)
        back_parts.append(after(back, *sent_blocks[1:]))

    back_total = add_up(every_other_back(back_parts))
    back_sum = back_total[:row_total].astype(bf16)
    gate_sum = back_total[row_total : row_total + 2, :row_total]
    gate_sum = gate_sum[:1] + gate_sum[1:]
    gate_halves = split_halves(gate_sum[:1])
    gate_column = contract_rows(
        jnp.concatenate(gate_halves + (jnp.zeros((6, gate_sum.shape[1]), bf16),), axis=0),
        jnp.eye(8, 128, dtype=bf16),
    ).astype(bf16)
    back_rows = jnp.concatenate([back_sum, gate_column], axis=1)
    back_rows = exchange(back_rows.reshape(experts, capacity, D + 128), expert_axis)
    back_rows = contract_rows(assign, back_rows.reshape(-1, D + 128))
    grad_sent = back_rows[:, :D] * gate
    grad_gate = back_rows[:, D : D + 1] + back_rows[:, D + 1 : D + 2]

    grad_out = grad_low.astype(f32)
    grad_logits = grad_gate * gate * (chosen - router)
    grad_normed_two = grad_sent + lax.dot_general(
        grad_logits,
        router_weight,
        (((1,), (1,)), ((), ())),
        precision=precise_mode,
        preferred_element_type=f32,
    )
    scaled_two = gain_two * grad_normed_two
    cube_two = scale_two * scale_two * scale_two
    grad_middle = (
        grad_out
        + scale_two * scaled_two
        - middle * cube_two * jnp.mean(scaled_two * middle, axis=-1, keepdims=True)
    )
    grad_branch = grad_middle.astype(bf16)

    grad_heads = jnp.concatenate(
        [
            contract_cols(output_weight, grad_branch[i * tok_count : (i + 1) * tok_count])
            for i in range(seq_count)
        ],
        axis=0,
    ).astype(bf16)
    grad_heads = exchange(
        grad_heads.reshape(GROUPS, GROUP_HEADS * HEAD_DIM, tok_count), group_axis
    )

    out_parts = [
        add_up([contract_cols(h, w) for h, w in zip(hidden, both_down)]).astype(bf16)
        for hidden in hidden_blocks
    ]
    result_parts = every_other_back(
        out_parts[:1] + [after(part, back_sum) for part in out_parts[1:]]
    )

    all_rows = jnp.concatenate(row_blocks, axis=0)
    all_grads = jnp.concatenate(grad_blocks, axis=0)
    all_gates = contract_rows(jnp.concatenate(gate_blocks, axis=1), gate_width)
    all_returned = (all_gates * all_grads.astype(f32)).astype(bf16)
    all_hidden = [jnp.concatenate(blocks, axis=0) for blocks in zip(*hidden_blocks)]
    all_pre = [
        (jnp.concatenate(blocks, axis=0).astype(f32) * all_gates[:, :1]).astype(bf16)
        for blocks in zip(*pre_blocks)
    ]
    cut = own_in.shape[1] // dp

    def reduced(left, rights):
        def columns(k):
            piece = [right[:, k * cut : (k + 1) * cut] for right in rights]
            return contract_rows(left, jnp.concatenate(piece, axis=1)).astype(bf16)

        came = [shift(columns(k), "dp", k) for k in range(1, dp)]
        mine = columns(0)
        own = add_up([mine[:, :cut]] + [part[:, :cut] for part in came])
        partner = add_up([mine[:, cut:]] + [part[:, cut:] for part in came]).astype(bf16)
        return own, partner

    in_grad, in_partner = reduced(all_rows, all_pre)
    down_grad, down_partner = reduced(all_returned, all_hidden)
    in_came = pair(after(in_partner, back_sum))
    result = after(add_up(result_parts).astype(bf16), grad_heads)
    returned_rows = exchange(result.reshape(experts, capacity, D), expert_axis).reshape(-1, D)
    grad_heads = after(grad_heads, in_came, returned_rows)


    outs = attention_backward(
        span_blocks,
        core,
        table,
        query,
        attended,
        lse,
        from_sources(grad_heads),
        kvs,
    )
    grad_query, grad_kvs, grad_table = outs[0], outs[1:-1], outs[-1]
    grad_kv = add_up(give_back(grad_kvs, "gb")).astype(bf16)
    grad_projected = jnp.concatenate([grad_query, grad_kv], axis=0)
    weight_all = jnp.concatenate([weight_query, weight_kv], axis=0)
    part_normed = contract_rows(grad_projected, weight_all).astype(bf16)
    down_came = pair(after(down_partner, part_normed))
    part_normed = part_normed.reshape(ga, ctx, tok_count, D)

    def over_context(parts):
        sums = {}
        for k in range(ctx):
            part = pick(parts, lax.rem(ctx_index - k + ctx, ctx))
            part = shift(part, "context", -k) if k else part
            from_ctx = lax.rem(ctx_index + k, ctx)
            for i in range(1 if ctx == HEAD_GROUPS else seq_count):
                kept = part.astype(f32)
                if ctx != HEAD_GROUPS:
                    kept = jnp.where(from_ctx // HEAD_GROUPS == i, kept, 0.0)
                sums[i] = sums[i] + kept if i in sums else kept
        return list(sums.values())

    if ga == 1:
        grad_normed = over_context(part_normed[0])
        first_sum = part_normed
    else:
        on_low = ga_index == 0
        total = over_context(jnp.transpose(part_normed, (1, 0, 2, 3)))[0]
        first_sum = jnp.where(on_low, total[1], total[0]).astype(bf16)
        came = shift(first_sum, "ga", 1).astype(f32)
        own_sum = jnp.where(on_low, total[0], total[1])
        grad_normed = [jnp.where(on_low, own_sum, came), jnp.where(on_low, came, own_sum)]

    padding = jnp.zeros((-grad_projected.shape[0] % BLOCK, grad_projected.shape[1]), bf16)
    qkv_part = lax.dot_general(
        after(group_normed, part_normed),
        jnp.concatenate([grad_projected, padding], axis=0),
        (((0,), (1,)), ((), ())),
        preferred_element_type=f32,
    ).astype(bf16)
    out_part_grad = add_up(
        [
            matmul(attended_low[i], grad_branch[i * tok_count : (i + 1) * tok_count])
            for i in range(seq_count)
        ]
    )
    router_grad = lax.dot_general(
        normalized_second,
        grad_logits,
        (((0,), (0,)), ((), ())),
        precision=precise_mode,
        preferred_element_type=f32,
    )
    gain_two_grad = jnp.sum(grad_normed_two * unit_two, axis=0)
    dense = jnp.concatenate(
        [out_part_grad, router_grad, gain_two_grad[:, None], jnp.zeros((D, 123), f32)], axis=1
    ).astype(bf16)
    bias_part = lax.dot_general(
        after(grad_table, part_normed)[:, 0],
        onehot,
        (((1,), (1,)), ((), ())),
        precision=precise_mode,
        preferred_element_type=f32,
    )
    width_qkv = qkv_part.shape[1]
    bias_grad = lax.dynamic_update_slice_in_dim(
        jnp.zeros((HEADS, bias_part.shape[1]), f32), bias_part, head_group * GROUP_HEADS, 0
    )

    own_rows = D // (ga * gb * ctx * dp)
    bias_rows = jnp.pad(bias_grad, ((0, 16 - HEADS), (0, width_qkv - bias_grad.shape[1])))

    def first_exchange(value, *riders):
        value = value.astype(bf16).reshape(experts, -1, value.shape[1])
        for rider in riders:
            rider = jnp.broadcast_to(rider.astype(bf16), (experts,) + rider.shape)
            value = jnp.concatenate([value, rider], axis=1)
        return add_up(list(exchange(value, expert_axis)))

    def second_exchange(value, *riders):
        value = value.astype(bf16).reshape(ctx * dp, own_rows, value.shape[1])
        for rider in riders:
            rider = jnp.broadcast_to(rider.astype(bf16), (ctx * dp,) + rider.shape)
            value = jnp.concatenate([value, rider], axis=1)
        return exchange(value, ("context", "dp"))

    dense = first_exchange(dense)
    summed = first_exchange(after(qkv_part, dense, returned_rows), bias_rows)
    bias_rows = jnp.pad(summed[-16:], ((0, 0), (0, dense.shape[1])))
    summed = after(
        jnp.concatenate([summed[:-16], dense], axis=1), first_sum, down_came
    )
    summed = second_exchange(summed, bias_rows).astype(f32)
    bias_grad = add_up(list(summed[:, own_rows:]))[:HEADS, : bias_grad.shape[1]].T
    dense = add_up(list(summed[:, :own_rows, width_qkv:]))
    summed = summed[:, :own_rows, :width_qkv].reshape(ctx, dp, own_rows, width_qkv)
    by_group = []
    for group in range(HEAD_GROUPS):
        by_group.append(add_up([summed[z, d] for z in range(group, ctx, HEAD_GROUPS) for d in range(dp)]))
    by_group = jnp.stack(by_group, axis=1)
    width = GROUP_HEADS * HEAD_DIM
    query_cols = by_group[:, :, :width].reshape(own_rows, 1, D)
    kv_cols = by_group[:, :, width : 3 * width].reshape(own_rows, HEADS, 2, HEAD_DIM)
    kv_cols = jnp.transpose(kv_cols, (0, 2, 1, 3)).reshape(own_rows, 2, D)
    qkv_total = jnp.concatenate([query_cols, kv_cols], axis=1).reshape(own_rows, 3 * D)
    first_row = (lax.axis_index(("ga", "gb", "context", "dp"))) * own_rows
    weight_rows = lax.dynamic_slice_in_dim(query_key_value_weight, first_row, own_rows, 0)
    gain_rows = lax.dynamic_slice_in_dim(gain_one, first_row, own_rows, 0)
    gain_one_total = jnp.sum(qkv_total * weight_rows.astype(f32), axis=1) / gain_rows

    returned = contract_rows(assign, returned_rows)
    output = (middle + gate * returned).astype(bf16)

    grad_normed = after(jnp.concatenate(grad_normed, axis=0), qkv_total, dense, bias_grad)
    scale_one = normalised(inputs)[0]
    scaled_one = gain_one * grad_normed
    cube_one = scale_one * scale_one * scale_one
    grad_inputs = (
        grad_middle
        + scale_one * scaled_one
        - inputs * cube_one * jnp.mean(scaled_one * inputs, axis=-1, keepdims=True)
    )

    return (
        output.reshape(seq_count, tok_count, D),
        grad_inputs.astype(bf16).reshape(seq_count, tok_count, D),
        qkv_total,
        dense[:, :D],
        gain_one_total,
        dense[:, D + 4],
        dense[:, D : D + 4],
        (in_grad + in_came.astype(f32))[None],
        (down_grad + down_came.astype(f32))[None],
        bias_grad,
    )


def solution(mesh):
    ctx = mesh.shape["context"]
    ga = max(GROUPS // ctx, 1)
    gb = mesh.shape["expert"] // ga
    fine = Mesh(
        mesh.devices.reshape(ga, gb, ctx, mesh.shape["dp"]), ("ga", "gb", "context", "dp")
    )
    expert = ("ga", "gb")
    blocks = ("ga", "gb", "context")
    everywhere = ("ga", "gb", "context", "dp")
    return jax.shard_map(
        local,
        mesh=fine,
        in_specs=(
            P("dp", blocks, None),
            P("dp", blocks, None),
            P(),
            P(),
            P(),
            P(),
            P(),
            P(expert, None, "context"),
            P(expert, None, "context"),
            P(),
            P(),
            P("dp", blocks),
            P("dp", blocks),
            P("dp", blocks),
        ),
        out_specs=(
            P("dp", blocks, None),
            P("dp", blocks, None),
            P(everywhere, None),
            P(everywhere, None),
            P(everywhere),
            P(everywhere),
            P(everywhere, None),
            P(expert, None, ("context", "dp")),
            P(expert, None, ("context", "dp")),
            P(),
        ),
        check_vma=False,
    )
```

```python
import functools

import jax
import jax.numpy as jnp
from jax import lax
from jax.experimental import pallas as pl
from jax.experimental.pallas import tpu as pltpu
from jax.sharding import Mesh, PartitionSpec as P

D = 768
HEADS = 12
HEAD_DIM = 64
GROUP_HEADS = 3
HEAD_GROUPS = HEADS // GROUP_HEADS
SEQ_DEV = 2
GROUPS = SEQ_DEV * HEAD_GROUPS
WIDTH = 256
BLOCK = 128

norm_epsilon = 1e-06
score_scale = 0.125
precise_mode = lax.Precision.HIGHEST
vmem_bytes = 50 * 1024 * 1024
f32 = jnp.float32
bf16 = jnp.bfloat16


def matmul(left, right):
    return jnp.dot(left, right, preferred_element_type=f32)


def contract_rows(left, right):
    return lax.dot_general(left, right, (((0,), (0,)), ((), ())), preferred_element_type=f32)


def contract_cols(left, right):
    return lax.dot_general(left, right, (((1,), (1,)), ((), ())), preferred_element_type=f32)


def skewed_table(table_row):
    wide = jnp.broadcast_to(table_row, (BLOCK, table_row.shape[1]))
    return pltpu.roll(wide, 1, 1, stride=1, stride_axis=0)


def key_rows(kv_refs, rows):
    for part, kv_ref in enumerate(kv_refs):
        count = kv_ref.shape[1]
        rows[part * count : (part + 1) * count, :] = kv_ref[...].T


def begins(block, core, cores, span_blocks):
    return ((block // span_blocks * cores + core) * span_blocks + block % span_blocks) * BLOCK


def key_begins(offset, core, parts, own_count, span_blocks):
    part, inside = divmod(offset, own_count)
    owner = lax.rem(core - part + parts, parts)
    return begins(inside // BLOCK, owner, parts, span_blocks)


def forward_kernel(parts, span_blocks, core_ref, table_ref, q_ref, *refs):
    kv_refs = refs[:parts]
    out_ref, full_ref, lse_ref, skew, score, weight, rows = refs[parts:]
    half = table_ref.shape[2] // 2
    own_count = kv_refs[0].shape[1]
    key_count = parts * own_count
    skew[...] = skewed_table(table_ref[0])
    key_rows(kv_refs, rows)
    blocks = WIDTH // BLOCK
    core = core_ref[0]

    def one_tile(tile, carry):
        lanes = pl.ds(pl.multiple_of(tile * WIDTH, WIDTH), WIDTH)
        query = q_ref[:, lanes] * jnp.asarray(score_scale, bf16)
        query = jnp.concatenate([query, jnp.zeros_like(query)], axis=0)
        start = half + begins(tile * blocks, core, parts, span_blocks)
        top = jnp.full((8, WIDTH), -jnp.inf, f32)
        for block in range(key_count // BLOCK):
            offset = block * BLOCK
            behind = start - key_begins(offset, core, parts, own_count, span_blocks)
            bias = skew[:, pl.ds(pl.multiple_of(behind, BLOCK), WIDTH)]
            part = matmul(rows[offset : offset + BLOCK, :], query) + bias
            score[offset : offset + BLOCK, :] = part
            top = jnp.maximum(top, jnp.max(part.reshape(BLOCK // 8, 8, WIDTH), axis=0))
        top = jnp.max(top, axis=0, keepdims=True)
        total = jnp.zeros((8, WIDTH), f32)
        for block in range(key_count // BLOCK):
            offset = block * BLOCK
            part = jnp.exp(score[offset : offset + BLOCK, :] - top)
            total = total + jnp.sum(part.reshape(BLOCK // 8, 8, WIDTH), axis=0)
            weight[offset : offset + BLOCK, :] = part.astype(bf16)
        total = jnp.sum(total, axis=0, keepdims=True)
        blended = jnp.zeros((HEAD_DIM, WIDTH), f32)
        for part, kv_ref in enumerate(kv_refs):
            own = weight[part * own_count : (part + 1) * own_count, :]
            blended = blended + matmul(kv_ref[HEAD_DIM:, :], own)
        blended = blended / total
        full_ref[:, lanes] = blended
        for i in range(blocks):
            piece = blended[:, i * BLOCK : (i + 1) * BLOCK]
            out_ref[tile * blocks + i] = piece.astype(bf16)
        lse_ref[0, :, lanes] = top + jnp.log(total)
        return carry

    lax.fori_loop(0, q_ref.shape[1] // WIDTH, one_tile, 0)


def backward_kernel(
    parts, span_blocks, core_ref, table_ref, q_ref, full_ref, lse_ref, grad_ref, *refs
):
    kv_refs = refs[:parts]
    dq_ref = refs[parts]
    dkv_refs = refs[parts + 1 : 2 * parts + 1]
    dtable_ref, skew, dskew, rows, dkv = refs[2 * parts + 1 :]
    span = table_ref.shape[2]
    half = span // 2
    own_count = kv_refs[0].shape[1]
    key_count = parts * own_count
    skew[...] = skewed_table(table_ref[0])
    key_rows(kv_refs, rows)
    dskew[...] = jnp.zeros_like(dskew)
    dkv[...] = jnp.zeros_like(dkv)
    blocks = WIDTH // BLOCK
    step = 2 * BLOCK
    core = core_ref[0]

    def one_tile(tile, carry):
        lanes = pl.ds(pl.multiple_of(tile * WIDTH, WIDTH), WIDTH)
        query = q_ref[:, lanes] * jnp.asarray(score_scale, bf16)
        grad = jnp.concatenate(
            [grad_ref[tile * blocks + i] for i in range(blocks)], axis=1
        )
        lse = lse_ref[0, :, lanes]
        delta = jnp.sum(grad.astype(f32) * full_ref[:, lanes], axis=0, keepdims=True)
        query = jnp.concatenate([query, jnp.zeros_like(query)], axis=0)
        grad = jnp.concatenate([jnp.zeros_like(grad), grad], axis=0)
        query_rows = query.T
        grad_rows = grad.T
        start = half + begins(tile * blocks, core, parts, span_blocks)
        dq = jnp.zeros((HEAD_DIM, WIDTH), f32)
        for offset in range(0, key_count, step):
            keys = rows[offset : offset + step, :]
            raw = matmul(keys, query)
            dprob = matmul(keys, grad)
            probs = []
            dscores = []
            for inner in range(0, step, BLOCK):
                behind = start - key_begins(offset + inner, core, parts, own_count, span_blocks)
                here = pl.ds(pl.multiple_of(behind, BLOCK), WIDTH)
                own = slice(inner, inner + BLOCK)
                prob = jnp.exp(raw[own] + skew[:, here] - lse)
                dscore = prob * (dprob[own] - delta)
                dskew[:, here] += dscore
                probs.append(prob.astype(bf16))
                dscores.append(dscore.astype(bf16))
            prob = jnp.concatenate(probs, axis=0)
            dscore = jnp.concatenate(dscores, axis=0)
            dkv[offset : offset + step, :] += matmul(dscore, query_rows) + matmul(prob, grad_rows)
            part, inside = divmod(offset, own_count)
            dq = dq + matmul(kv_refs[part][:HEAD_DIM, inside : inside + step], dscore)
        dq_ref[:, lanes] = (dq * score_scale).astype(bf16)
        return carry

    lax.fori_loop(0, q_ref.shape[1] // WIDTH, one_tile, 0)
    for part, dkv_ref in enumerate(dkv_refs):
        dkv_ref[...] = dkv[part * own_count : (part + 1) * own_count, :].T.astype(bf16)
    folded = dskew[...]
    count = BLOCK
    while count > 1:
        count //= 2
        folded = folded[:count] + pltpu.roll(folded[count:], span - count, 1)
    dtable_ref[0] = pltpu.roll(folded, span - 1, 1)


def stack_spec(*shape):
    return pl.BlockSpec((1,) + shape, lambda head: (head, 0, 0))


def rows_spec(*shape):
    return pl.BlockSpec(shape, lambda head: (head, 0))


def place_spec(blocks):
    return pl.BlockSpec((blocks, HEAD_DIM, BLOCK), lambda head: (0, head, 0))


def attention_forward(span_blocks, core, table, query, kvs):
    count, span, parts = query.shape[1], table.shape[2], len(kvs)
    keys = parts * count
    scalars = pl.BlockSpec(memory_space=pltpu.SMEM)
    return pl.pallas_call(
        functools.partial(forward_kernel, parts, span_blocks),
        grid=(GROUP_HEADS,),
        in_specs=[scalars, stack_spec(1, span), rows_spec(HEAD_DIM, count)]
        + [rows_spec(2 * HEAD_DIM, count)] * parts,
        out_specs=[
            place_spec(count // BLOCK),
            rows_spec(HEAD_DIM, count),
            stack_spec(1, count),
        ],
        out_shape=[
            jax.ShapeDtypeStruct((count // BLOCK, GROUP_HEADS * HEAD_DIM, BLOCK), bf16),
            jax.ShapeDtypeStruct((GROUP_HEADS * HEAD_DIM, count), f32),
            jax.ShapeDtypeStruct((GROUP_HEADS, 1, count), f32),
        ],
        scratch_shapes=[
            pltpu.VMEM((BLOCK, span), f32),
            pltpu.VMEM((keys, WIDTH), f32),
            pltpu.VMEM((keys, WIDTH), bf16),
            pltpu.VMEM((keys, 2 * HEAD_DIM), bf16),
        ],
        compiler_params=pltpu.CompilerParams(vmem_limit_bytes=vmem_bytes),
        cost_estimate=pl.CostEstimate(
            flops=4 * GROUP_HEADS * HEAD_DIM * count * keys * 4,
            bytes_accessed=4 * GROUP_HEADS * HEAD_DIM * (count + keys) * 2,
            transcendentals=GROUP_HEADS * count * keys,
        ),
        name="attention_forward",
    )(core, table, query, *kvs)


def attention_backward(span_blocks, core, table, query, full, lse, grad, kvs):
    count, span, parts = query.shape[1], table.shape[2], len(kvs)
    keys = parts * count
    scalars = pl.BlockSpec(memory_space=pltpu.SMEM)
    return pl.pallas_call(
        functools.partial(backward_kernel, parts, span_blocks),
        grid=(GROUP_HEADS,),
        in_specs=[
            scalars,
            stack_spec(1, span),
            rows_spec(HEAD_DIM, count),
            rows_spec(HEAD_DIM, count),
            stack_spec(1, count),
            place_spec(count // BLOCK),
        ]
        + [rows_spec(2 * HEAD_DIM, count)] * parts,
        out_specs=[rows_spec(HEAD_DIM, count)]
        + [rows_spec(2 * HEAD_DIM, count)] * parts
        + [stack_spec(1, span)],
        out_shape=[jax.ShapeDtypeStruct((GROUP_HEADS * HEAD_DIM, count), bf16)]
        + [jax.ShapeDtypeStruct((GROUP_HEADS * 2 * HEAD_DIM, count), bf16)] * parts
        + [jax.ShapeDtypeStruct((GROUP_HEADS, 1, span), f32)],
        scratch_shapes=[
            pltpu.VMEM((BLOCK, span), f32),
            pltpu.VMEM((BLOCK, span), f32),
            pltpu.VMEM((keys, 2 * HEAD_DIM), bf16),
            pltpu.VMEM((keys, 2 * HEAD_DIM), f32),
        ],
        compiler_params=pltpu.CompilerParams(vmem_limit_bytes=vmem_bytes),
        cost_estimate=pl.CostEstimate(
            flops=10 * GROUP_HEADS * HEAD_DIM * count * keys * 4,
            bytes_accessed=4 * GROUP_HEADS * HEAD_DIM * (count + keys) * 4,
            transcendentals=GROUP_HEADS * count * keys,
        ),
        name="attention_backward",
    )(core, table, query, full, lse, grad, *kvs)


def shift(value, axis, step):
    size = lax.axis_size(axis)
    return lax.ppermute(value, axis, [(i, (i + step) % size) for i in range(size)])


def pick(value, index, dim=0):
    return lax.dynamic_index_in_dim(value, index, dim, keepdims=False)


def spread(parts, axis):
    return [parts[0]] + [shift(parts[k], axis, k) for k in range(1, len(parts))]


def give_back(parts, axis):
    return [parts[0]] + [shift(parts[k], axis, -k) for k in range(1, len(parts))]


def scatter_sum(value, axis, dim, wire=bf16):
    size = lax.axis_size(axis)
    index = lax.axis_index(axis)
    if size == 2:
        low = lax.index_in_dim(value, 0, dim, keepdims=False)
        high = lax.index_in_dim(value, 1, dim, keepdims=False)
        first = index == 0
        got = shift(jnp.where(first, high, low).astype(wire), axis, 1)
        return jnp.where(first, low, high).astype(f32) + got.astype(f32)
    total = pick(value, index, dim).astype(f32)
    for k in range(1, size):
        part = pick(value, lax.rem(index + k, size), dim).astype(wire)
        total = total + shift(part, axis, k).astype(f32)
    return total


def sum_everywhere(value, axes):
    for axis in axes:
        size = lax.axis_size(axis)
        step = 1
        while step < size:
            value = value + lax.ppermute(value, axis, [(i, i ^ step) for i in range(size)])
            step *= 2
    return value


def scatter_rows(value, *others):
    ga, gb, ctx, dp = (lax.axis_size(a) for a in ("ga", "gb", "context", "dp"))
    rows, cols = value.shape
    own = rows // (ga * gb * ctx * dp)
    value = value.reshape(ga, gb, ctx * dp * own, cols)
    value = after(scatter_sum(value, "gb", 1), *others)
    value = scatter_sum(value, "ga", 0)
    value = value.reshape(ctx, dp, own, cols)
    return scatter_sum(value, "dp", 1)


def split_halves(value):
    high = value.astype(bf16)
    return high, (value - high.astype(f32)).astype(bf16)


def gelu_parts(values):
    c = 0.7978845608028654
    square = values * values
    bent = jnp.tanh(c * values * (1.0 + 0.044715 * square))
    act = 0.5 * values * (1.0 + bent)
    slope = 0.5 * (1.0 + bent) + 0.5 * values * (1.0 - bent * bent) * c * (
        1.0 + 3 * 0.044715 * square
    )
    return act, slope


def after(value, *others):
    width = value.shape[-1]
    for other in others:
        first = other.reshape(-1, other.shape[-1])[:1]
        if first.shape[1] < width:
            first = jnp.concatenate([first] * -(-width // first.shape[1]), axis=1)
        first = first[:, :width]
        value = jnp.where(first == first, value, jnp.zeros_like(value))
    return value


def add_up(parts):
    total = parts[0].astype(f32)
    for part in parts[1:]:
        total = total + part.astype(f32)
    return total


def exchange(value, axis):
    return lax.all_to_all(value, axis, 0, 0, tiled=True)


def local(
    tokens,
    cotangent,
    query_key_value_weight,
    output_weight,
    gain_one,
    gain_two,
    router_weight,
    w_in,
    w_down,
    position_bias,
    bucket,
    route,
    slot,
    dropped,
):
    seq_count, tok_count = tokens.shape[:2]
    row_count = seq_count * tok_count
    ga, gb, ctx, dp = (lax.axis_size(a) for a in ("ga", "gb", "context", "dp"))
    experts = ga * gb
    capacity = (5 * row_count + 4 * experts - 1) // (4 * experts)
    group_rows = GROUPS * tok_count
    expert_axis = ("ga", "gb")
    group_axis = ("ga", "context")
    ga_index, gb_index, ctx_index = (lax.axis_index(a) for a in ("ga", "gb", "context"))
    group_index = lax.axis_index(group_axis)
    head_group = lax.rem(group_index, HEAD_GROUPS)
    in_order = tok_count % BLOCK != 0

    outgoing = jnp.broadcast_to(tokens[:, None], (SEQ_DEV, HEAD_GROUPS, tok_count, D))
    group_tokens = exchange(outgoing.reshape(GROUPS, tok_count, D), group_axis)
    group_tokens = group_tokens.reshape(group_rows, D)
    span_blocks = ctx * tok_count // BLOCK
    core = gb_index.astype(jnp.int32)[None]

    weight_group = query_key_value_weight.T.reshape(3, HEAD_GROUPS, GROUP_HEADS, HEAD_DIM, D)
    weight_group = pick(weight_group, head_group, 1)
    weight_query = weight_group[0].reshape(GROUP_HEADS * HEAD_DIM, D)
    weight_kv = jnp.transpose(weight_group[1:], (1, 0, 2, 3)).reshape(-1, D)

    def pair(value):
        return lax.ppermute(value, "context", [(i, i ^ 1) for i in range(ctx)])

    def every_other(value):
        return [value] + [shift(value, "context", 2 * k) for k in range(1, ctx // 2)]

    def every_other_back(parts):
        return [parts[0]] + [shift(parts[k], "context", -2 * k) for k in range(1, len(parts))]


    dp_index = lax.axis_index("dp")

    def by_owner(weight):
        cut = weight.shape[1] // dp
        if dp == 2:
            low, high = weight[:, :cut], weight[:, cut:]
            first = dp_index == 0
            parts = [jnp.where(first, low, high), jnp.where(first, high, low)]
            return jnp.concatenate(parts, axis=1)
        return jnp.roll(weight.reshape(D, dp, cut), -dp_index, axis=1).reshape(D, -1)

    own_in, own_down = by_owner(w_in[0]), by_owner(w_down[0])

    route_flat = route.reshape(-1)
    position = route_flat * capacity + slot.reshape(-1)
    assign = (
        (jnp.arange(experts * capacity, dtype=jnp.int32)[:, None] == position[None, :])
        & (dropped.reshape(-1) == 0)[None, :]
    ).astype(bf16)
    grad_low = cotangent.reshape(row_count, D)
    grad_buffer = matmul(assign, grad_low).astype(bf16).reshape(experts, capacity, D)
    expert_index = lax.axis_index(expert_axis)

    def swap(blocks):
        swapped = jnp.zeros_like(blocks)
        for k in range(experts):
            part = pick(blocks, lax.rem(expert_index + k, experts))
            part = shift(part, expert_axis, k) if k else part
            came_from = lax.rem(expert_index - k + experts, experts)
            swapped = lax.dynamic_update_index_in_dim(swapped, part, came_from, 0)
        return swapped.reshape(-1, D)

    grad_rows = swap(grad_buffer)

    onehot = (
        jnp.arange(position_bias.shape[0], dtype=jnp.int32)[:, None]
        == jnp.pad(bucket[::-1], (0, 1), constant_values=-1)[None, :]
    ).astype(f32)
    bias_heads = lax.dynamic_slice_in_dim(position_bias.T, head_group * GROUP_HEADS, GROUP_HEADS, 0)
    table = jnp.dot(bias_heads, onehot, precision=precise_mode, preferred_element_type=f32)
    table = table[:, None, :]

    def normalised(values):
        scale = lax.rsqrt(jnp.mean(values * values, axis=-1, keepdims=True) + norm_epsilon)
        return scale, values * scale

    group_normed = (normalised(group_tokens.astype(f32))[1] * gain_one).astype(bf16)
    own_kv = contract_cols(weight_kv, group_normed).astype(bf16)
    kvs = [own_kv] + [shift(own_kv, "gb", k) for k in range(1, gb)]
    query = contract_cols(weight_query, group_normed).astype(bf16)
    query = after(query, grad_rows)

    grad_blocks = every_other(after(grad_rows, group_normed))
    both_in = [own_in, pair(after(own_in, group_normed))]

    attended_parts, attended, lse = attention_forward(
        span_blocks, core, table, query, kvs
    )

    def to_sources(parts):
        parts = parts.reshape(group_rows // BLOCK, -1, BLOCK)
        if in_order:
            parts = jnp.transpose(
                parts.reshape(group_rows // BLOCK, parts.shape[1], BLOCK // tok_count, tok_count),
                (0, 2, 1, 3),
            ).reshape(GROUPS, parts.shape[1], tok_count)
        return parts

    def from_sources(parts):
        if in_order:
            merged = BLOCK // tok_count
            parts = jnp.transpose(
                parts.reshape(GROUPS // merged, merged, parts.shape[1], tok_count), (0, 2, 1, 3)
            ).reshape(GROUPS // merged, parts.shape[1], BLOCK)
        return parts

    attended_low = exchange(to_sources(attended_parts), group_axis)
    attended_low = attended_low.reshape(seq_count, D, tok_count)
    both_down = [own_down, pair(after(own_down, attended_low))]

    inputs = tokens.reshape(row_count, D).astype(f32)
    branch = jnp.concatenate(
        [contract_rows(attended_low[i], output_weight) for i in range(seq_count)], axis=0
    )
    middle = inputs + branch
    scale_two, unit_two = normalised(middle)
    normalized_second = unit_two * gain_two
    router_logits = jnp.dot(
        normalized_second, router_weight, precision=precise_mode, preferred_element_type=f32
    )
    router = jax.nn.softmax(router_logits, axis=-1)
    chosen = (route_flat[:, None] == jnp.arange(experts, dtype=jnp.int32)[None, :]).astype(f32)
    gate = jnp.sum(router * chosen, axis=-1, keepdims=True)

    gate_high, gate_low = split_halves(gate)
    payload = jnp.concatenate(
        [
            after(
                normalized_second.astype(bf16), *grad_blocks[1:], both_in[1]
            ),
            gate_high,
            gate_low,
            jnp.zeros((row_count, 126), bf16),
        ],
        axis=1,
    )
    buffer = matmul(assign, payload).astype(bf16).reshape(experts, capacity, D + 128)
    received = exchange(buffer, expert_axis).reshape(-1, D + 128)
    row_total = received.shape[0]
    gate_rows = contract_cols(jnp.eye(16, 128, dtype=bf16), received[:, D:]).astype(bf16)
    gate_rows = jnp.pad(gate_rows, ((0, 0), (0, -row_total % D)))[:, :D]
    sent_blocks = every_other(jnp.concatenate([received[:, :D], gate_rows], axis=0))
    row_blocks = [block[:row_total] for block in sent_blocks]
    gate_blocks = [block[row_total:, :row_total] for block in sent_blocks]
    gate_width = jnp.where(jnp.arange(16)[:, None] < 2, 1.0, 0.0) * jnp.ones((1, D), f32)
    gate_width = gate_width.astype(bf16)

    ones = jnp.ones((8, own_in.shape[1]), bf16)
    hidden_blocks, pre_blocks, back_parts = [], [], []
    for rows_now, grads_now in zip(row_blocks, grad_blocks):
        hidden_blocks.append([])
        pre_blocks.append([])
        back = gate_part = 0.0
        for weight_in, weight_down in zip(both_in, both_down):
            grad_hidden = matmul(after(grads_now, sent_blocks[0]), weight_down)
            act, slope = gelu_parts(matmul(rows_now, weight_in))
            hidden = act.astype(bf16)
            grad_pre = (grad_hidden * slope).astype(bf16)
            hidden_blocks[-1].append(hidden)
            pre_blocks[-1].append(grad_pre)
            back = back + contract_cols(grad_pre, weight_in)
            product = (grad_hidden * hidden.astype(f32)).astype(bf16)
            gate_part = gate_part + contract_cols(ones, product)[:1]
        gate_part = jnp.concatenate(
            split_halves(gate_part) + (jnp.zeros((14, row_total), bf16),), axis=0
        )
        gate_part = jnp.pad(gate_part, ((0, 0), (0, -row_total % D)))[:, :D]
        back = jnp.concatenate([back.astype(bf16), gate_part], axis=0)
        back_parts.append(after(back, *sent_blocks[1:]))

    back_total = add_up(every_other_back(back_parts))
    back_sum = back_total[:row_total].astype(bf16)
    gate_sum = back_total[row_total : row_total + 2, :row_total]
    gate_sum = gate_sum[:1] + gate_sum[1:]
    gate_halves = split_halves(gate_sum[:1])
    gate_column = contract_rows(
        jnp.concatenate(gate_halves + (jnp.zeros((6, gate_sum.shape[1]), bf16),), axis=0),
        jnp.eye(8, 128, dtype=bf16),
    ).astype(bf16)
    back_rows = jnp.concatenate([back_sum, gate_column], axis=1)
    back_rows = exchange(back_rows.reshape(experts, capacity, D + 128), expert_axis)
    back_rows = contract_rows(assign, back_rows.reshape(-1, D + 128))
    grad_sent = back_rows[:, :D] * gate
    grad_gate = back_rows[:, D : D + 1] + back_rows[:, D + 1 : D + 2]

    grad_out = grad_low.astype(f32)
    grad_logits = grad_gate * gate * (chosen - router)
    grad_normed_two = grad_sent + lax.dot_general(
        grad_logits,
        router_weight,
        (((1,), (1,)), ((), ())),
        precision=precise_mode,
        preferred_element_type=f32,
    )
    scaled_two = gain_two * grad_normed_two
    cube_two = scale_two * scale_two * scale_two
    grad_middle = (
        grad_out
        + scale_two * scaled_two
        - middle * cube_two * jnp.mean(scaled_two * middle, axis=-1, keepdims=True)
    )
    grad_branch = grad_middle.astype(bf16)

    grad_heads = jnp.concatenate(
        [
            contract_cols(output_weight, grad_branch[i * tok_count : (i + 1) * tok_count])
            for i in range(seq_count)
        ],
        axis=0,
    ).astype(bf16)
    grad_heads = exchange(
        grad_heads.reshape(GROUPS, GROUP_HEADS * HEAD_DIM, tok_count), group_axis
    )

    out_parts = [
        add_up([contract_cols(h, w) for h, w in zip(hidden, both_down)]).astype(bf16)
        for hidden in hidden_blocks
    ]
    result_parts = every_other_back(
        out_parts[:1] + [after(part, grad_heads) for part in out_parts[1:]]
    )

    all_rows = jnp.concatenate(row_blocks, axis=0)
    all_grads = jnp.concatenate(grad_blocks, axis=0)
    all_gates = contract_rows(jnp.concatenate(gate_blocks, axis=1), gate_width)
    all_returned = (all_gates * all_grads.astype(f32)).astype(bf16)
    all_hidden = [jnp.concatenate(blocks, axis=0) for blocks in zip(*hidden_blocks)]
    all_pre = [
        (jnp.concatenate(blocks, axis=0).astype(f32) * all_gates[:, :1]).astype(bf16)
        for blocks in zip(*pre_blocks)
    ]
    cut = own_in.shape[1] // dp

    def reduced(left, rights):
        def columns(k):
            piece = [right[:, k * cut : (k + 1) * cut] for right in rights]
            return contract_rows(left, jnp.concatenate(piece, axis=1)).astype(bf16)

        came = [shift(columns(k), "dp", k) for k in range(1, dp)]
        mine = columns(0)
        own = add_up([mine[:, :cut]] + [part[:, :cut] for part in came])
        partner = add_up([mine[:, cut:]] + [part[:, cut:] for part in came]).astype(bf16)
        return own, partner

    in_grad, in_partner = reduced(all_rows, all_pre)
    down_grad, down_partner = reduced(all_returned, all_hidden)
    in_came = pair(after(in_partner, back_sum))
    grad_heads = after(grad_heads, in_came)


    outs = attention_backward(
        span_blocks,
        core,
        table,
        query,
        attended,
        lse,
        from_sources(grad_heads),
        kvs,
    )
    grad_query, grad_kvs, grad_table = outs[0], outs[1:-1], outs[-1]
    grad_kv = add_up(give_back(grad_kvs, "gb")).astype(bf16)
    grad_projected = jnp.concatenate([grad_query, grad_kv], axis=0)
    weight_all = jnp.concatenate([weight_query, weight_kv], axis=0)
    part_normed = contract_rows(grad_projected, weight_all).astype(bf16)
    down_came = pair(after(down_partner, part_normed))
    part_normed = part_normed.reshape(ga, ctx, tok_count, D)

    def over_context(parts):
        sums = {}
        for k in range(ctx):
            part = pick(parts, lax.rem(ctx_index - k + ctx, ctx))
            part = shift(part, "context", -k) if k else part
            from_ctx = lax.rem(ctx_index + k, ctx)
            for i in range(1 if ctx == HEAD_GROUPS else seq_count):
                kept = part.astype(f32)
                if ctx != HEAD_GROUPS:
                    kept = jnp.where(from_ctx // HEAD_GROUPS == i, kept, 0.0)
                sums[i] = sums[i] + kept if i in sums else kept
        return list(sums.values())

    if ga == 1:
        grad_normed = over_context(part_normed[0])
        first_sum = part_normed
    else:
        on_low = ga_index == 0
        total = over_context(jnp.transpose(part_normed, (1, 0, 2, 3)))[0]
        first_sum = jnp.where(on_low, total[1], total[0]).astype(bf16)
        came = shift(first_sum, "ga", 1).astype(f32)
        own_sum = jnp.where(on_low, total[0], total[1])
        grad_normed = [jnp.where(on_low, own_sum, came), jnp.where(on_low, came, own_sum)]

    padding = jnp.zeros((-grad_projected.shape[0] % BLOCK, grad_projected.shape[1]), bf16)
    qkv_part = lax.dot_general(
        after(group_normed, part_normed),
        jnp.concatenate([grad_projected, padding], axis=0),
        (((0,), (1,)), ((), ())),
        preferred_element_type=f32,
    ).astype(bf16)
    out_part_grad = add_up(
        [
            matmul(attended_low[i], grad_branch[i * tok_count : (i + 1) * tok_count])
            for i in range(seq_count)
        ]
    )
    router_grad = lax.dot_general(
        normalized_second,
        grad_logits,
        (((0,), (0,)), ((), ())),
        precision=precise_mode,
        preferred_element_type=f32,
    )
    gain_two_grad = jnp.sum(grad_normed_two * unit_two, axis=0)
    dense = jnp.concatenate(
        [out_part_grad, router_grad, gain_two_grad[:, None], jnp.zeros((D, 123), f32)], axis=1
    ).astype(bf16)
    bias_part = lax.dot_general(
        after(grad_table, part_normed)[:, 0],
        onehot,
        (((1,), (1,)), ((), ())),
        precision=precise_mode,
        preferred_element_type=f32,
    )
    width_qkv = qkv_part.shape[1]
    bias_grad = lax.dynamic_update_slice_in_dim(
        jnp.zeros((HEADS, bias_part.shape[1]), f32), bias_part, head_group * GROUP_HEADS, 0
    )

    own_rows = D // (ga * gb * ctx * dp)
    bias_rows = jnp.pad(bias_grad, ((0, 16 - HEADS), (0, width_qkv - bias_grad.shape[1])))

    def first_exchange(value, *riders):
        value = value.astype(bf16).reshape(experts, -1, value.shape[1])
        for rider in riders:
            rider = jnp.broadcast_to(rider.astype(bf16), (experts,) + rider.shape)
            value = jnp.concatenate([value, rider], axis=1)
        return add_up(list(exchange(value, expert_axis)))

    def second_exchange(value, *riders):
        value = value.astype(bf16).reshape(ctx * dp, own_rows, value.shape[1])
        for rider in riders:
            rider = jnp.broadcast_to(rider.astype(bf16), (ctx * dp,) + rider.shape)
            value = jnp.concatenate([value, rider], axis=1)
        return exchange(value, ("context", "dp"))

    dense = first_exchange(dense)
    summed = first_exchange(after(qkv_part, dense), bias_rows)
    bias_shape = bias_grad.shape
    bias_row = summed[-16:][:HEADS, : bias_shape[1]].reshape(1, -1)
    bias_rows = jnp.pad(
        bias_row, ((0, 7), (0, summed.shape[1] + dense.shape[1] - bias_row.shape[1]))
    )
    summed = after(
        jnp.concatenate([summed[:-16], dense], axis=1), first_sum, down_came
    )
    summed = second_exchange(summed, bias_rows).astype(f32)
    bias_grad = add_up(list(summed[:, own_rows, : bias_row.shape[1]])).reshape(bias_shape).T
    dense = add_up(list(summed[:, :own_rows, width_qkv:]))
    summed = summed[:, :own_rows, :width_qkv].reshape(ctx, dp, own_rows, width_qkv)
    by_group = []
    for group in range(HEAD_GROUPS):
        by_group.append(add_up([summed[z, d] for z in range(group, ctx, HEAD_GROUPS) for d in range(dp)]))
    by_group = jnp.stack(by_group, axis=1)
    width = GROUP_HEADS * HEAD_DIM
    query_cols = by_group[:, :, :width].reshape(own_rows, 1, D)
    kv_cols = by_group[:, :, width : 3 * width].reshape(own_rows, HEADS, 2, HEAD_DIM)
    kv_cols = jnp.transpose(kv_cols, (0, 2, 1, 3)).reshape(own_rows, 2, D)
    qkv_total = jnp.concatenate([query_cols, kv_cols], axis=1).reshape(own_rows, 3 * D)
    first_row = (lax.axis_index(("ga", "gb", "context", "dp"))) * own_rows
    weight_rows = lax.dynamic_slice_in_dim(query_key_value_weight, first_row, own_rows, 0)
    gain_rows = lax.dynamic_slice_in_dim(gain_one, first_row, own_rows, 0)
    gain_one_total = jnp.sum(qkv_total * weight_rows.astype(f32), axis=1) / gain_rows

    result = after(add_up(result_parts).astype(bf16), part_normed.reshape(-1, D))
    returned = contract_rows(assign, swap(result.reshape(experts, capacity, D)))
    output = (middle + gate * returned).astype(bf16)

    grad_normed = jnp.concatenate(grad_normed, axis=0)
    scale_one = normalised(inputs)[0]
    scaled_one = gain_one * grad_normed
    cube_one = scale_one * scale_one * scale_one
    grad_inputs = (
        grad_middle
        + scale_one * scaled_one
        - inputs * cube_one * jnp.mean(scaled_one * inputs, axis=-1, keepdims=True)
    )

    return (
        output.reshape(seq_count, tok_count, D),
        grad_inputs.astype(bf16).reshape(seq_count, tok_count, D),
        qkv_total,
        dense[:, :D],
        gain_one_total,
        dense[:, D + 4],
        dense[:, D : D + 4],
        (in_grad + in_came.astype(f32))[None],
        (down_grad + down_came.astype(f32))[None],
        bias_grad,
    )


def solution(mesh):
    ctx = mesh.shape["context"]
    ga = max(GROUPS // ctx, 1)
    gb = mesh.shape["expert"] // ga
    fine = Mesh(
        mesh.devices.reshape(ga, gb, ctx, mesh.shape["dp"]), ("ga", "gb", "context", "dp")
    )
    expert = ("ga", "gb")
    blocks = ("ga", "gb", "context")
    everywhere = ("ga", "gb", "context", "dp")
    return jax.shard_map(
        local,
        mesh=fine,
        in_specs=(
            P("dp", blocks, None),
            P("dp", blocks, None),
            P(),
            P(),
            P(),
            P(),
            P(),
            P(expert, None, "context"),
            P(expert, None, "context"),
            P(),
            P(),
            P("dp", blocks),
            P("dp", blocks),
            P("dp", blocks),
        ),
        out_specs=(
            P("dp", blocks, None),
            P("dp", blocks, None),
            P(everywhere, None),
            P(everywhere, None),
            P(everywhere),
            P(everywhere),
            P(everywhere, None),
            P(expert, None, ("context", "dp")),
            P(expert, None, ("context", "dp")),
            P(),
        ),
        check_vma=False,
    )
```

```python
import functools

import jax
import jax.numpy as jnp
from jax import lax
from jax.experimental import pallas as pl
from jax.experimental.pallas import tpu as pltpu
from jax.sharding import Mesh, PartitionSpec as P

D = 768
HEADS = 12
HEAD_DIM = 64
GROUP_HEADS = 3
HEAD_GROUPS = HEADS // GROUP_HEADS
SEQ_DEV = 2
GROUPS = SEQ_DEV * HEAD_GROUPS
WIDTH = 256
BLOCK = 128

norm_epsilon = 1e-06
score_scale = 0.125
precise_mode = lax.Precision.HIGHEST
vmem_bytes = 50 * 1024 * 1024
f32 = jnp.float32
bf16 = jnp.bfloat16


def matmul(left, right):
    return jnp.dot(left, right, preferred_element_type=f32)


def contract_rows(left, right):
    return lax.dot_general(left, right, (((0,), (0,)), ((), ())), preferred_element_type=f32)


def contract_cols(left, right):
    return lax.dot_general(left, right, (((1,), (1,)), ((), ())), preferred_element_type=f32)


def skewed_table(table_row):
    wide = jnp.broadcast_to(table_row, (BLOCK, table_row.shape[1]))
    return pltpu.roll(wide, 1, 1, stride=1, stride_axis=0)


def key_rows(kv_refs, rows):
    for part, kv_ref in enumerate(kv_refs):
        count = kv_ref.shape[1]
        rows[part * count : (part + 1) * count, :] = kv_ref[...].T


def begins(block, core, cores, span_blocks):
    return ((block // span_blocks * cores + core) * span_blocks + block % span_blocks) * BLOCK


def key_begins(offset, core, parts, own_count, span_blocks):
    part, inside = divmod(offset, own_count)
    owner = lax.rem(core - part + parts, parts)
    return begins(inside // BLOCK, owner, parts, span_blocks)


def forward_kernel(parts, span_blocks, core_ref, table_ref, q_ref, *refs):
    kv_refs = refs[:parts]
    out_ref, full_ref, lse_ref, skew, score, weight, rows = refs[parts:]
    half = table_ref.shape[2] // 2
    own_count = kv_refs[0].shape[1]
    key_count = parts * own_count
    skew[...] = skewed_table(table_ref[0])
    key_rows(kv_refs, rows)
    blocks = WIDTH // BLOCK
    core = core_ref[0]

    def one_tile(tile, carry):
        lanes = pl.ds(pl.multiple_of(tile * WIDTH, WIDTH), WIDTH)
        query = q_ref[:, lanes] * jnp.asarray(score_scale, bf16)
        query = jnp.concatenate([query, jnp.zeros_like(query)], axis=0)
        start = half + begins(tile * blocks, core, parts, span_blocks)
        top = jnp.full((8, WIDTH), -jnp.inf, f32)
        for block in range(key_count // BLOCK):
            offset = block * BLOCK
            behind = start - key_begins(offset, core, parts, own_count, span_blocks)
            bias = skew[:, pl.ds(pl.multiple_of(behind, BLOCK), WIDTH)]
            part = matmul(rows[offset : offset + BLOCK, :], query) + bias
            score[offset : offset + BLOCK, :] = part
            top = jnp.maximum(top, jnp.max(part.reshape(BLOCK // 8, 8, WIDTH), axis=0))
        top = jnp.max(top, axis=0, keepdims=True)
        total = jnp.zeros((8, WIDTH), f32)
        for block in range(key_count // BLOCK):
            offset = block * BLOCK
            part = jnp.exp(score[offset : offset + BLOCK, :] - top)
            total = total + jnp.sum(part.reshape(BLOCK // 8, 8, WIDTH), axis=0)
            weight[offset : offset + BLOCK, :] = part.astype(bf16)
        total = jnp.sum(total, axis=0, keepdims=True)
        blended = jnp.zeros((HEAD_DIM, WIDTH), f32)
        for part, kv_ref in enumerate(kv_refs):
            own = weight[part * own_count : (part + 1) * own_count, :]
            blended = blended + matmul(kv_ref[HEAD_DIM:, :], own)
        blended = blended / total
        full_ref[:, lanes] = blended
        for i in range(blocks):
            piece = blended[:, i * BLOCK : (i + 1) * BLOCK]
            out_ref[tile * blocks + i] = piece.astype(bf16)
        lse_ref[0, :, lanes] = top + jnp.log(total)
        return carry

    lax.fori_loop(0, q_ref.shape[1] // WIDTH, one_tile, 0)


def backward_kernel(
    parts, span_blocks, core_ref, table_ref, q_ref, full_ref, lse_ref, grad_ref, *refs
):
    kv_refs = refs[:parts]
    dq_ref = refs[parts]
    dkv_refs = refs[parts + 1 : 2 * parts + 1]
    dtable_ref, skew, dskew, rows, dkv = refs[2 * parts + 1 :]
    span = table_ref.shape[2]
    half = span // 2
    own_count = kv_refs[0].shape[1]
    key_count = parts * own_count
    skew[...] = skewed_table(table_ref[0])
    key_rows(kv_refs, rows)
    dskew[...] = jnp.zeros_like(dskew)
    dkv[...] = jnp.zeros_like(dkv)
    blocks = WIDTH // BLOCK
    step = 2 * BLOCK
    core = core_ref[0]

    def one_tile(tile, carry):
        lanes = pl.ds(pl.multiple_of(tile * WIDTH, WIDTH), WIDTH)
        query = q_ref[:, lanes] * jnp.asarray(score_scale, bf16)
        grad = jnp.concatenate(
            [grad_ref[tile * blocks + i] for i in range(blocks)], axis=1
        )
        lse = lse_ref[0, :, lanes]
        delta = jnp.sum(grad.astype(f32) * full_ref[:, lanes], axis=0, keepdims=True)
        query = jnp.concatenate([query, jnp.zeros_like(query)], axis=0)
        grad = jnp.concatenate([jnp.zeros_like(grad), grad], axis=0)
        query_rows = query.T
        grad_rows = grad.T
        start = half + begins(tile * blocks, core, parts, span_blocks)
        dq = jnp.zeros((HEAD_DIM, WIDTH), f32)
        for offset in range(0, key_count, step):
            keys = rows[offset : offset + step, :]
            raw = matmul(keys, query)
            dprob = matmul(keys, grad)
            probs = []
            dscores = []
            for inner in range(0, step, BLOCK):
                behind = start - key_begins(offset + inner, core, parts, own_count, span_blocks)
                here = pl.ds(pl.multiple_of(behind, BLOCK), WIDTH)
                own = slice(inner, inner + BLOCK)
                prob = jnp.exp(raw[own] + skew[:, here] - lse)
                dscore = prob * (dprob[own] - delta)
                dskew[:, here] += dscore
                probs.append(prob.astype(bf16))
                dscores.append(dscore.astype(bf16))
            prob = jnp.concatenate(probs, axis=0)
            dscore = jnp.concatenate(dscores, axis=0)
            dkv[offset : offset + step, :] += matmul(dscore, query_rows) + matmul(prob, grad_rows)
            part, inside = divmod(offset, own_count)
            dq = dq + matmul(kv_refs[part][:HEAD_DIM, inside : inside + step], dscore)
        dq_ref[:, lanes] = (dq * score_scale).astype(bf16)
        return carry

    lax.fori_loop(0, q_ref.shape[1] // WIDTH, one_tile, 0)
    for part, dkv_ref in enumerate(dkv_refs):
        dkv_ref[...] = dkv[part * own_count : (part + 1) * own_count, :].T.astype(bf16)
    folded = dskew[...]
    count = BLOCK
    while count > 1:
        count //= 2
        folded = folded[:count] + pltpu.roll(folded[count:], span - count, 1)
    dtable_ref[0] = pltpu.roll(folded, span - 1, 1)


def stack_spec(*shape):
    return pl.BlockSpec((1,) + shape, lambda head: (head, 0, 0))


def rows_spec(*shape):
    return pl.BlockSpec(shape, lambda head: (head, 0))


def place_spec(blocks):
    return pl.BlockSpec((blocks, HEAD_DIM, BLOCK), lambda head: (0, head, 0))


def attention_forward(span_blocks, core, table, query, kvs):
    count, span, parts = query.shape[1], table.shape[2], len(kvs)
    keys = parts * count
    scalars = pl.BlockSpec(memory_space=pltpu.SMEM)
    return pl.pallas_call(
        functools.partial(forward_kernel, parts, span_blocks),
        grid=(GROUP_HEADS,),
        in_specs=[scalars, stack_spec(1, span), rows_spec(HEAD_DIM, count)]
        + [rows_spec(2 * HEAD_DIM, count)] * parts,
        out_specs=[
            place_spec(count // BLOCK),
            rows_spec(HEAD_DIM, count),
            stack_spec(1, count),
        ],
        out_shape=[
            jax.ShapeDtypeStruct((count // BLOCK, GROUP_HEADS * HEAD_DIM, BLOCK), bf16),
            jax.ShapeDtypeStruct((GROUP_HEADS * HEAD_DIM, count), f32),
            jax.ShapeDtypeStruct((GROUP_HEADS, 1, count), f32),
        ],
        scratch_shapes=[
            pltpu.VMEM((BLOCK, span), f32),
            pltpu.VMEM((keys, WIDTH), f32),
            pltpu.VMEM((keys, WIDTH), bf16),
            pltpu.VMEM((keys, 2 * HEAD_DIM), bf16),
        ],
        compiler_params=pltpu.CompilerParams(vmem_limit_bytes=vmem_bytes),
        cost_estimate=pl.CostEstimate(
            flops=4 * GROUP_HEADS * HEAD_DIM * count * keys * 4,
            bytes_accessed=4 * GROUP_HEADS * HEAD_DIM * (count + keys) * 2,
            transcendentals=GROUP_HEADS * count * keys,
        ),
        name="attention_forward",
    )(core, table, query, *kvs)


def attention_backward(span_blocks, core, table, query, full, lse, grad, kvs):
    count, span, parts = query.shape[1], table.shape[2], len(kvs)
    keys = parts * count
    scalars = pl.BlockSpec(memory_space=pltpu.SMEM)
    return pl.pallas_call(
        functools.partial(backward_kernel, parts, span_blocks),
        grid=(GROUP_HEADS,),
        in_specs=[
            scalars,
            stack_spec(1, span),
            rows_spec(HEAD_DIM, count),
            rows_spec(HEAD_DIM, count),
            stack_spec(1, count),
            place_spec(count // BLOCK),
        ]
        + [rows_spec(2 * HEAD_DIM, count)] * parts,
        out_specs=[rows_spec(HEAD_DIM, count)]
        + [rows_spec(2 * HEAD_DIM, count)] * parts
        + [stack_spec(1, span)],
        out_shape=[jax.ShapeDtypeStruct((GROUP_HEADS * HEAD_DIM, count), bf16)]
        + [jax.ShapeDtypeStruct((GROUP_HEADS * 2 * HEAD_DIM, count), bf16)] * parts
        + [jax.ShapeDtypeStruct((GROUP_HEADS, 1, span), f32)],
        scratch_shapes=[
            pltpu.VMEM((BLOCK, span), f32),
            pltpu.VMEM((BLOCK, span), f32),
            pltpu.VMEM((keys, 2 * HEAD_DIM), bf16),
            pltpu.VMEM((keys, 2 * HEAD_DIM), f32),
        ],
        compiler_params=pltpu.CompilerParams(vmem_limit_bytes=vmem_bytes),
        cost_estimate=pl.CostEstimate(
            flops=10 * GROUP_HEADS * HEAD_DIM * count * keys * 4,
            bytes_accessed=4 * GROUP_HEADS * HEAD_DIM * (count + keys) * 4,
            transcendentals=GROUP_HEADS * count * keys,
        ),
        name="attention_backward",
    )(core, table, query, full, lse, grad, *kvs)


def shift(value, axis, step):
    size = lax.axis_size(axis)
    return lax.ppermute(value, axis, [(i, (i + step) % size) for i in range(size)])


def pick(value, index, dim=0):
    return lax.dynamic_index_in_dim(value, index, dim, keepdims=False)


def spread(parts, axis):
    return [parts[0]] + [shift(parts[k], axis, k) for k in range(1, len(parts))]


def give_back(parts, axis):
    return [parts[0]] + [shift(parts[k], axis, -k) for k in range(1, len(parts))]


def scatter_sum(value, axis, dim, wire=bf16):
    size = lax.axis_size(axis)
    index = lax.axis_index(axis)
    if size == 2:
        low = lax.index_in_dim(value, 0, dim, keepdims=False)
        high = lax.index_in_dim(value, 1, dim, keepdims=False)
        first = index == 0
        got = shift(jnp.where(first, high, low).astype(wire), axis, 1)
        return jnp.where(first, low, high).astype(f32) + got.astype(f32)
    total = pick(value, index, dim).astype(f32)
    for k in range(1, size):
        part = pick(value, lax.rem(index + k, size), dim).astype(wire)
        total = total + shift(part, axis, k).astype(f32)
    return total


def sum_everywhere(value, axes):
    for axis in axes:
        size = lax.axis_size(axis)
        step = 1
        while step < size:
            value = value + lax.ppermute(value, axis, [(i, i ^ step) for i in range(size)])
            step *= 2
    return value


def scatter_rows(value, *others):
    ga, gb, ctx, dp = (lax.axis_size(a) for a in ("ga", "gb", "context", "dp"))
    rows, cols = value.shape
    own = rows // (ga * gb * ctx * dp)
    value = value.reshape(ga, gb, ctx * dp * own, cols)
    value = after(scatter_sum(value, "gb", 1), *others)
    value = scatter_sum(value, "ga", 0)
    value = value.reshape(ctx, dp, own, cols)
    return scatter_sum(value, "dp", 1)


def split_halves(value):
    high = value.astype(bf16)
    return high, (value - high.astype(f32)).astype(bf16)


def gelu_parts(values):
    c = 0.7978845608028654
    square = values * values
    bent = jnp.tanh(c * values * (1.0 + 0.044715 * square))
    act = 0.5 * values * (1.0 + bent)
    slope = 0.5 * (1.0 + bent) + 0.5 * values * (1.0 - bent * bent) * c * (
        1.0 + 3 * 0.044715 * square
    )
    return act, slope


def after(value, *others):
    width = value.shape[-1]
    for other in others:
        first = other.reshape(-1, other.shape[-1])[:1]
        if first.shape[1] < width:
            first = jnp.concatenate([first] * -(-width // first.shape[1]), axis=1)
        first = first[:, :width]
        value = jnp.where(first == first, value, jnp.zeros_like(value))
    return value


def add_up(parts):
    total = parts[0].astype(f32)
    for part in parts[1:]:
        total = total + part.astype(f32)
    return total


def exchange(value, axis):
    return lax.all_to_all(value, axis, 0, 0, tiled=True)


def local(
    tokens,
    cotangent,
    query_key_value_weight,
    output_weight,
    gain_one,
    gain_two,
    router_weight,
    w_in,
    w_down,
    position_bias,
    bucket,
    route,
    slot,
    dropped,
):
    seq_count, tok_count = tokens.shape[:2]
    row_count = seq_count * tok_count
    ga, gb, ctx, dp = (lax.axis_size(a) for a in ("ga", "gb", "context", "dp"))
    experts = ga * gb
    capacity = (5 * row_count + 4 * experts - 1) // (4 * experts)
    group_rows = GROUPS * tok_count
    expert_axis = ("ga", "gb")
    group_axis = ("ga", "context")
    ga_index, gb_index, ctx_index = (lax.axis_index(a) for a in ("ga", "gb", "context"))
    group_index = lax.axis_index(group_axis)
    head_group = lax.rem(group_index, HEAD_GROUPS)
    in_order = tok_count % BLOCK != 0

    outgoing = jnp.broadcast_to(tokens[:, None], (SEQ_DEV, HEAD_GROUPS, tok_count, D))
    group_tokens = exchange(outgoing.reshape(GROUPS, tok_count, D), group_axis)
    group_tokens = group_tokens.reshape(group_rows, D)
    span_blocks = ctx * tok_count // BLOCK
    core = gb_index.astype(jnp.int32)[None]

    weight_group = query_key_value_weight.T.reshape(3, HEAD_GROUPS, GROUP_HEADS, HEAD_DIM, D)
    weight_group = pick(weight_group, head_group, 1)
    weight_query = weight_group[0].reshape(GROUP_HEADS * HEAD_DIM, D)
    weight_kv = jnp.transpose(weight_group[1:], (1, 0, 2, 3)).reshape(-1, D)

    def pair(value):
        return lax.ppermute(value, "context", [(i, i ^ 1) for i in range(ctx)])

    def every_other(value):
        return [value] + [shift(value, "context", 2 * k) for k in range(1, ctx // 2)]

    def every_other_back(parts):
        return [parts[0]] + [shift(parts[k], "context", -2 * k) for k in range(1, len(parts))]


    dp_index = lax.axis_index("dp")

    def by_owner(weight):
        cut = weight.shape[1] // dp
        if dp == 2:
            low, high = weight[:, :cut], weight[:, cut:]
            first = dp_index == 0
            parts = [jnp.where(first, low, high), jnp.where(first, high, low)]
            return jnp.concatenate(parts, axis=1)
        return jnp.roll(weight.reshape(D, dp, cut), -dp_index, axis=1).reshape(D, -1)

    own_in, own_down = by_owner(w_in[0]), by_owner(w_down[0])

    route_flat = route.reshape(-1)
    position = route_flat * capacity + slot.reshape(-1)
    assign = (
        (jnp.arange(experts * capacity, dtype=jnp.int32)[:, None] == position[None, :])
        & (dropped.reshape(-1) == 0)[None, :]
    ).astype(bf16)
    grad_low = cotangent.reshape(row_count, D)
    grad_buffer = matmul(assign, grad_low).astype(bf16).reshape(experts, capacity, D)
    expert_index = lax.axis_index(expert_axis)

    def swap(blocks):
        swapped = jnp.zeros_like(blocks)
        for k in range(experts):
            part = pick(blocks, lax.rem(expert_index + k, experts))
            part = shift(part, expert_axis, k) if k else part
            came_from = lax.rem(expert_index - k + experts, experts)
            swapped = lax.dynamic_update_index_in_dim(swapped, part, came_from, 0)
        return swapped.reshape(-1, D)

    grad_rows = swap(grad_buffer)

    onehot = (
        jnp.arange(position_bias.shape[0], dtype=jnp.int32)[:, None]
        == jnp.pad(bucket[::-1], (0, 1), constant_values=-1)[None, :]
    ).astype(f32)
    bias_heads = lax.dynamic_slice_in_dim(position_bias.T, head_group * GROUP_HEADS, GROUP_HEADS, 0)
    table = jnp.dot(bias_heads, onehot, precision=precise_mode, preferred_element_type=f32)
    table = table[:, None, :]

    def normalised(values):
        scale = lax.rsqrt(jnp.mean(values * values, axis=-1, keepdims=True) + norm_epsilon)
        return scale, values * scale

    group_normed = (normalised(group_tokens.astype(f32))[1] * gain_one).astype(bf16)
    own_kv = contract_cols(weight_kv, group_normed).astype(bf16)
    kvs = [own_kv] + [shift(own_kv, "gb", k) for k in range(1, gb)]
    query = contract_cols(weight_query, group_normed).astype(bf16)
    query = after(query, grad_rows)

    grad_blocks = every_other(after(grad_rows, group_normed))
    both_in = [own_in, pair(after(own_in, group_normed))]

    attended_parts, attended, lse = attention_forward(
        span_blocks, core, table, query, kvs
    )

    def to_sources(parts):
        parts = parts.reshape(group_rows // BLOCK, -1, BLOCK)
        if in_order:
            parts = jnp.transpose(
                parts.reshape(group_rows // BLOCK, parts.shape[1], BLOCK // tok_count, tok_count),
                (0, 2, 1, 3),
            ).reshape(GROUPS, parts.shape[1], tok_count)
        return parts

    def from_sources(parts):
        if in_order:
            merged = BLOCK // tok_count
            parts = jnp.transpose(
                parts.reshape(GROUPS // merged, merged, parts.shape[1], tok_count), (0, 2, 1, 3)
            ).reshape(GROUPS // merged, parts.shape[1], BLOCK)
        return parts

    attended_low = exchange(to_sources(attended_parts), group_axis)
    attended_low = attended_low.reshape(seq_count, D, tok_count)
    both_down = [own_down, pair(after(own_down, attended_low))]

    inputs = tokens.reshape(row_count, D).astype(f32)
    branch = jnp.concatenate(
        [contract_rows(attended_low[i], output_weight) for i in range(seq_count)], axis=0
    )
    middle = inputs + branch
    scale_two, unit_two = normalised(middle)
    normalized_second = unit_two * gain_two
    router_logits = jnp.dot(
        normalized_second, router_weight, precision=precise_mode, preferred_element_type=f32
    )
    router = jax.nn.softmax(router_logits, axis=-1)
    chosen = (route_flat[:, None] == jnp.arange(experts, dtype=jnp.int32)[None, :]).astype(f32)
    gate = jnp.sum(router * chosen, axis=-1, keepdims=True)

    gate_high, gate_low = split_halves(gate)
    payload = jnp.concatenate(
        [
            after(
                normalized_second.astype(bf16), *grad_blocks[1:], both_in[1]
            ),
            gate_high,
            gate_low,
            jnp.zeros((row_count, 126), bf16),
        ],
        axis=1,
    )
    buffer = matmul(assign, payload).astype(bf16).reshape(experts, capacity, D + 128)
    received = exchange(buffer, expert_axis).reshape(-1, D + 128)
    row_total = received.shape[0]
    gate_rows = contract_cols(jnp.eye(16, 128, dtype=bf16), received[:, D:]).astype(bf16)
    gate_rows = jnp.pad(gate_rows, ((0, 0), (0, -row_total % D)))[:, :D]
    sent_blocks = every_other(jnp.concatenate([received[:, :D], gate_rows], axis=0))
    row_blocks = [block[:row_total] for block in sent_blocks]
    gate_blocks = [block[row_total:, :row_total] for block in sent_blocks]
    gate_width = jnp.where(jnp.arange(16)[:, None] < 2, 1.0, 0.0) * jnp.ones((1, D), f32)
    gate_width = gate_width.astype(bf16)

    ones = jnp.ones((8, own_in.shape[1]), bf16)
    hidden_blocks, pre_blocks, back_parts = [], [], []
    for rows_now, grads_now in zip(row_blocks, grad_blocks):
        hidden_blocks.append([])
        pre_blocks.append([])
        back = gate_part = 0.0
        for weight_in, weight_down in zip(both_in, both_down):
            grad_hidden = matmul(after(grads_now, sent_blocks[0]), weight_down)
            act, slope = gelu_parts(matmul(rows_now, weight_in))
            hidden = act.astype(bf16)
            grad_pre = (grad_hidden * slope).astype(bf16)
            hidden_blocks[-1].append(hidden)
            pre_blocks[-1].append(grad_pre)
            back = back + contract_cols(grad_pre, weight_in)
            product = (grad_hidden * hidden.astype(f32)).astype(bf16)
            gate_part = gate_part + contract_cols(ones, product)[:1]
        gate_part = jnp.concatenate(
            split_halves(gate_part) + (jnp.zeros((14, row_total), bf16),), axis=0
        )
        gate_part = jnp.pad(gate_part, ((0, 0), (0, -row_total % D)))[:, :D]
        back = jnp.concatenate([back.astype(bf16), gate_part], axis=0)
        back_parts.append(after(back, *sent_blocks[1:]))

    back_total = add_up(every_other_back(back_parts))
    back_sum = back_total[:row_total].astype(bf16)
    gate_sum = back_total[row_total : row_total + 2, :row_total]
    gate_sum = gate_sum[:1] + gate_sum[1:]
    gate_halves = split_halves(gate_sum[:1])
    gate_column = contract_rows(
        jnp.concatenate(gate_halves + (jnp.zeros((6, gate_sum.shape[1]), bf16),), axis=0),
        jnp.eye(8, 128, dtype=bf16),
    ).astype(bf16)
    back_rows = jnp.concatenate([back_sum, gate_column], axis=1)
    back_rows = exchange(back_rows.reshape(experts, capacity, D + 128), expert_axis)
    back_rows = contract_rows(assign, back_rows.reshape(-1, D + 128))
    grad_sent = back_rows[:, :D] * gate
    grad_gate = back_rows[:, D : D + 1] + back_rows[:, D + 1 : D + 2]

    grad_out = grad_low.astype(f32)
    grad_logits = grad_gate * gate * (chosen - router)
    grad_normed_two = grad_sent + lax.dot_general(
        grad_logits,
        router_weight,
        (((1,), (1,)), ((), ())),
        precision=precise_mode,
        preferred_element_type=f32,
    )
    scaled_two = gain_two * grad_normed_two
    cube_two = scale_two * scale_two * scale_two
    grad_middle = (
        grad_out
        + scale_two * scaled_two
        - middle * cube_two * jnp.mean(scaled_two * middle, axis=-1, keepdims=True)
    )
    grad_branch = grad_middle.astype(bf16)

    grad_heads = jnp.concatenate(
        [
            contract_cols(output_weight, grad_branch[i * tok_count : (i + 1) * tok_count])
            for i in range(seq_count)
        ],
        axis=0,
    ).astype(bf16)
    grad_heads = exchange(
        grad_heads.reshape(GROUPS, GROUP_HEADS * HEAD_DIM, tok_count), group_axis
    )

    out_parts = [
        add_up([contract_cols(h, w) for h, w in zip(hidden, both_down)]).astype(bf16)
        for hidden in hidden_blocks
    ]
    result_parts = every_other_back(
        out_parts[:1] + [after(part, grad_heads) for part in out_parts[1:]]
    )

    all_rows = jnp.concatenate(row_blocks, axis=0)
    all_grads = jnp.concatenate(grad_blocks, axis=0)
    all_gates = contract_rows(jnp.concatenate(gate_blocks, axis=1), gate_width)
    all_returned = (all_gates * all_grads.astype(f32)).astype(bf16)
    all_hidden = [jnp.concatenate(blocks, axis=0) for blocks in zip(*hidden_blocks)]
    all_pre = [
        (jnp.concatenate(blocks, axis=0).astype(f32) * all_gates[:, :1]).astype(bf16)
        for blocks in zip(*pre_blocks)
    ]
    cut = own_in.shape[1] // dp

    def reduced(left, rights):
        def columns(k):
            piece = [right[:, k * cut : (k + 1) * cut] for right in rights]
            return contract_rows(left, jnp.concatenate(piece, axis=1)).astype(bf16)

        came = [shift(columns(k), "dp", k) for k in range(1, dp)]
        mine = columns(0)
        own = add_up([mine[:, :cut]] + [part[:, :cut] for part in came])
        partner = add_up([mine[:, cut:]] + [part[:, cut:] for part in came]).astype(bf16)
        return own, partner

    in_grad, in_partner = reduced(all_rows, all_pre)
    down_grad, down_partner = reduced(all_returned, all_hidden)
    in_came = pair(after(in_partner, back_sum))
    grad_heads = after(grad_heads, in_came)


    outs = attention_backward(
        span_blocks,
        core,
        table,
        query,
        attended,
        lse,
        from_sources(grad_heads),
        kvs,
    )
    grad_query, grad_kvs, grad_table = outs[0], outs[1:-1], outs[-1]
    grad_kv = add_up(give_back(grad_kvs, "gb")).astype(bf16)
    grad_projected = jnp.concatenate([grad_query, grad_kv], axis=0)
    weight_all = jnp.concatenate([weight_query, weight_kv], axis=0)
    part_normed = contract_rows(grad_projected, weight_all).astype(bf16)
    down_came = pair(after(down_partner, part_normed))
    part_normed = part_normed.reshape(ga, ctx, tok_count, D)

    def over_context(parts):
        sums = {}
        for k in range(ctx):
            part = pick(parts, lax.rem(ctx_index - k + ctx, ctx))
            part = shift(part, "context", -k) if k else part
            from_ctx = lax.rem(ctx_index + k, ctx)
            for i in range(1 if ctx == HEAD_GROUPS else seq_count):
                kept = part.astype(f32)
                if ctx != HEAD_GROUPS:
                    kept = jnp.where(from_ctx // HEAD_GROUPS == i, kept, 0.0)
                sums[i] = sums[i] + kept if i in sums else kept
        return list(sums.values())

    if ga == 1:
        grad_normed = over_context(part_normed[0])
        first_sum = part_normed
    else:
        on_low = ga_index == 0
        total = over_context(jnp.transpose(part_normed, (1, 0, 2, 3)))[0]
        first_sum = jnp.where(on_low, total[1], total[0]).astype(bf16)
        came = shift(first_sum, "ga", 1).astype(f32)
        own_sum = jnp.where(on_low, total[0], total[1])
        grad_normed = [jnp.where(on_low, own_sum, came), jnp.where(on_low, came, own_sum)]

    padding = jnp.zeros((-grad_projected.shape[0] % BLOCK, grad_projected.shape[1]), bf16)
    qkv_part = lax.dot_general(
        after(group_normed, part_normed),
        jnp.concatenate([grad_projected, padding], axis=0),
        (((0,), (1,)), ((), ())),
        preferred_element_type=f32,
    ).astype(bf16)
    out_part_grad = add_up(
        [
            matmul(attended_low[i], grad_branch[i * tok_count : (i + 1) * tok_count])
            for i in range(seq_count)
        ]
    )
    router_grad = lax.dot_general(
        normalized_second,
        grad_logits,
        (((0,), (0,)), ((), ())),
        precision=precise_mode,
        preferred_element_type=f32,
    )
    gain_two_grad = jnp.sum(grad_normed_two * unit_two, axis=0)
    dense = jnp.concatenate(
        [out_part_grad, router_grad, gain_two_grad[:, None], jnp.zeros((D, 123), f32)], axis=1
    ).astype(bf16)
    bias_part = lax.dot_general(
        after(grad_table, part_normed)[:, 0],
        onehot,
        (((1,), (1,)), ((), ())),
        precision=precise_mode,
        preferred_element_type=f32,
    )
    width_qkv = qkv_part.shape[1]
    bias_grad = lax.dynamic_update_slice_in_dim(
        jnp.zeros((HEADS, bias_part.shape[1]), f32), bias_part, head_group * GROUP_HEADS, 0
    )

    own_rows = D // (ga * gb * ctx * dp)
    bias_rows = jnp.pad(bias_grad, ((0, 16 - HEADS), (0, width_qkv - bias_grad.shape[1])))

    def first_exchange(value, *riders):
        value = value.astype(bf16).reshape(experts, -1, value.shape[1])
        for rider in riders:
            rider = jnp.broadcast_to(rider.astype(bf16), (experts,) + rider.shape)
            value = jnp.concatenate([value, rider], axis=1)
        return add_up(list(exchange(value, expert_axis)))

    def second_exchange(value, *riders):
        value = value.astype(bf16).reshape(ctx * dp, own_rows, value.shape[1])
        for rider in riders:
            rider = jnp.broadcast_to(rider.astype(bf16), (ctx * dp,) + rider.shape)
            value = jnp.concatenate([value, rider], axis=1)
        return exchange(value, ("context", "dp"))

    dense = first_exchange(dense)
    part_rows = part_normed.reshape(-1, D)
    dense = second_exchange(after(dense, part_rows))
    summed = first_exchange(after(qkv_part, dense), bias_rows)
    dense = add_up(list(dense))
    bias_shape = bias_grad.shape
    bias_row = summed[-16:][:HEADS, : bias_shape[1]].reshape(1, -1)
    bias_rows = jnp.pad(bias_row, ((0, 7), (0, width_qkv - bias_row.shape[1])))
    summed = after(summed[:-16], first_sum, down_came)
    summed = second_exchange(summed, bias_rows).astype(f32)
    bias_grad = add_up(list(summed[:, own_rows, : bias_row.shape[1]])).reshape(bias_shape).T
    summed = summed[:, :own_rows].reshape(ctx, dp, own_rows, width_qkv)
    by_group = []
    for group in range(HEAD_GROUPS):
        by_group.append(add_up([summed[z, d] for z in range(group, ctx, HEAD_GROUPS) for d in range(dp)]))
    by_group = jnp.stack(by_group, axis=1)
    width = GROUP_HEADS * HEAD_DIM
    query_cols = by_group[:, :, :width].reshape(own_rows, 1, D)
    kv_cols = by_group[:, :, width : 3 * width].reshape(own_rows, HEADS, 2, HEAD_DIM)
    kv_cols = jnp.transpose(kv_cols, (0, 2, 1, 3)).reshape(own_rows, 2, D)
    qkv_total = jnp.concatenate([query_cols, kv_cols], axis=1).reshape(own_rows, 3 * D)
    first_row = (lax.axis_index(("ga", "gb", "context", "dp"))) * own_rows
    weight_rows = lax.dynamic_slice_in_dim(query_key_value_weight, first_row, own_rows, 0)
    gain_rows = lax.dynamic_slice_in_dim(gain_one, first_row, own_rows, 0)
    gain_one_total = jnp.sum(qkv_total * weight_rows.astype(f32), axis=1) / gain_rows

    result = after(add_up(result_parts).astype(bf16), part_normed.reshape(-1, D))
    returned = contract_rows(assign, swap(result.reshape(experts, capacity, D)))
    output = (middle + gate * returned).astype(bf16)

    grad_normed = jnp.concatenate(grad_normed, axis=0)
    scale_one = normalised(inputs)[0]
    scaled_one = gain_one * grad_normed
    cube_one = scale_one * scale_one * scale_one
    grad_inputs = (
        grad_middle
        + scale_one * scaled_one
        - inputs * cube_one * jnp.mean(scaled_one * inputs, axis=-1, keepdims=True)
    )

    return (
        output.reshape(seq_count, tok_count, D),
        grad_inputs.astype(bf16).reshape(seq_count, tok_count, D),
        qkv_total,
        dense[:, :D],
        gain_one_total,
        dense[:, D + 4],
        dense[:, D : D + 4],
        (after(in_grad, part_rows) + in_came.astype(f32))[None],
        (down_grad + down_came.astype(f32))[None],
        bias_grad,
    )


def solution(mesh):
    ctx = mesh.shape["context"]
    ga = max(GROUPS // ctx, 1)
    gb = mesh.shape["expert"] // ga
    fine = Mesh(
        mesh.devices.reshape(ga, gb, ctx, mesh.shape["dp"]), ("ga", "gb", "context", "dp")
    )
    expert = ("ga", "gb")
    blocks = ("ga", "gb", "context")
    everywhere = ("ga", "gb", "context", "dp")
    return jax.shard_map(
        local,
        mesh=fine,
        in_specs=(
            P("dp", blocks, None),
            P("dp", blocks, None),
            P(),
            P(),
            P(),
            P(),
            P(),
            P(expert, None, "context"),
            P(expert, None, "context"),
            P(),
            P(),
            P("dp", blocks),
            P("dp", blocks),
            P("dp", blocks),
        ),
        out_specs=(
            P("dp", blocks, None),
            P("dp", blocks, None),
            P(everywhere, None),
            P(everywhere, None),
            P(everywhere),
            P(everywhere),
            P(everywhere, None),
            P(expert, None, ("context", "dp")),
            P(expert, None, ("context", "dp")),
            P(),
        ),
        check_vma=False,
    )
```
